256 devices in a mesh: frow: 8 (over x, core), fcol: 32 (over z, y).
Axes of the slice: x: 4, y: 4, z: 8, core: 2. Of those that a mesh axis runs over, the one named last changes fastest.
Arguments:
- facet_image: bfloat16 [4096, 16384], P('frow', 'fcol'), may hold values from -6 to 6
- row_offsets: int32 [2], replicated, may hold values from 0 to 65280
- col_offsets: int32 [2], replicated, may hold values from 0 to 65280
- vis_subgrid: int32 [131072], P(('frow', 'fcol')), may hold values from 0 to 3
- vis_u: int32 [131072], P(('frow', 'fcol')), may hold values from 0 to 255
- vis_v: int32 [131072], P(('frow', 'fcol')), may hold values from 0 to 255
- observed: float32 [2, 131072], P(None, ('frow', 'fcol')), may hold values from -6 to 6
Outputs:
- facet_residual: float32 [4096, 16384], P('frow', 'fcol')
- residual_vis: float32 [2, 131072], P(None, ('frow', 'fcol'))
The draws below stay inside these ranges and needn't reach their ends.
Inputs may be any that keep to these rules, and one draw needn't show every extreme that they name: `vis_subgrid`: subgrid numbers count row by row over the 2 x 2 subgrids.
All inputs are finite; a program needn't handle non-finite values.
Results may differ from the reference program's by a relative error of at most 0.023.
Values may be sent and summed in bfloat16 or wider, within the bound.
No kernel may reach another device: no remote copies, remote signals or barrier semaphores. Data moves between devices by JAX's collectives and lax.ppermute only.
A program may use at most 64 MiB of HBM per device.

```python
import math
import jax
import jax.numpy as jnp
import numpy as np
from jax import lax

SKY = 65536
FS = 512
SG = 256
NR = 2
NC = 2
NVIS = 131072
N_FROW = 8
N_FCOL = 32


def with_ends(drawn, rng, least, largest):
    index_at = [jax.random.randint(jax.random.fold_in(rng, axis), (), 0, length) for axis, length in enumerate(drawn.shape)]
    main_axis = drawn.shape.index(max(drawn.shape))
    next_to = index_at[:main_axis] + [(index_at[main_axis] + 1) % drawn.shape[main_axis]] + index_at[main_axis + 1:]
    return drawn.at[tuple(index_at)].set(least).at[tuple(next_to)].set(largest)


def block_levels(key, extent, split, low, largest):
    loudness = 1.0
    for dim, parts in split:
        heights = jax.random.uniform(jax.random.fold_in(jax.random.fold_in(key, 6), dim), (parts,), jnp.float32, low / len(split), largest / len(split))
        loudness = loudness * jnp.repeat(jnp.exp(heights), extent[dim] // parts).reshape((-1,) + (1,) * (len(extent) - 1 - dim))
    return loudness


def rank_table(number_of, slope):
    loads = [(1 << 20) // math.isqrt(rank ** slope) + 1 for rank in range(1, number_of + 1)]
    deviation = 1 + sum(loads) // (1 << 30)
    return np.cumsum(np.array([max(1, weight // deviation) for weight in loads]))


def ranked(key, shape, amount, lean):
    table = rank_table(amount, lean)
    pick = jax.random.randint(jax.random.fold_in(key, 1), shape, 0, int(table[amount - 1]))
    standing = jnp.searchsorted(jnp.asarray(table, jnp.int32), pick, side="right")
    return jax.random.permutation(jax.random.fold_in(key, 2), amount)[standing].astype(jnp.int32)


def scatter_about(stream_key, dims, deviation, bound, pieces=(), kind=jnp.bfloat16):
    values = jax.random.normal(stream_key, dims, jnp.float32) * deviation
    if len(pieces) > 0:
        values = block_levels(stream_key, dims, pieces, -0.22, 0.18) * values
    return jnp.clip(values, min=-bound, max=bound).astype(kind)


def setup_inputs(seed: int = 0) -> dict:
    streams_of = jax.random.split(jax.random.key(seed), 8)
    facet_image = scatter_about(streams_of[0], (FS * N_FROW, FS * N_FCOL), 1.0, 6.0, ((0, 8), (1, 32)))
    row_offsets = jax.random.randint(streams_of[1], (NR,), 0, SKY - SG + 1).astype(jnp.int32)
    col_offsets = jax.random.randint(streams_of[2], (NC,), 0, SKY - SG + 1).astype(jnp.int32)
    vis_subgrid = with_ends(ranked(streams_of[3], (NVIS,), NR * NC, 2), jax.random.fold_in(streams_of[3], 3), 0, (NR * NC) - 1).astype(jnp.int32)
    vis_u = with_ends(jax.random.randint(streams_of[4], (NVIS,), 0, SG), jax.random.fold_in(streams_of[4], 1), 0, SG - 1).astype(jnp.int32)
    vis_v = with_ends(jax.random.randint(streams_of[5], (NVIS,), 0, SG), jax.random.fold_in(streams_of[5], 1), 0, SG - 1).astype(jnp.int32)
    observed = scatter_about(streams_of[6], (2, NVIS), 1.0, 6.0, ((1, 256),), jnp.float32)
    return dict(facet_image=facet_image, row_offsets=row_offsets, col_offsets=col_offsets, vis_subgrid=vis_subgrid, vis_u=vis_u, vis_v=vis_v, observed=observed)


def wrapped(frequency, position):
    high_part = frequency // 256
    low_part = frequency % 256
    return (high_part * (position * 256 % SKY) + low_part * position) % SKY

def sky_tables(start, positions):
    frequency = start + jnp.arange(SG, dtype=jnp.int32)[:, None]
    angles = wrapped(frequency, positions[None, :]).astype(jnp.float32) * (2.0 * math.pi / SKY)
    return (jnp.cos(angles).astype(jnp.bfloat16), jnp.sin(angles).astype(jnp.bfloat16))

def grid_tables():
    counter = jnp.arange(SG, dtype=jnp.int32)
    angles = (counter[:, None] * counter[None, :] % SG).astype(jnp.float32) * (2.0 * math.pi / SG)
    return (jnp.cos(angles).astype(jnp.bfloat16), jnp.sin(angles).astype(jnp.bfloat16))

def reference(facet_image, row_offsets, col_offsets, vis_subgrid, vis_u, vis_v, observed):
    f32 = jnp.float32
    hp = lax.Precision.HIGHEST
    scale_in = 1.0 / (FS * math.sqrt(N_FROW * N_FCOL))
    scale_out = 1.0 / (SG * math.sqrt(NR * NC))
    row_pos = (jnp.arange(N_FROW, dtype=jnp.int32)[:, None] * (SKY // N_FROW) + jnp.arange(FS, dtype=jnp.int32)[None, :] * (SKY // (N_FROW * FS))).reshape(-1)
    col_pos = (jnp.arange(N_FCOL, dtype=jnp.int32)[:, None] * (SKY // N_FCOL) + jnp.arange(FS, dtype=jnp.int32)[None, :] * (SKY // (N_FCOL * FS))).reshape(-1)
    row_tabs = [sky_tables(row_offsets[row_pick], row_pos) for row_pick in range(NR)]
    col_tabs = [sky_tables(col_offsets[col_pick], col_pos) for col_pick in range(NC)]
    blocks = facet_image.astype(f32).reshape(N_FROW * FS, N_FCOL, FS)
    col_sums = []
    for col_pick in range(NC):
        cos_tab, sin_tab = col_tabs[col_pick]
        p_full = jnp.einsum('xjy,bjy->xjb', blocks, cos_tab.astype(f32).reshape(SG, N_FCOL, FS)).astype(jnp.bfloat16)
        q_full = jnp.einsum('xjy,bjy->xjb', blocks, sin_tab.astype(f32).reshape(SG, N_FCOL, FS)).astype(jnp.bfloat16)
        col_sums.append((p_full.astype(f32).sum(axis=1), q_full.astype(f32).sum(axis=1)))
    real_list = []
    imag_list = []
    for row_pick in range(NR):
        crow = row_tabs[row_pick][0].astype(f32)
        srow = row_tabs[row_pick][1].astype(f32)
        for col_pick in range(NC):
            psum, qsum = col_sums[col_pick]
            real_list.append((jnp.dot(crow, psum, precision=hp) - jnp.dot(srow, qsum, precision=hp)) * scale_in)
            imag_list.append(-(jnp.dot(crow, qsum, precision=hp) + jnp.dot(srow, psum, precision=hp)) * scale_in)
    sub_real = jnp.stack(real_list).astype(jnp.bfloat16).reshape(NR * NC * SG, SG)
    sub_imag = jnp.stack(imag_list).astype(jnp.bfloat16).reshape(NR * NC * SG, SG)
    kcos, ksin = grid_tables()
    w_real = (jnp.dot(sub_real, kcos, preferred_element_type=f32) - jnp.dot(sub_imag, ksin, preferred_element_type=f32)).astype(jnp.bfloat16)
    w_imag = (jnp.dot(sub_real, ksin, preferred_element_type=f32) + jnp.dot(sub_imag, kcos, preferred_element_type=f32)).astype(jnp.bfloat16)
    w_real = w_real.astype(f32).reshape(NR * NC, SG, SG)
    w_imag = w_imag.astype(f32).reshape(NR * NC, SG, SG)
    kc32 = kcos.astype(f32)
    ks32 = ksin.astype(f32)
    hat_real = (jnp.einsum('au,sav->suv', kc32, w_real) - jnp.einsum('au,sav->suv', ks32, w_imag)) / SG
    hat_imag = (jnp.einsum('au,sav->suv', ks32, w_real) + jnp.einsum('au,sav->suv', kc32, w_imag)) / SG
    cell_ids = ((vis_subgrid * SG + vis_u) * SG + vis_v).astype(jnp.int32)
    model_vis = jnp.stack([hat_real.reshape(-1)[cell_ids], hat_imag.reshape(-1)[cell_ids]])
    residual = observed - model_vis
    cells_all = NR * NC * SG * SG
    ghat_real = jax.ops.segment_sum(residual[0], cell_ids, num_segments=cells_all).astype(jnp.bfloat16).reshape(NR * NC * SG, SG)
    ghat_imag = jax.ops.segment_sum(residual[1], cell_ids, num_segments=cells_all).astype(jnp.bfloat16).reshape(NR * NC * SG, SG)
    v_real = (jnp.dot(ghat_real, kcos, preferred_element_type=f32) + jnp.dot(ghat_imag, ksin, preferred_element_type=f32)).astype(jnp.bfloat16)
    v_imag = (jnp.dot(ghat_imag, kcos, preferred_element_type=f32) - jnp.dot(ghat_real, ksin, preferred_element_type=f32)).astype(jnp.bfloat16)
    v_real = v_real.astype(f32).reshape(NR * NC, SG, SG)
    v_imag = v_imag.astype(f32).reshape(NR * NC, SG, SG)
    back_real = ((jnp.einsum('au,sub->sab', kc32, v_real) + jnp.einsum('au,sub->sab', ks32, v_imag)) / SG).astype(jnp.bfloat16)
    back_imag = ((jnp.einsum('au,sub->sab', kc32, v_imag) - jnp.einsum('au,sub->sab', ks32, v_real)) / SG).astype(jnp.bfloat16)
    image = jnp.zeros((N_FROW * FS, N_FCOL * FS), f32)
    for col_pick in range(NC):
        u_real = jnp.zeros((N_FROW * FS, SG), f32)
        u_imag = jnp.zeros((N_FROW * FS, SG), f32)
        for row_pick in range(NR):
            crow, srow = row_tabs[row_pick]
            sub_index = row_pick * NC + col_pick
            g_real = back_real[sub_index]
            g_imag = back_imag[sub_index]
            u_real = u_real + jnp.dot(crow.T, g_real, preferred_element_type=f32) - jnp.dot(srow.T, g_imag, preferred_element_type=f32)
            u_imag = u_imag + jnp.dot(crow.T, g_imag, preferred_element_type=f32) + jnp.dot(srow.T, g_real, preferred_element_type=f32)
        ccol, scol = col_tabs[col_pick]
        image = image + jnp.dot(u_real.astype(jnp.bfloat16), ccol, preferred_element_type=f32) - jnp.dot(u_imag.astype(jnp.bfloat16), scol, preferred_element_type=f32)
    return (image * scale_out, residual)
```

```python
import math

import jax
import jax.numpy as jnp
import numpy as np
from jax import lax
from jax.sharding import PartitionSpec as P

SKY = 65536
SG = 256
NR = 2
NC = 2
HALF = SG // 2
BOTH = ("frow", "fcol")


def wrapped(frequency, position):
    high_part = frequency // 256
    low_part = frequency % 256
    return (high_part * (position * 256 % SKY) + low_part * position) % SKY


def phase_tables(frequency, position):
    angles = wrapped(frequency, position).astype(jnp.float32) * (2.0 * math.pi / SKY)
    return jnp.cos(angles), jnp.sin(angles)


def outer_tables(frequency, step, position):
    coarse_c, coarse_s = phase_tables(frequency[::16, None], position[None, :])
    fine_c, fine_s = phase_tables(step * jnp.arange(16, dtype=jnp.int32)[:, None], position[None, :])
    cos = coarse_c[:, None] * fine_c[None] - coarse_s[:, None] * fine_s[None]
    sin = coarse_s[:, None] * fine_c[None] + coarse_c[:, None] * fine_s[None]
    shape = (frequency.shape[0], position.shape[0])
    return cos.reshape(shape).astype(jnp.bfloat16), sin.reshape(shape).astype(jnp.bfloat16)


def grid_tables():
    counter = np.arange(SG)
    angles = (counter[:, None] * counter[None, :] % SG).astype(np.float64) * (2.0 * math.pi / SG)
    return (jnp.asarray(np.cos(angles), jnp.bfloat16), jnp.asarray(np.sin(angles), jnp.bfloat16))


def exchange(blocks, axes, groups):
    return lax.all_to_all(blocks, axes, 0, 0, tiled=True, axis_index_groups=groups)


def dot(left, right):
    return jnp.dot(left, right, preferred_element_type=jnp.float32)


def contract_first(left, right):
    return lax.dot_general(left, right, (((0,), (0,)), ((), ())), preferred_element_type=jnp.float32)


def contract_last(left, right):
    return lax.dot_general(left, right, (((1,), (1,)), ((), ())), preferred_element_type=jnp.float32)


def shards(facet, row_offsets, col_offsets, vis_subgrid, vis_u, vis_v, observed):
    f32, bf16 = jnp.float32, jnp.bfloat16
    rows_count, cols_count = lax.axis_size("frow"), lax.axis_size("fcol")
    side = facet.shape[0]
    n_vis = vis_u.shape[0]
    chips = rows_count // 2
    x_groups = [[2 * chip + core for chip in range(chips)] for core in range(2)]
    core_groups = [[2 * chip, 2 * chip + 1] for chip in range(chips)]
    grid_groups = [
        [(2 * chip + core) * cols_count + col for core in range(2) for col in range(cols_count)] for chip in range(chips)
    ]
    row_index, col_index = lax.axis_index("frow"), lax.axis_index("fcol")
    core = row_index % 2
    chip = row_index // 2
    scale_in = 1.0 / (side * math.sqrt(rows_count * cols_count))
    scale_out = 1.0 / (SG * math.sqrt(NR * NC))
    swap = [(index, index ^ 1) for index in range(rows_count)]

    facet_pair = jnp.concatenate([facet, lax.ppermute(facet, "frow", swap)], 0)
    vis_own = jnp.concatenate(
        [jnp.stack([vis_subgrid, vis_u, vis_v]).astype(bf16), observed.astype(bf16), jnp.zeros((3, n_vis), bf16)], 0
    )
    vis_pair = jnp.concatenate([vis_own, lax.ppermute(vis_own, "frow", swap)], 1)
    vis_all = exchange(jnp.broadcast_to(vis_pair, (chips,) + vis_pair.shape), "frow", x_groups)
    vis_n = vis_all.transpose(1, 0, 2).reshape(8, -1)

    counter = jnp.arange(SG, dtype=jnp.int32)
    line = jnp.arange(side, dtype=jnp.int32)
    row_step = SKY // (rows_count * side)
    col_step = SKY // (cols_count * side)
    row_pos = row_index * (SKY // rows_count) + line * row_step
    row_pos_pair = jnp.concatenate([row_pos, (row_index ^ 1) * (SKY // rows_count) + line * row_step])
    col_pos = col_index * (SKY // cols_count) + line * col_step

    row_tabs = [outer_tables(row_offsets[r] + counter, 1, row_pos_pair) for r in range(NR)]
    col_tabs = [outer_tables(col_offsets[c] + counter, 1, col_pos) for c in range(NC)]

    parts = []
    halves = []
    for c in range(NC):
        tab = jnp.concatenate([lax.dynamic_slice_in_dim(t, core * HALF, HALF, 0) for t in col_tabs[c]], 0)
        halves.append(contract_last(facet_pair, tab).astype(bf16))
    right = jnp.concatenate(halves, 1)
    for r in range(NR):
        with_cos = dot(row_tabs[r][0], right)
        with_sin = dot(row_tabs[r][1], right)
        for c in range(NC):
            at = 2 * c * HALF
            cp, cq = with_cos[:, at:at + HALF], with_cos[:, at + HALF:at + 2 * HALF]
            sp, sq = with_sin[:, at:at + HALF], with_sin[:, at + HALF:at + 2 * HALF]
            parts.append(jnp.stack([(cp - sq) * scale_in, -(cq + sp) * scale_in]).astype(bf16))
    mine = exchange(jnp.stack(parts), "frow", x_groups).astype(f32).sum(0).astype(bf16)

    in_sub = vis_n[0:1] == chip.astype(bf16)
    vis_u_hot = ((vis_n[1:2] == counter[:, None].astype(bf16)) & in_sub).astype(bf16)
    v_half = (core * HALF + jnp.arange(HALF, dtype=jnp.int32))[:, None].astype(bf16)
    v_hot = vis_n[2:3] == v_half
    zero = jnp.zeros((), bf16)
    weights = jnp.concatenate(
        [
            jnp.where(v_hot, vis_n[3:4], zero),
            jnp.where(v_hot, vis_n[4:5], zero),
            v_hot.astype(bf16),
        ],
        0,
    )
    sums = contract_last(vis_u_hot, weights).astype(bf16)
    planes = jnp.concatenate([mine, sums.reshape(SG, 3, HALF).transpose(1, 0, 2)], 0)
    rows_each = SG // cols_count
    pieces = planes.reshape(5, cols_count, rows_each, HALF).transpose(1, 0, 2, 3)
    piece = exchange(pieces, "fcol", None).astype(f32).sum(0).astype(bf16)
    gathered = exchange(jnp.broadcast_to(piece, (2 * cols_count,) + piece.shape), BOTH, grid_groups)
    full = (
        gathered.reshape(2, cols_count, 5, rows_each, HALF)
        .transpose(2, 1, 3, 0, 4)
        .reshape(5, SG, SG)
    )

    kcos, ksin = grid_tables()
    forward_block = jnp.concatenate(
        [jnp.concatenate([kcos, ksin], 1), jnp.concatenate([-ksin, kcos], 1)], 0
    )
    inverse_block = jnp.concatenate(
        [jnp.concatenate([kcos, -ksin], 1), jnp.concatenate([ksin, kcos], 1)], 0
    )
    w_both = dot(jnp.concatenate([full[0], full[1]], 1), forward_block).astype(bf16)
    with_cos = dot(kcos, w_both)
    with_sin = dot(ksin, w_both)
    hat_real = (with_cos[:, :SG] - with_sin[:, SG:]) / SG
    hat_imag = (with_sin[:, :SG] + with_cos[:, SG:]) / SG
    count = full[4].astype(f32)
    ghat = jnp.concatenate(
        [full[2].astype(f32) - count * hat_real, full[3].astype(f32) - count * hat_imag], 1
    ).astype(bf16)
    v_both = dot(ghat, inverse_block).astype(bf16)
    back_cos = dot(kcos, v_both)
    back_sin = dot(ksin, v_both)
    back = jnp.stack(
        [
            ((back_cos[:, :SG] + back_sin[:, SG:]) / SG).astype(bf16),
            ((back_cos[:, SG:] - back_sin[:, :SG]) / SG).astype(bf16),
        ]
    )
    my_half = lax.dynamic_slice_in_dim(back, core * HALF, HALF, 1)
    by_chip = exchange(jnp.broadcast_to(my_half, (chips,) + my_half.shape), "frow", x_groups)
    by_core = exchange(jnp.broadcast_to(by_chip, (2,) + by_chip.shape), "frow", core_groups)
    back_all = by_core.transpose(1, 2, 0, 3, 4).reshape(NR * NC, 2, SG, SG)

    ask = vis_all[:, :3, :n_vis].transpose(1, 0, 2).reshape(3, -1)
    u_hot = ((ask[1:2] == counter[:, None].astype(bf16)) & (ask[0:1] == chip.astype(bf16))).astype(bf16)
    v_hot_ask = (ask[2:3] == counter[:, None].astype(bf16)).astype(f32)
    hat_both = jnp.concatenate([hat_real, hat_imag], 1)
    hat_high = hat_both.astype(bf16)
    hat_low = (hat_both - hat_high.astype(f32)).astype(bf16)
    lines = contract_first(hat_high, u_hot) + contract_first(hat_low, u_hot)
    values = jnp.stack([(lines[:SG] * v_hot_ask).sum(0), (lines[SG:] * v_hot_ask).sum(0)])
    answers = exchange(values.reshape(2, chips, n_vis).transpose(1, 0, 2), "frow", x_groups)
    residual = observed - answers.sum(0)

    image = jnp.zeros((side, side), f32)
    for c in range(NC):
        u_both = jnp.zeros((side, 2 * SG), f32)
        for r in range(NR):
            g_real, g_imag = back_all[r * NC + c, 0], back_all[r * NC + c, 1]
            right_side = jnp.concatenate(
                [jnp.concatenate([g_real, g_imag], 1), jnp.concatenate([-g_imag, g_real], 1)], 0
            )
            tab = jnp.concatenate([t[:, :side] for t in row_tabs[r]], 0)
            u_both = u_both + contract_first(tab, right_side)
        image = image + dot(u_both.astype(bf16), jnp.concatenate([col_tabs[c][0], -col_tabs[c][1]], 0))
    return (image * scale_out, residual)


def solution(mesh):
    in_specs = (
        P("frow", "fcol"),
        P(),
        P(),
        P(("frow", "fcol")),
        P(("frow", "fcol")),
        P(("frow", "fcol")),
        P(None, ("frow", "fcol")),
    )
    out_specs = (P("frow", "fcol"), P(None, ("frow", "fcol")))
    return jax.shard_map(shards, mesh=mesh, in_specs=in_specs, out_specs=out_specs, check_vma=False)
```

```python
import functools
import math

import jax
import jax.numpy as jnp
import ml_dtypes
import numpy as np
from jax import lax
from jax.experimental import pallas as pl
from jax.experimental.pallas import tpu as pltpu
from jax.sharding import PartitionSpec as P

SKY = 65536
SG = 256
NR = 2
NC = 2
HALF = SG // 2
BOTH = ("frow", "fcol")


def wave(count):
    count = count & (SKY - 1)
    turned = count + SKY // 8
    near = (turned & (SKY // 4 - 1)) - SKY // 8
    quarter = lax.shift_right_logical(turned, 14) & 3
    t = near.astype(jnp.float32) * (2.0 * math.pi / SKY)
    q = t * t
    sin = t * (1.0 + q * (-1.0 / 6 + q * (1.0 / 120 + q * (-1.0 / 5040 + q * (1.0 / 362880)))))
    cos = 1.0 + q * (-0.5 + q * (1.0 / 24 + q * (-1.0 / 720 + q * (1.0 / 40320))))
    odd = (quarter & 1) == 1
    one, two = jnp.where(odd, sin, cos), jnp.where(odd, cos, sin)
    return (
        jnp.where((quarter == 1) | (quarter == 2), -one, one),
        jnp.where(quarter >= 2, -two, two),
    )


def lanes(n):
    return lax.broadcasted_iota(jnp.int32, (1, n), 1)


def sublanes(n):
    return lax.broadcasted_iota(jnp.int32, (n, 1), 0)


def spread(coarse, fine, store):
    for k in range(coarse[0].shape[0]):
        c, s = coarse[0][k:k + 1], coarse[1][k:k + 1]
        store(k * 16, c * fine[0] - s * fine[1], s * fine[0] + c * fine[1])


def forward_tables_kernel(rows_count, cols_count, info, facet, row_tab, col_tab, pq):
    bf16 = jnp.bfloat16
    side = facet.shape[0]
    row_index, col_index = info[4], info[5]
    core = row_index % 2
    unit = sublanes(16)

    col_step = SKY // (cols_count * side)
    col_base = col_index * (SKY // cols_count)
    for c in range(NC):
        freq = info[2 + c] + core * HALF + lanes(HALF)
        coarse = wave((col_base + 16 * col_step * sublanes(side // 16)) * freq)
        fine = wave((col_step * unit) * freq)

        def store(at, cos, sin, c=c):
            col_tab[at:at + 16, 2 * c * HALF:(2 * c + 1) * HALF] = cos.astype(bf16)
            col_tab[at:at + 16, (2 * c + 1) * HALF:(2 * c + 2) * HALF] = sin.astype(bf16)

        spread(coarse, fine, store)
    pq[...] = jnp.dot(facet[...], col_tab[...], preferred_element_type=jnp.float32).astype(bf16)

    row_step = SKY // (rows_count * side)
    for f in range(2):
        base = (row_index ^ f) * (SKY // rows_count)
        pos = base + row_step * lanes(side)
        fine = wave(unit * pos)
        for r in range(NR):
            coarse = wave((info[r] + 16 * unit) * pos)

            def store(at, cos, sin, r=r, f=f):
                row_tab[2 * r, at:at + 16, f * side:(f + 1) * side] = cos.astype(bf16)
                row_tab[2 * r + 1, at:at + 16, f * side:(f + 1) * side] = sin.astype(bf16)

            spread(coarse, fine, store)


def contributions_kernel(scale, facet, row_tab, col_tab, pq, out, right):
    side = facet.shape[0]
    f32, bf16 = jnp.float32, jnp.bfloat16
    right[:side] = pq[...]
    right[side:] = jnp.dot(facet[...], col_tab[...], preferred_element_type=f32).astype(bf16)
    for r in range(NR):
        with_cos = jnp.dot(row_tab[2 * r], right[...], preferred_element_type=f32)
        with_sin = jnp.dot(row_tab[2 * r + 1], right[...], preferred_element_type=f32)
        for c in range(NC):
            at = 2 * c * HALF
            cp, cq = with_cos[:, at:at + HALF], with_cos[:, at + HALF:at + 2 * HALF]
            sp, sq = with_sin[:, at:at + HALF], with_sin[:, at + HALF:at + 2 * HALF]
            out[r * NC + c, 0] = ((cp - sq) * scale).astype(bf16)
            out[r * NC + c, 1] = (-(cq + sp) * scale).astype(bf16)


def back_tables_kernel(rows_count, cols_count, side, info, row_tab, col_tab):
    bf16 = jnp.bfloat16
    row_index, col_index = info[4], info[5]
    unit = sublanes(16)
    row_step = SKY // (rows_count * side)
    row_base = row_index * (SKY // rows_count)
    for r in range(NR):
        freq = info[r] + lanes(SG)
        coarse = wave((row_base + 16 * row_step * sublanes(side // 16)) * freq)
        fine = wave((row_step * unit) * freq)

        def store(at, cos, sin, r=r):
            row_tab[2 * r, at:at + 16] = cos.astype(bf16)
            row_tab[2 * r + 1, at:at + 16] = sin.astype(bf16)

        spread(coarse, fine, store)
    col_step = SKY // (cols_count * side)
    pos = col_index * (SKY // cols_count) + col_step * lanes(side)
    fine = wave(unit * pos)
    for c in range(NC):
        coarse = wave((info[2 + c] + 16 * unit) * pos)

        def store(at, cos, sin, c=c):
            col_tab[2 * c, at:at + 16] = cos.astype(bf16)
            col_tab[2 * c + 1, at:at + 16] = (-sin).astype(bf16)

        spread(coarse, fine, store)


def image_kernel(scale, back, row_tab, col_tab, out, grid, both):
    f32, bf16 = jnp.float32, jnp.bfloat16
    for c in range(NC):
        real = imag = None
        for r in range(NR):
            for k in range(2):
                for half in range(2):
                    grid[:, k * SG + half * HALF:k * SG + (half + 1) * HALF] = back[half, r * NC + c, k]
            cos = jnp.dot(row_tab[2 * r], grid[...], preferred_element_type=f32)
            sin = jnp.dot(row_tab[2 * r + 1], grid[...], preferred_element_type=f32)
            re, im = cos[:, :SG] - sin[:, SG:], cos[:, SG:] + sin[:, :SG]
            real = re if real is None else real + re
            imag = im if imag is None else imag + im
        both[:, :SG] = real.astype(bf16)
        both[:, SG:] = imag.astype(bf16)
        part = jnp.dot(both[:, :SG], col_tab[2 * c], preferred_element_type=f32)
        part = part + jnp.dot(both[:, SG:], col_tab[2 * c + 1], preferred_element_type=f32)
        if c == 0:
            out[...] = part
        else:
            out[...] = (out[...] + part) * scale


def grids_kernel(full, kcos, ksin, forward, inverse, hat, back, cat):
    f32, bf16 = jnp.float32, jnp.bfloat16
    cat[:, :SG] = full[0]
    cat[:, SG:] = full[1]
    cat[...] = jnp.dot(cat[...], forward[...], preferred_element_type=f32).astype(bf16)
    with_cos = jnp.dot(kcos[...], cat[...], preferred_element_type=f32)
    with_sin = jnp.dot(ksin[...], cat[...], preferred_element_type=f32)
    hat_real = (with_cos[:, :SG] - with_sin[:, SG:]) * (1.0 / SG)
    hat_imag = (with_sin[:, :SG] + with_cos[:, SG:]) * (1.0 / SG)
    for k, part in enumerate((hat_real, hat_imag)):
        high = part.astype(bf16)
        hat[0, k] = high
        hat[1, k] = (part - high.astype(f32)).astype(bf16)
    count = full[4].astype(f32)
    cat[:, :SG] = (full[2].astype(f32) - count * hat_real).astype(bf16)
    cat[:, SG:] = (full[3].astype(f32) - count * hat_imag).astype(bf16)
    cat[...] = jnp.dot(cat[...], inverse[...], preferred_element_type=f32).astype(bf16)
    with_cos = jnp.dot(kcos[...], cat[...], preferred_element_type=f32)
    with_sin = jnp.dot(ksin[...], cat[...], preferred_element_type=f32)
    real = ((with_cos[:, :SG] + with_sin[:, SG:]) * (1.0 / SG)).astype(bf16)
    imag = ((with_cos[:, SG:] - with_sin[:, :SG]) * (1.0 / SG)).astype(bf16)
    for half in range(2):
        back[half, 0] = real[:, half * HALF:(half + 1) * HALF]
        back[half, 1] = imag[:, half * HALF:(half + 1) * HALF]


def answers_kernel(info, ask, hat, out):
    f32, bf16 = jnp.float32, jnp.bfloat16
    row_index = info[4]
    core = row_index % 2
    chip = (row_index // 2).astype(f32)
    n = ask.shape[2]
    counter = sublanes(SG).astype(f32)
    dims = (((0,), (0,)), ((), ()))
    for k in range(ask.shape[0] // 2):
        mine = ask[2 * k + core].astype(f32)
        hot = jnp.where((mine[1:2] == counter) & (mine[0:1] == chip), 1.0, 0.0).astype(bf16)
        pick = mine[2:3] == counter
        for part in range(2):
            line = lax.dot_general(hat[0, part], hot, dims, preferred_element_type=f32)
            line = line + lax.dot_general(hat[1, part], hot, dims, preferred_element_type=f32)
            out[k, part:part + 1] = jnp.sum(jnp.where(pick, line, 0.0), axis=0, keepdims=True)


def pack_kernel(subgrid, u, v, observed, out):
    f32 = jnp.float32
    zero = jnp.zeros((3, u.shape[1]), f32)
    rows = [subgrid[...].astype(f32), u[...].astype(f32), v[...].astype(f32), observed[...], zero]
    out[...] = jnp.concatenate(rows, 0).astype(jnp.bfloat16)


def gridding_kernel(info, vis, out):
    f32, bf16 = jnp.float32, jnp.bfloat16
    row_index = info[4]
    chip = (row_index // 2).astype(f32)
    v_at = (sublanes(HALF) + (row_index % 2) * HALF).astype(f32)
    counter = sublanes(SG).astype(f32)
    total = jnp.zeros((SG, 3 * HALF), f32)
    for k in range(vis.shape[0]):
        one = vis[k].astype(f32)
        hot = jnp.where((one[1:2] == counter) & (one[0:1] == chip), 1.0, 0.0).astype(bf16)
        pick = one[2:3] == v_at
        right = jnp.concatenate(
            [jnp.where(pick, one[3:4], 0.0), jnp.where(pick, one[4:5], 0.0), jnp.where(pick, 1.0, 0.0)], 0
        ).astype(bf16)
        total = total + lax.dot_general(hot, right, (((1,), (1,)), ((), ())), preferred_element_type=f32)
    for p in range(3):
        out[p] = total[:, p * HALF:(p + 1) * HALF].astype(bf16)


def call(kernel, out_shape, name, scratch=(), scalars=0, cost=0):
    smem, vmem = pl.BlockSpec(memory_space=pltpu.SMEM), pl.BlockSpec(memory_space=pltpu.VMEM)

    def run(*args):
        return pl.pallas_call(
            kernel,
            out_shape=out_shape,
            in_specs=[smem] * scalars + [vmem] * (len(args) - scalars),
            out_specs=jax.tree.map(lambda _: vmem, out_shape),
            scratch_shapes=list(scratch),
            compiler_params=pltpu.CompilerParams(vmem_limit_bytes=24 * 2**20),
            cost_estimate=pl.CostEstimate(flops=cost, bytes_accessed=2**20, transcendentals=0),
            name=name,
        )(*args)

    return run


def grid_tables():
    counter = np.arange(SG)
    angles = (counter[:, None] * counter[None, :] % SG).astype(np.float64) * (2.0 * math.pi / SG)
    return np.cos(angles).astype(ml_dtypes.bfloat16), np.sin(angles).astype(ml_dtypes.bfloat16)


def exchange(blocks, axes, groups):
    return lax.all_to_all(blocks, axes, 0, 0, tiled=True, axis_index_groups=groups)


def shape(*dims, dtype=jnp.bfloat16):
    return jax.ShapeDtypeStruct(dims, dtype)


def shards(facet, row_offsets, col_offsets, vis_subgrid, vis_u, vis_v, observed):
    f32, bf16 = jnp.float32, jnp.bfloat16
    rows_count, cols_count = lax.axis_size("frow"), lax.axis_size("fcol")
    side = facet.shape[0]
    n_vis = vis_u.shape[0]
    chips = rows_count // 2
    x_groups = [[2 * chip + core for chip in range(chips)] for core in range(2)]
    core_groups = [[2 * chip, 2 * chip + 1] for chip in range(chips)]
    grid_groups = [
        [(2 * chip + core) * cols_count + col for core in range(2) for col in range(cols_count)] for chip in range(chips)
    ]
    row_index, col_index = lax.axis_index("frow"), lax.axis_index("fcol")
    core = row_index % 2
    scale_in = 1.0 / (side * math.sqrt(rows_count * cols_count))
    scale_out = 1.0 / (SG * math.sqrt(NR * NC))
    info = jnp.concatenate([row_offsets, col_offsets, jnp.stack([row_index, col_index])]).astype(jnp.int32)

    facet_other = lax.ppermute(facet, "frow", [(index, index ^ 1) for index in range(rows_count)])
    vis_own = call(pack_kernel, shape(8, n_vis), "pack")(
        vis_subgrid.reshape(1, n_vis), vis_u.reshape(1, n_vis), vis_v.reshape(1, n_vis), observed
    )
    vis_all = exchange(jnp.broadcast_to(vis_own, (rows_count, 8, n_vis)), "frow", None)

    row_tab, col_tab, pq = call(
        functools.partial(forward_tables_kernel, rows_count, cols_count),
        (shape(4, SG, 2 * side), shape(side, 4 * HALF), shape(side, 4 * HALF)),
        "forward_tables", scalars=1, cost=10**9,
    )(info, facet)
    parts = call(
        functools.partial(contributions_kernel, scale_in), shape(NR * NC, 2, SG, HALF), "contributions",
        scratch=[pltpu.VMEM((2 * side, 4 * HALF), bf16)], cost=2 * 10**9,
    )(facet_other, row_tab, col_tab, pq)
    mine = exchange(parts, "frow", x_groups).astype(f32).sum(0).astype(bf16)

    sums = call(gridding_kernel, shape(3, SG, HALF), "gridding", scalars=1, cost=10**9)(info, vis_all)
    planes = jnp.concatenate([mine, sums], 0)
    rows_each = SG // cols_count
    pieces = planes.reshape(5, cols_count, rows_each, HALF).transpose(1, 0, 2, 3)
    piece = exchange(pieces, "fcol", None).astype(f32).sum(0).astype(bf16)
    gathered = exchange(jnp.broadcast_to(piece, (2 * cols_count,) + piece.shape), BOTH, grid_groups)
    full = (
        gathered.reshape(2, cols_count, 5, rows_each, HALF)
        .transpose(2, 1, 3, 0, 4)
        .reshape(5, SG, SG)
    )

    kcos, ksin = grid_tables()
    forward_block = np.concatenate([np.concatenate([kcos, ksin], 1), np.concatenate([-ksin, kcos], 1)], 0)
    inverse_block = np.concatenate([np.concatenate([kcos, -ksin], 1), np.concatenate([ksin, kcos], 1)], 0)
    hat, back = call(
        grids_kernel, (shape(2, 2, SG, SG), shape(2, 2, SG, HALF)), "grids",
        scratch=[pltpu.VMEM((SG, 2 * SG), bf16)], cost=10**9,
    )(full, kcos, ksin, forward_block, inverse_block)
    my_half = lax.dynamic_index_in_dim(back, core, 0, False)
    by_chip = exchange(jnp.broadcast_to(my_half, (chips,) + my_half.shape), "frow", x_groups)
    by_core = exchange(jnp.broadcast_to(by_chip, (2,) + by_chip.shape), "frow", core_groups)

    values = call(answers_kernel, shape(chips, 2, n_vis, dtype=f32), "answers", scalars=1, cost=10**9)(info, vis_all, hat)
    answers = exchange(values, "frow", x_groups)
    residual = observed - answers.sum(0)

    back_row, back_col = call(
        functools.partial(back_tables_kernel, rows_count, cols_count, side),
        (shape(4, side, SG), shape(4, SG, side)), "back_tables", scalars=1, cost=10**9,
    )(info)
    image = call(
        functools.partial(image_kernel, scale_out), shape(side, side, dtype=f32), "image",
        scratch=[pltpu.VMEM((SG, 2 * SG), bf16), pltpu.VMEM((side, 2 * SG), bf16)], cost=2 * 10**9,
    )(by_core, back_row, back_col)
    return (image, residual)


def solution(mesh):
    in_specs = (
        P("frow", "fcol"),
        P(),
        P(),
        P(("frow", "fcol")),
        P(("frow", "fcol")),
        P(("frow", "fcol")),
        P(None, ("frow", "fcol")),
    )
    out_specs = (P("frow", "fcol"), P(None, ("frow", "fcol")))
    return jax.shard_map(shards, mesh=mesh, in_specs=in_specs, out_specs=out_specs, check_vma=False)
```

```python
import functools
import math

import jax
import jax.numpy as jnp
import ml_dtypes
import numpy as np
from jax import lax
from jax.experimental import pallas as pl
from jax.experimental.pallas import tpu as pltpu
from jax.sharding import PartitionSpec as P

SKY = 65536
SG = 256
NR = 2
NC = 2
HALF = SG // 2
LANES = 128


def wave(count):
    count = count & (SKY - 1)
    turned = count + SKY // 8
    near = (turned & (SKY // 4 - 1)) - SKY // 8
    quarter = lax.shift_right_logical(turned, 14) & 3
    t = near.astype(jnp.float32) * (2.0 * math.pi / SKY)
    q = t * t
    sin = t * (1.0 + q * (-1.0 / 6 + q * (1.0 / 120 + q * (-1.0 / 5040 + q * (1.0 / 362880)))))
    cos = 1.0 + q * (-0.5 + q * (1.0 / 24 + q * (-1.0 / 720 + q * (1.0 / 40320))))
    odd = (quarter & 1) == 1
    one, two = jnp.where(odd, sin, cos), jnp.where(odd, cos, sin)
    return (
        jnp.where((quarter == 1) | (quarter == 2), -one, one),
        jnp.where(quarter >= 2, -two, two),
    )


def lanes(n):
    return lax.broadcasted_iota(jnp.int32, (1, n), 1)


def sublanes(n):
    return lax.broadcasted_iota(jnp.int32, (n, 1), 0)


def spread(coarse, fine, store):
    for k in range(coarse[0].shape[0]):
        c, s = coarse[0][k:k + 1], coarse[1][k:k + 1]
        store(k * 16, c * fine[0] - s * fine[1], s * fine[0] + c * fine[1])


def back_tables_kernel(rows_count, cols_count, side, info, row_tab, col_tab):
    bf16 = jnp.bfloat16
    row_index, col_index = info[4], info[5]
    unit = sublanes(16)
    row_step = SKY // (rows_count * side)
    row_base = row_index * (SKY // rows_count)
    for r in range(NR):
        freq = info[r] + lanes(SG)
        coarse = wave((row_base + 16 * row_step * sublanes(side // 16)) * freq)
        fine = wave((row_step * unit) * freq)

        def store(at, cos, sin, r=r):
            row_tab[2 * r, at:at + 16] = cos.astype(bf16)
            row_tab[2 * r + 1, at:at + 16] = sin.astype(bf16)

        spread(coarse, fine, store)
    col_step = SKY // (cols_count * side)
    pos = col_index * (SKY // cols_count) + col_step * lanes(side)
    fine = wave(unit * pos)
    for c in range(NC):
        coarse = wave((info[2 + c] + 16 * unit) * pos)

        def store(at, cos, sin, c=c):
            col_tab[2 * c, at:at + 16] = cos.astype(bf16)
            col_tab[2 * c + 1, at:at + 16] = (-sin).astype(bf16)

        spread(coarse, fine, store)


def columns_kernel(cols_count, info, facet, subgrid, u, v, observed, out, col_tab):
    f32, bf16 = jnp.float32, jnp.bfloat16
    side = facet.shape[0]
    col_index = info[5]
    unit = sublanes(16)
    col_step = SKY // (cols_count * side)
    col_base = col_index * (SKY // cols_count)
    rows = [subgrid[...].astype(f32), u[...].astype(f32), v[...].astype(f32), observed[...]]
    vis = jnp.concatenate(rows + [jnp.zeros((11, side), f32)], 0).astype(bf16)
    for c in range(NC):
        freq = info[2 + c] + lanes(SG)
        coarse = wave((col_base + 16 * col_step * sublanes(side // 16)) * freq)
        fine = wave((col_step * unit) * freq)

        def store(at, cos, sin, c=c):
            for h in range(2):
                half = slice(h * HALF, (h + 1) * HALF)
                left = (2 * h + c) * SG
                col_tab[at:at + 16, left:left + HALF] = cos[:, half].astype(bf16)
                col_tab[at:at + 16, left + HALF:left + SG] = sin[:, half].astype(bf16)

        spread(coarse, fine, store)
    for h in range(2):
        part = jnp.dot(facet[...], col_tab[:, 2 * h * SG:2 * (h + 1) * SG], preferred_element_type=f32)
        out[h, :side] = part.astype(bf16)
        out[h, side:] = vis


def row_tables_kernel(rows_count, side, info, row_tab):
    bf16 = jnp.bfloat16
    chip = info[4] // 2
    unit = sublanes(16)
    row_step = SKY // (rows_count * side)
    for f in range(2):
        pos = (2 * chip + f) * (SKY // rows_count) + row_step * lanes(side)
        fine = wave(unit * pos)
        for r in range(NR):
            coarse = wave((info[r] + 16 * unit) * pos)

            def store(at, cos, sin, r=r, f=f):
                row_tab[2 * r, at:at + 16, f * side:(f + 1) * side] = cos.astype(bf16)
                row_tab[2 * r + 1, at:at + 16, f * side:(f + 1) * side] = sin.astype(bf16)

            spread(coarse, fine, store)


def contributions_kernel(scale, halves, row_tab, out, right):
    f32, bf16 = jnp.float32, jnp.bfloat16
    side = row_tab.shape[2] // 2
    vis = []
    for f in range(2):
        right[f * side:(f + 1) * side] = halves[f, :side]
        some = halves[f, side:]
        vis += [some[:, k * LANES:(k + 1) * LANES] for k in range(side // LANES)]
    for s in range(NR * NC):
        for k, some in enumerate(vis):
            at = 2 * SG + 16 * k
            out[s, at:at + 16] = some
    for r in range(NR):
        with_cos = jnp.dot(row_tab[2 * r], right[...], preferred_element_type=f32)
        with_sin = jnp.dot(row_tab[2 * r + 1], right[...], preferred_element_type=f32)
        for c in range(NC):
            at = 2 * c * HALF
            cp, cq = with_cos[:, at:at + HALF], with_cos[:, at + HALF:at + 2 * HALF]
            sp, sq = with_sin[:, at:at + HALF], with_sin[:, at + HALF:at + 2 * HALF]
            out[r * NC + c, :SG] = ((cp - sq) * scale).astype(bf16)
            out[r * NC + c, SG:2 * SG] = (-(cq + sp) * scale).astype(bf16)


def vis_rows(block):
    count = block.shape[0] // 16
    return jnp.concatenate([block[16 * k:16 * k + 8] for k in range(count)], 1)


def gridding_kernel(info, parts, pieces, planes):
    f32, bf16 = jnp.float32, jnp.bfloat16
    row_index = info[4]
    chip = (row_index // 2).astype(f32)
    v_at = (sublanes(HALF) + (row_index % 2) * HALF).astype(f32)
    counter = sublanes(SG).astype(f32)
    count = parts.shape[0]
    total = jnp.zeros((SG, 3 * HALF), f32)
    for k in range(count):
        one = vis_rows(parts[k, 2 * SG:].astype(f32))
        hot = jnp.where((one[1:2] == counter) & (one[0:1] == chip), 1.0, 0.0).astype(bf16)
        pick = one[2:3] == v_at
        right = jnp.concatenate(
            [jnp.where(pick, one[3:4], 0.0), jnp.where(pick, one[4:5], 0.0), jnp.where(pick, 1.0, 0.0)], 0
        ).astype(bf16)
        total = total + lax.dot_general(hot, right, (((1,), (1,)), ((), ())), preferred_element_type=f32)
    for p in range(2):
        some = parts[0, p * SG:(p + 1) * SG].astype(f32)
        for k in range(1, count):
            some = some + parts[k, p * SG:(p + 1) * SG].astype(f32)
        planes[p] = some
    for p in range(3):
        planes[2 + p] = total[:, p * HALF:(p + 1) * HALF]
    each = SG // pieces.shape[0]
    for j in range(pieces.shape[0]):
        rows = [planes[p, j * each:(j + 1) * each] for p in range(5)]
        pieces[j] = jnp.concatenate(rows, 0).astype(bf16)


def pieces_sum_kernel(pieces, out):
    f32, bf16 = jnp.float32, jnp.bfloat16
    total = pieces[0].astype(f32)
    for j in range(1, pieces.shape[0]):
        total = total + pieces[j].astype(f32)
    total = total.astype(bf16)
    for j in range(out.shape[0]):
        out[j] = total


def grids_kernel(info, pieces, vis, kcos, ksin, forward, inverse, out, planes, cat, hat):
    f32, bf16 = jnp.float32, jnp.bfloat16
    row_index = info[4]
    core = row_index % 2
    chip = (row_index // 2).astype(f32)
    count = pieces.shape[1]
    each = SG // count
    for h in range(2):
        for j in range(count):
            some = pieces[h, j].astype(f32)
            for p in range(5):
                planes[p, j * each:(j + 1) * each, h * HALF:(h + 1) * HALF] = some[p * each:(p + 1) * each]
    cat[:, :SG] = planes[0].astype(bf16)
    cat[:, SG:] = planes[1].astype(bf16)
    cat[...] = jnp.dot(cat[...], forward[...], preferred_element_type=f32).astype(bf16)
    with_cos = jnp.dot(kcos[...], cat[...], preferred_element_type=f32)
    with_sin = jnp.dot(ksin[...], cat[...], preferred_element_type=f32)
    hat_real = (with_cos[:, :SG] - with_sin[:, SG:]) * (1.0 / SG)
    hat_imag = (with_sin[:, :SG] + with_cos[:, SG:]) * (1.0 / SG)
    hat[:, :SG] = hat_real.astype(bf16)
    hat[:, SG:] = hat_imag.astype(bf16)
    cat[:, :SG] = (planes[2] - planes[4] * hat_real).astype(bf16)
    cat[:, SG:] = (planes[3] - planes[4] * hat_imag).astype(bf16)
    cat[...] = jnp.dot(cat[...], inverse[...], preferred_element_type=f32).astype(bf16)
    with_cos = jnp.dot(kcos[...], cat[...], preferred_element_type=f32)
    with_sin = jnp.dot(ksin[...], cat[...], preferred_element_type=f32)
    real = (with_cos[:, :SG] + with_sin[:, SG:]) * (1.0 / SG)
    imag = (with_cos[:, SG:] - with_sin[:, :SG]) * (1.0 / SG)
    real = jnp.where(core == 0, real[:, :HALF], real[:, HALF:]).astype(bf16)
    imag = jnp.where(core == 0, imag[:, :HALF], imag[:, HALF:]).astype(bf16)
    counter = sublanes(SG).astype(f32)
    each = vis.shape[1] // 2
    for k in range(vis.shape[0]):
        out[k, :SG] = real
        out[k, SG:2 * SG] = imag
        ask = vis_rows(jnp.where(core == 0, vis[k, :each].astype(f32), vis[k, each:].astype(f32)))
        hot = jnp.where((ask[1:2] == counter) & (ask[0:1] == chip), 1.0, 0.0).astype(bf16)
        pick = ask[2:3] == counter
        line = lax.dot_general(hat[...], hot, (((0,), (0,)), ((), ())), preferred_element_type=f32)
        rows = []
        for part in range(2):
            value = jnp.sum(jnp.where(pick, line[part * SG:(part + 1) * SG], 0.0), axis=0, keepdims=True)
            rows += [value[:, i * LANES:(i + 1) * LANES] for i in range(value.shape[1] // LANES)]
        rows.append(jnp.zeros((16 - len(rows), LANES), f32))
        out[k, 2 * SG:] = jnp.concatenate(rows, 0).astype(bf16)


def image_kernel(scale, info, back, row_tab, col_tab, observed, out, residual, grid, both):
    f32, bf16 = jnp.float32, jnp.bfloat16
    core = info[4] % 2
    model = jnp.zeros((16, LANES), f32)
    for s in range(NR * NC):
        model = model + jnp.where(core == 0, back[0, s, 2 * SG:].astype(f32), back[1, s, 2 * SG:].astype(f32))
    count = observed.shape[1] // LANES
    for part in range(2):
        for i in range(count):
            at = slice(i * LANES, (i + 1) * LANES)
            residual[part:part + 1, at] = observed[part:part + 1, at] - model[part * count + i:part * count + i + 1]
    for c in range(NC):
        real = imag = None
        for r in range(NR):
            for k in range(2):
                for half in range(2):
                    at = k * SG + half * HALF
                    grid[:, at:at + HALF] = back[half, r * NC + c, k * SG:(k + 1) * SG]
            cos = jnp.dot(row_tab[2 * r], grid[...], preferred_element_type=f32)
            sin = jnp.dot(row_tab[2 * r + 1], grid[...], preferred_element_type=f32)
            re, im = cos[:, :SG] - sin[:, SG:], cos[:, SG:] + sin[:, :SG]
            real = re if real is None else real + re
            imag = im if imag is None else imag + im
        both[:, :SG] = real.astype(bf16)
        both[:, SG:] = imag.astype(bf16)
        part = jnp.dot(both[:, :SG], col_tab[2 * c], preferred_element_type=f32)
        part = part + jnp.dot(both[:, SG:], col_tab[2 * c + 1], preferred_element_type=f32)
        if c == 0:
            out[...] = part
        else:
            out[...] = (out[...] + part) * scale


def call(kernel, out_shape, name, scratch=(), scalars=0, cost=0):
    smem, vmem = pl.BlockSpec(memory_space=pltpu.SMEM), pl.BlockSpec(memory_space=pltpu.VMEM)

    def run(*args):
        return pl.pallas_call(
            kernel,
            out_shape=out_shape,
            in_specs=[smem] * scalars + [vmem] * (len(args) - scalars),
            out_specs=jax.tree.map(lambda _: vmem, out_shape),
            scratch_shapes=list(scratch),
            compiler_params=pltpu.CompilerParams(vmem_limit_bytes=24 * 2**20),
            cost_estimate=pl.CostEstimate(flops=cost, bytes_accessed=2**20, transcendentals=0),
            name=name,
        )(*args)

    return run


def grid_tables():
    counter = np.arange(SG)
    angles = (counter[:, None] * counter[None, :] % SG).astype(np.float64) * (2.0 * math.pi / SG)
    return np.cos(angles).astype(ml_dtypes.bfloat16), np.sin(angles).astype(ml_dtypes.bfloat16)


def exchange(blocks, axes, groups):
    return lax.all_to_all(blocks, axes, 0, 0, tiled=True, axis_index_groups=groups)


def shape(*dims, dtype=jnp.bfloat16):
    return jax.ShapeDtypeStruct(dims, dtype)


def shards(facet, row_offsets, col_offsets, vis_subgrid, vis_u, vis_v, observed):
    f32, bf16 = jnp.float32, jnp.bfloat16
    rows_count, cols_count = lax.axis_size("frow"), lax.axis_size("fcol")
    side = facet.shape[0]
    n_vis = vis_u.shape[0]
    chips = rows_count // 2
    each = SG // cols_count
    x_groups = [[2 * chip + core for chip in range(chips)] for core in range(2)]
    core_groups = [[2 * chip, 2 * chip + 1] for chip in range(chips)]
    row_index, col_index = lax.axis_index("frow"), lax.axis_index("fcol")
    scale_in = 1.0 / (side * math.sqrt(rows_count * cols_count))
    scale_out = 1.0 / (SG * math.sqrt(NR * NC))
    info = jnp.concatenate([row_offsets, col_offsets, jnp.stack([row_index, col_index])]).astype(jnp.int32)

    halves = call(
        functools.partial(columns_kernel, cols_count), shape(2, side + 16, 4 * HALF), "columns",
        scratch=[pltpu.VMEM((side, 8 * HALF), bf16)], scalars=1, cost=10**9,
    )(info, facet, vis_subgrid.reshape(1, n_vis), vis_u.reshape(1, n_vis), vis_v.reshape(1, n_vis), observed)
    halves = exchange(halves, "frow", core_groups)
    row_tab = call(
        functools.partial(row_tables_kernel, rows_count, side), shape(4, SG, 2 * side), "row_tables", scalars=1, cost=10**9
    )(info)
    vis_rows_count = 16 * 2 * n_vis // LANES
    parts = call(
        functools.partial(contributions_kernel, scale_in), shape(NR * NC, 2 * SG + vis_rows_count, HALF), "contributions",
        scratch=[pltpu.VMEM((2 * side, 4 * HALF), bf16)], cost=2 * 10**9,
    )(halves, row_tab)
    parts = exchange(parts, "frow", x_groups)

    pieces = call(
        gridding_kernel, shape(cols_count, 5 * each, HALF), "gridding",
        scratch=[pltpu.VMEM((5, SG, HALF), f32)], scalars=1, cost=10**9,
    )(info, parts)
    pieces = exchange(pieces, "fcol", None)
    pieces = call(pieces_sum_kernel, shape(cols_count, 5 * each, HALF), "pieces_sum", cost=10**6)(pieces)
    pieces = exchange(pieces, "fcol", None)
    pieces = exchange(jnp.broadcast_to(pieces, (2,) + pieces.shape), "frow", core_groups)

    kcos, ksin = grid_tables()
    forward_block = np.concatenate([np.concatenate([kcos, ksin], 1), np.concatenate([-ksin, kcos], 1)], 0)
    inverse_block = np.concatenate([np.concatenate([kcos, -ksin], 1), np.concatenate([ksin, kcos], 1)], 0)
    back = call(
        grids_kernel, shape(chips, 2 * SG + 16, HALF), "grids",
        scratch=[pltpu.VMEM((5, SG, SG), f32), pltpu.VMEM((SG, 2 * SG), bf16), pltpu.VMEM((SG, 2 * SG), bf16)],
        scalars=1, cost=10**9,
    )(info, pieces, parts[:, 2 * SG:], kcos, ksin, forward_block, inverse_block)
    back = exchange(back, "frow", x_groups)
    back = exchange(jnp.broadcast_to(back, (2,) + back.shape), "frow", core_groups)

    back_row, back_col = call(
        functools.partial(back_tables_kernel, rows_count, cols_count, side),
        (shape(4, side, SG), shape(4, SG, side)), "back_tables", scalars=1, cost=10**9,
    )(info)
    return call(
        functools.partial(image_kernel, scale_out),
        (shape(side, side, dtype=f32), shape(2, n_vis, dtype=f32)), "image",
        scratch=[pltpu.VMEM((SG, 2 * SG), bf16), pltpu.VMEM((side, 2 * SG), bf16)], scalars=1, cost=2 * 10**9,
    )(info, back, back_row, back_col, observed)


def solution(mesh):
    in_specs = (
        P("frow", "fcol"),
        P(),
        P(),
        P(("frow", "fcol")),
        P(("frow", "fcol")),
        P(("frow", "fcol")),
        P(None, ("frow", "fcol")),
    )
    out_specs = (P("frow", "fcol"), P(None, ("frow", "fcol")))
    return jax.shard_map(shards, mesh=mesh, in_specs=in_specs, out_specs=out_specs, check_vma=False)
```

```python
import functools
import math

import jax
import jax.numpy as jnp
import ml_dtypes
import numpy as np
from jax import lax
from jax.experimental import pallas as pl
from jax.experimental.pallas import tpu as pltpu
from jax.sharding import PartitionSpec as P

SKY = 65536
SG = 256
NR = 2
NC = 2
HALF = SG // 2
LANES = 128


def wave(count):
    count = count & (SKY - 1)
    turned = count + SKY // 8
    near = (turned & (SKY // 4 - 1)) - SKY // 8
    quarter = lax.shift_right_logical(turned, 14) & 3
    t = near.astype(jnp.float32) * (2.0 * math.pi / SKY)
    q = t * t
    sin = t * (1.0 + q * (-1.0 / 6 + q * (1.0 / 120 + q * (-1.0 / 5040 + q * (1.0 / 362880)))))
    cos = 1.0 + q * (-0.5 + q * (1.0 / 24 + q * (-1.0 / 720 + q * (1.0 / 40320))))
    odd = (quarter & 1) == 1
    one, two = jnp.where(odd, sin, cos), jnp.where(odd, cos, sin)
    return (
        jnp.where((quarter == 1) | (quarter == 2), -one, one),
        jnp.where(quarter >= 2, -two, two),
    )


def lanes(n):
    return lax.broadcasted_iota(jnp.int32, (1, n), 1)


def sublanes(n):
    return lax.broadcasted_iota(jnp.int32, (n, 1), 0)


def spread(coarse, fine, store):
    for k in range(coarse[0].shape[0]):
        c, s = coarse[0][k:k + 1], coarse[1][k:k + 1]
        store(k * 16, c * fine[0] - s * fine[1], s * fine[0] + c * fine[1])


def place():
    return lax.axis_index("frow"), lax.axis_index("fcol")


def columns_kernel(cols_count, offsets, facet, subgrid, u, v, observed, out, col_tab, image, indices, seen, sems):
    f32, bf16 = jnp.float32, jnp.bfloat16
    side = facet.shape[0]
    copies = [
        pltpu.make_async_copy(facet, image, sems.at[0]),
        pltpu.make_async_copy(subgrid, indices.at[0], sems.at[1]),
        pltpu.make_async_copy(u, indices.at[1], sems.at[2]),
        pltpu.make_async_copy(v, indices.at[2], sems.at[3]),
        pltpu.make_async_copy(observed, seen, sems.at[4]),
    ]
    for copy in copies:
        copy.start()
    _, col_index = place()
    unit = sublanes(16)
    col_step = SKY // (cols_count * side)
    col_base = col_index * (SKY // cols_count)
    for c in range(NC):
        freq = offsets[c] + lanes(SG)
        coarse = wave((col_base + 16 * col_step * sublanes(side // 16)) * freq)
        fine = wave((col_step * unit) * freq)

        def store(at, cos, sin, c=c):
            for h in range(2):
                half = slice(h * HALF, (h + 1) * HALF)
                left = (2 * h + c) * SG
                col_tab[at:at + 16, left:left + HALF] = cos[:, half].astype(bf16)
                col_tab[at:at + 16, left + HALF:left + SG] = sin[:, half].astype(bf16)

        spread(coarse, fine, store)
    for copy in copies:
        copy.wait()
    vis = jnp.concatenate([indices[n].astype(f32) for n in range(3)] + [seen[...], jnp.zeros((3, side), f32)], 0)
    vis = jnp.concatenate([vis[:, :side // 2], vis[:, side // 2:]], 0).astype(bf16)
    for h in range(2):
        part = jnp.dot(image[...], col_tab[:, 2 * h * SG:2 * (h + 1) * SG], preferred_element_type=f32)
        out[h, :side] = part.astype(bf16)
        out[h, side:, :side // 2] = vis
        out[h, side:, side // 2:] = vis


def row_tables_kernel(rows_count, side, offsets, row_tab):
    bf16 = jnp.bfloat16
    row_index, _ = place()
    chip = row_index // 2
    unit = sublanes(16)
    row_step = SKY // (rows_count * side)
    for f in range(2):
        pos = (2 * chip + f) * (SKY // rows_count) + row_step * lanes(side)
        fine = wave(unit * pos)
        for r in range(NR):
            coarse = wave((offsets[r] + 16 * unit) * pos)

            def store(at, cos, sin, r=r, f=f):
                row_tab[2 * r, at:at + 16, f * side:(f + 1) * side] = cos.astype(bf16)
                row_tab[2 * r + 1, at:at + 16, f * side:(f + 1) * side] = sin.astype(bf16)

            spread(coarse, fine, store)


def contributions_kernel(scale, halves, row_tab, out, right):
    f32, bf16 = jnp.float32, jnp.bfloat16
    side = row_tab.shape[2] // 2
    vis = []
    for f in range(2):
        right[f * side:(f + 1) * side] = halves[f, :side]
        some = halves[f, side:]
        vis += [some[:, k * LANES:(k + 1) * LANES] for k in range(side // 2 // LANES)]
    for s in range(NR * NC):
        for k, some in enumerate(vis):
            at = 2 * SG + 16 * k
            out[s, at:at + 16] = some
    for r in range(NR):
        with_cos = jnp.dot(row_tab[2 * r], right[...], preferred_element_type=f32)
        with_sin = jnp.dot(row_tab[2 * r + 1], right[...], preferred_element_type=f32)
        for c in range(NC):
            at = 2 * c * HALF
            cp, cq = with_cos[:, at:at + HALF], with_cos[:, at + HALF:at + 2 * HALF]
            sp, sq = with_sin[:, at:at + HALF], with_sin[:, at + HALF:at + 2 * HALF]
            out[r * NC + c, :SG] = ((cp - sq) * scale).astype(bf16)
            out[r * NC + c, SG:2 * SG] = (-(cq + sp) * scale).astype(bf16)


def vis_rows(block):
    count = block.shape[0] // 16
    return jnp.concatenate(
        [block[16 * k + 8 * part:16 * k + 8 * part + 8] for part in range(2) for k in range(count)], 1
    )


def gridding_kernel(parts, pieces, planes):
    f32, bf16 = jnp.float32, jnp.bfloat16
    row_index, _ = place()
    chip = (row_index // 2).astype(f32)
    v_at = (sublanes(HALF) + (row_index % 2) * HALF).astype(f32)
    counter = sublanes(SG).astype(f32)
    count = parts.shape[0]
    total = jnp.zeros((SG, 3 * HALF), f32)
    for k in range(count):
        one = vis_rows(parts[k, 2 * SG:].astype(f32))
        u_here = jnp.where(one[0:1] == chip, one[1:2], -1.0)
        hot = jnp.where(u_here == counter, 1.0, 0.0).astype(bf16)
        pick = one[2:3] == v_at
        right = jnp.concatenate(
            [jnp.where(pick, one[3:4], 0.0), jnp.where(pick, one[4:5], 0.0), jnp.where(pick, 1.0, 0.0)], 0
        ).astype(bf16)
        total = total + lax.dot_general(hot, right, (((1,), (1,)), ((), ())), preferred_element_type=f32)
    for p in range(2):
        some = parts[0, p * SG:(p + 1) * SG].astype(f32)
        for k in range(1, count):
            some = some + parts[k, p * SG:(p + 1) * SG].astype(f32)
        planes[p] = some
    for p in range(3):
        planes[2 + p] = total[:, p * HALF:(p + 1) * HALF]
    each = SG // pieces.shape[0]
    for j in range(pieces.shape[0]):
        rows = [planes[p, j * each:(j + 1) * each] for p in range(5)]
        pieces[j] = jnp.concatenate(rows, 0).astype(bf16)


def pieces_sum_kernel(pieces, out):
    f32, bf16 = jnp.float32, jnp.bfloat16
    total = pieces[0].astype(f32)
    for j in range(1, pieces.shape[0]):
        total = total + pieces[j].astype(f32)
    total = total.astype(bf16)
    for j in range(out.shape[0]):
        out[j] = total


def grids_kernel(pieces, parts, grid_left, forward, inverse_left, inverse, out, planes, cat, tall, hat):
    f32, bf16 = jnp.float32, jnp.bfloat16
    row_index, _ = place()
    core = row_index % 2
    chip = (row_index // 2).astype(f32)
    count = pieces.shape[1]
    each = SG // count
    for h in range(2):
        for j in range(count):
            some = pieces[h, j].astype(f32)
            for p in range(5):
                planes[p, j * each:(j + 1) * each, h * HALF:(h + 1) * HALF] = some[p * each:(p + 1) * each]
    cat[:, :SG] = planes[0].astype(bf16)
    cat[:, SG:] = planes[1].astype(bf16)
    wide = jnp.dot(cat[...], forward[...], preferred_element_type=f32).astype(bf16)
    tall[:SG] = wide[:, :SG]
    tall[SG:] = wide[:, SG:]
    model = jnp.dot(grid_left[...], tall[...], preferred_element_type=f32) * (1.0 / SG)
    hat_real, hat_imag = model[:SG], model[SG:]
    cat[:, :SG] = (planes[2] - planes[4] * hat_real).astype(bf16)
    cat[:, SG:] = (planes[3] - planes[4] * hat_imag).astype(bf16)
    hat[:, :SG] = hat_real.astype(bf16)
    hat[:, SG:] = hat_imag.astype(bf16)
    wide = jnp.dot(cat[...], inverse[...], preferred_element_type=f32)
    for k in range(2):
        some = wide[:, k * SG:(k + 1) * SG]
        tall[k * SG:(k + 1) * SG, :HALF] = jnp.where(core == 0, some[:, :HALF], some[:, HALF:]).astype(bf16)
    back = jnp.dot(inverse_left[...], tall[:, :HALF], preferred_element_type=f32) * (1.0 / SG)
    back = back.astype(bf16)
    counter = sublanes(SG).astype(f32)
    vis_each = (parts.shape[1] - 2 * SG) // 2
    for k in range(parts.shape[0]):
        out[k, :2 * SG] = back
        first = parts[k, 2 * SG:2 * SG + vis_each].astype(f32)
        second = parts[k, 2 * SG + vis_each:].astype(f32)
        ask = vis_rows(jnp.where(core == 0, first, second))
        u_here = jnp.where(ask[0:1] == chip, ask[1:2], -1.0)
        hot = jnp.where(u_here == counter, 1.0, 0.0).astype(bf16)
        pick = ask[2:3] == counter
        line = lax.dot_general(hat[...], hot, (((0,), (0,)), ((), ())), preferred_element_type=f32)
        rows = []
        for part in range(2):
            value = jnp.sum(jnp.where(pick, line[part * SG:(part + 1) * SG], 0.0), axis=0, keepdims=True)
            rows += [value[:, i * LANES:(i + 1) * LANES] for i in range(value.shape[1] // LANES)]
        rows.append(jnp.zeros((16 - len(rows), LANES), f32))
        out[k, 2 * SG:] = jnp.concatenate(rows, 0).astype(bf16)


def back_tables_kernel(rows_count, cols_count, side, offsets_row, offsets_col, row_tab, col_tab):
    bf16 = jnp.bfloat16
    row_index, col_index = place()
    unit = sublanes(16)
    row_step = SKY // (rows_count * side)
    row_base = row_index * (SKY // rows_count)
    for r in range(NR):
        freq = offsets_row[r] + lanes(SG)
        coarse = wave((row_base + 16 * row_step * sublanes(side // 16)) * freq)
        fine = wave((row_step * unit) * freq)

        def store(at, cos, sin, r=r):
            row_tab[at:at + 16, 2 * r * SG:(2 * r + 1) * SG] = cos.astype(bf16)
            row_tab[at:at + 16, (2 * r + 1) * SG:(2 * r + 2) * SG] = sin.astype(bf16)

        spread(coarse, fine, store)
    col_step = SKY // (cols_count * side)
    pos = col_index * (SKY // cols_count) + col_step * lanes(side)
    fine = wave(unit * pos)
    for c in range(NC):
        coarse = wave((offsets_col[c] + 16 * unit) * pos)

        def store(at, cos, sin, c=c):
            left = 2 * c * SG + at
            col_tab[left:left + 16] = cos.astype(bf16)
            col_tab[left + SG:left + SG + 16] = (-sin).astype(bf16)

        spread(coarse, fine, store)


def image_kernel(scale, back, row_tab, col_tab, observed, out, residual, right, both, image, seen, sems):
    f32, bf16 = jnp.float32, jnp.bfloat16
    row_index, _ = place()
    core = row_index % 2
    fetch = pltpu.make_async_copy(observed, seen, sems.at[0])
    fetch.start()
    for c in range(NC):
        for r in range(NR):
            for half in range(2):
                real = back[half, r * NC + c, :SG]
                imag = back[half, r * NC + c, SG:2 * SG]
                top, at = 2 * r * SG, half * HALF
                right[top:top + SG, at:at + HALF] = real
                right[top:top + SG, SG + at:SG + at + HALF] = imag
                right[top + SG:top + 2 * SG, at:at + HALF] = -imag
                right[top + SG:top + 2 * SG, SG + at:SG + at + HALF] = real
        part = jnp.dot(row_tab[...], right[...], preferred_element_type=f32)
        both[:, 2 * c * SG:2 * (c + 1) * SG] = part.astype(bf16)
    chunks = sems.shape[0] - 1
    side = both.shape[0]
    step = side // chunks
    writes = []
    for n in range(chunks):
        at = slice(n * step, (n + 1) * step)
        image[at] = jnp.dot(both[at], col_tab[...], preferred_element_type=f32) * scale
        write = pltpu.make_async_copy(image.at[at], out.at[at], sems.at[1 + n])
        write.start()
        writes.append(write)
    fetch.wait()
    model = jnp.zeros((16, LANES), f32)
    for s in range(NR * NC):
        model = model + jnp.where(core == 0, back[0, s, 2 * SG:].astype(f32), back[1, s, 2 * SG:].astype(f32))
    count = observed.shape[1] // LANES
    for part in range(2):
        for i in range(count):
            at = slice(i * LANES, (i + 1) * LANES)
            residual[part:part + 1, at] = seen[part:part + 1, at] - model[part * count + i:part * count + i + 1]
    for write in writes:
        write.wait()


def call(kernel, out_shape, name, spaces, scratch=(), cost=0, outs=None, room=24):
    kinds = {"s": pltpu.SMEM, "v": pltpu.VMEM, "a": pl.ANY}
    several = isinstance(out_shape, tuple)
    outs = outs or "v" * (len(out_shape) if several else 1)
    out_specs = tuple(pl.BlockSpec(memory_space=kinds[kind]) for kind in outs)
    return pl.pallas_call(
        kernel,
        out_shape=out_shape,
        in_specs=[pl.BlockSpec(memory_space=kinds[kind]) for kind in spaces],
        out_specs=out_specs if several else out_specs[0],
        scratch_shapes=list(scratch),
        compiler_params=pltpu.CompilerParams(vmem_limit_bytes=room * 2**20),
        cost_estimate=pl.CostEstimate(flops=cost, bytes_accessed=2**20, transcendentals=0),
        name=name,
    )


def grid_tables():
    counter = np.arange(SG)
    angles = (counter[:, None] * counter[None, :] % SG).astype(np.float64) * (2.0 * math.pi / SG)
    return np.cos(angles).astype(ml_dtypes.bfloat16), np.sin(angles).astype(ml_dtypes.bfloat16)


def exchange(blocks, axes, groups):
    return lax.all_to_all(blocks, axes, 0, 0, tiled=True, axis_index_groups=groups)


def shape(*dims, dtype=jnp.bfloat16):
    return jax.ShapeDtypeStruct(dims, dtype)


def shards(facet, row_offsets, col_offsets, vis_subgrid, vis_u, vis_v, observed):
    f32, bf16 = jnp.float32, jnp.bfloat16
    rows_count, cols_count = lax.axis_size("frow"), lax.axis_size("fcol")
    side = facet.shape[0]
    n_vis = vis_u.shape[0]
    chips = rows_count // 2
    each = SG // cols_count
    x_groups = [[2 * chip + core for chip in range(chips)] for core in range(2)]
    core_groups = [[2 * chip, 2 * chip + 1] for chip in range(chips)]
    scale_in = 1.0 / (side * math.sqrt(rows_count * cols_count))
    scale_out = 1.0 / (SG * math.sqrt(NR * NC))
    line = (1, n_vis)

    halves = call(
        functools.partial(columns_kernel, cols_count), shape(2, side + 16, 4 * HALF), "columns", "saaaaa",
        scratch=[
            pltpu.VMEM((side, 8 * HALF), bf16), pltpu.VMEM((side, side), bf16), pltpu.VMEM((3,) + line, jnp.int32),
            pltpu.VMEM((2, n_vis), f32), pltpu.SemaphoreType.DMA((5,)),
        ],
        cost=10**9, room=60,
    )(col_offsets, facet, vis_subgrid.reshape(line), vis_u.reshape(line), vis_v.reshape(line), observed)
    halves = exchange(halves, "frow", core_groups)
    row_tab = call(
        functools.partial(row_tables_kernel, rows_count, side), shape(4, SG, 2 * side), "row_tables", "s", cost=10**9
    )(row_offsets)
    vis_rows_count = 8 * 2 * n_vis // LANES
    parts = call(
        functools.partial(contributions_kernel, scale_in), shape(NR * NC, 2 * SG + vis_rows_count, HALF),
        "contributions", "vv", scratch=[pltpu.VMEM((2 * side, 4 * HALF), bf16)], cost=2 * 10**9,
    )(halves, row_tab)
    parts = exchange(parts, "frow", x_groups)

    pieces = call(
        gridding_kernel, shape(cols_count, 5 * each, HALF), "gridding", "v",
        scratch=[pltpu.VMEM((5, SG, HALF), f32)], cost=10**9,
    )(parts)
    pieces = exchange(pieces, "fcol", None)
    pieces = call(pieces_sum_kernel, shape(cols_count, 5 * each, HALF), "pieces_sum", "v", cost=10**6)(pieces)
    pieces = exchange(pieces, "fcol", None)
    pieces = exchange(jnp.broadcast_to(pieces, (2,) + pieces.shape), "frow", core_groups)

    kcos, ksin = grid_tables()
    block = [np.concatenate(pair, 1) for pair in ((kcos, ksin), (-ksin, kcos), (kcos, -ksin), (ksin, kcos))]
    forward_block = np.concatenate([block[0], block[1]], 0)
    inverse_block = np.concatenate([block[2], block[3]], 0)
    back = call(
        grids_kernel, shape(chips, 2 * SG + 16, HALF), "grids", "vvvvvv",
        scratch=[
            pltpu.VMEM((5, SG, SG), f32), pltpu.VMEM((SG, 2 * SG), bf16), pltpu.VMEM((2 * SG, SG), bf16),
            pltpu.VMEM((SG, 2 * SG), bf16),
        ],
        cost=10**9,
    )(pieces, parts, inverse_block, forward_block, forward_block, inverse_block)
    back = exchange(back, "frow", x_groups)
    back = exchange(jnp.broadcast_to(back, (2,) + back.shape), "frow", core_groups)

    back_row, back_col = call(
        functools.partial(back_tables_kernel, rows_count, cols_count, side),
        (shape(side, 4 * SG), shape(4 * SG, side)), "back_tables", "ss", cost=10**9,
    )(row_offsets, col_offsets)
    chunks = 4
    return call(
        functools.partial(image_kernel, scale_out),
        (shape(side, side, dtype=f32), shape(2, n_vis, dtype=f32)), "image", "vvva", outs="av",
        scratch=[
            pltpu.VMEM((4 * SG, 2 * SG), bf16), pltpu.VMEM((side, 4 * SG), bf16), pltpu.VMEM((side, side), f32),
            pltpu.VMEM((2, n_vis), f32), pltpu.SemaphoreType.DMA((1 + chunks,)),
        ],
        cost=2 * 10**9,
    )(back, back_row, back_col, observed)


def solution(mesh):
    in_specs = (
        P("frow", "fcol"),
        P(),
        P(),
        P(("frow", "fcol")),
        P(("frow", "fcol")),
        P(("frow", "fcol")),
        P(None, ("frow", "fcol")),
    )
    out_specs = (P("frow", "fcol"), P(None, ("frow", "fcol")))
    return jax.shard_map(shards, mesh=mesh, in_specs=in_specs, out_specs=out_specs, check_vma=False)
```

```python
import functools
import math

import jax
import jax.numpy as jnp
import ml_dtypes
import numpy as np
from jax import lax
from jax.experimental import pallas as pl
from jax.experimental.pallas import tpu as pltpu
from jax.sharding import PartitionSpec as P

SKY = 65536
SG = 256
NR = 2
NC = 2
HALF = SG // 2
LANES = 128


def wave(count):
    count = count & (SKY - 1)
    turned = count + SKY // 8
    near = (turned & (SKY // 4 - 1)) - SKY // 8
    quarter = lax.shift_right_logical(turned, 14) & 3
    t = near.astype(jnp.float32) * (2.0 * math.pi / SKY)
    q = t * t
    sin = t * (1.0 + q * (-1.0 / 6 + q * (1.0 / 120 + q * (-1.0 / 5040 + q * (1.0 / 362880)))))
    cos = 1.0 + q * (-0.5 + q * (1.0 / 24 + q * (-1.0 / 720 + q * (1.0 / 40320))))
    odd = (quarter & 1) == 1
    one, two = jnp.where(odd, sin, cos), jnp.where(odd, cos, sin)
    return (
        jnp.where((quarter == 1) | (quarter == 2), -one, one),
        jnp.where(quarter >= 2, -two, two),
    )


def lanes(n):
    return lax.broadcasted_iota(jnp.int32, (1, n), 1)


def sublanes(n):
    return lax.broadcasted_iota(jnp.int32, (n, 1), 0)


def spread(coarse, fine, store):
    for k in range(coarse[0].shape[0]):
        c, s = coarse[0][k:k + 1], coarse[1][k:k + 1]
        store(k * 16, c * fine[0] - s * fine[1], s * fine[0] + c * fine[1])


def place():
    return lax.axis_index("frow"), lax.axis_index("fcol")


def columns_kernel(cols_count, offsets, facet, subgrid, u, v, observed, own, send, col_tab, image, indices, seen, sems):
    f32, bf16 = jnp.float32, jnp.bfloat16
    side = facet.shape[0]
    copies = [
        pltpu.make_async_copy(facet, image, sems.at[0]),
        pltpu.make_async_copy(subgrid, indices.at[0], sems.at[1]),
        pltpu.make_async_copy(u, indices.at[1], sems.at[2]),
        pltpu.make_async_copy(v, indices.at[2], sems.at[3]),
        pltpu.make_async_copy(observed, seen, sems.at[4]),
    ]
    for copy in copies:
        copy.start()
    row_index, col_index = place()
    core = row_index % 2
    unit = sublanes(16)
    col_step = SKY // (cols_count * side)
    col_base = col_index * (SKY // cols_count)
    for c in range(NC):
        freq = offsets[c] + lanes(SG)
        coarse = wave((col_base + 16 * col_step * sublanes(side // 16)) * freq)
        fine = wave((col_step * unit) * freq)

        def store(at, cos, sin, c=c):
            for h in range(2):
                half = slice(h * HALF, (h + 1) * HALF)
                left = (2 * h + c) * SG
                col_tab[at:at + 16, left:left + HALF] = cos[:, half].astype(bf16)
                col_tab[at:at + 16, left + HALF:left + SG] = sin[:, half].astype(bf16)

        spread(coarse, fine, store)
    for copy in copies:
        copy.wait()
    vis = jnp.concatenate([indices[n].astype(f32) for n in range(3)] + [seen[...], jnp.zeros((3, side), f32)], 0)
    vis = jnp.concatenate([vis[:, :side // 2], vis[:, side // 2:]], 0).astype(bf16)
    for out, half in ((send, 1 - core), (own, core)):
        tab = col_tab[:, pl.ds(pl.multiple_of(half * 2 * SG, 2 * SG), 2 * SG)]
        out[:side] = jnp.dot(image[...], tab, preferred_element_type=f32).astype(bf16)
        out[side:, :side // 2] = vis
        out[side:, side // 2:] = vis


def row_tables_kernel(rows_count, side, offsets, row_tab):
    bf16 = jnp.bfloat16
    row_index, _ = place()
    unit = sublanes(16)
    row_step = SKY // (rows_count * side)
    for f in range(2):
        pos = (row_index ^ f) * (SKY // rows_count) + row_step * lanes(side)
        fine = wave(unit * pos)
        for r in range(NR):
            coarse = wave((offsets[r] + 16 * unit) * pos)

            def store(at, cos, sin, r=r, f=f):
                row_tab[2 * r, at:at + 16, f * side:(f + 1) * side] = cos.astype(bf16)
                row_tab[2 * r + 1, at:at + 16, f * side:(f + 1) * side] = sin.astype(bf16)

            spread(coarse, fine, store)


def contributions_kernel(scale, own, other, row_tab, out, right):
    f32, bf16 = jnp.float32, jnp.bfloat16
    side = row_tab.shape[2] // 2
    vis = []
    for f, half in enumerate((own, other)):
        right[f * side:(f + 1) * side] = half[:side]
        some = half[side:]
        vis += [some[:, k * LANES:(k + 1) * LANES] for k in range(side // 2 // LANES)]
    for s in range(NR * NC):
        for k, some in enumerate(vis):
            at = 2 * SG + 16 * k
            out[s, at:at + 16] = some
    for r in range(NR):
        with_cos = jnp.dot(row_tab[2 * r], right[...], preferred_element_type=f32)
        with_sin = jnp.dot(row_tab[2 * r + 1], right[...], preferred_element_type=f32)
        for c in range(NC):
            at = 2 * c * HALF
            cp, cq = with_cos[:, at:at + HALF], with_cos[:, at + HALF:at + 2 * HALF]
            sp, sq = with_sin[:, at:at + HALF], with_sin[:, at + HALF:at + 2 * HALF]
            out[r * NC + c, :SG] = ((cp - sq) * scale).astype(bf16)
            out[r * NC + c, SG:2 * SG] = (-(cq + sp) * scale).astype(bf16)


def vis_rows(block):
    count = block.shape[0] // 16
    return jnp.concatenate(
        [block[16 * k + 8 * part:16 * k + 8 * part + 8] for part in range(2) for k in range(count)], 1
    )


def gridding_kernel(parts, pieces, planes):
    f32, bf16 = jnp.float32, jnp.bfloat16
    row_index, _ = place()
    chip = (row_index // 2).astype(f32)
    v_at = (sublanes(HALF) + (row_index % 2) * HALF).astype(f32)
    counter = sublanes(SG).astype(f32)
    count = parts.shape[0]
    total = jnp.zeros((SG, 3 * HALF), f32)
    for k in range(count):
        one = vis_rows(parts[k, 2 * SG:].astype(f32))
        u_here = jnp.where(one[0:1] == chip, one[1:2], -1.0)
        hot = jnp.where(u_here == counter, 1.0, 0.0).astype(bf16)
        pick = one[2:3] == v_at
        right = jnp.concatenate(
            [jnp.where(pick, one[3:4], 0.0), jnp.where(pick, one[4:5], 0.0), jnp.where(pick, 1.0, 0.0)], 0
        ).astype(bf16)
        total = total + lax.dot_general(hot, right, (((1,), (1,)), ((), ())), preferred_element_type=f32)
    for p in range(2):
        some = parts[0, p * SG:(p + 1) * SG].astype(f32)
        for k in range(1, count):
            some = some + parts[k, p * SG:(p + 1) * SG].astype(f32)
        planes[p] = some
    for p in range(3):
        planes[2 + p] = total[:, p * HALF:(p + 1) * HALF]
    each = SG // pieces.shape[0]
    for j in range(pieces.shape[0]):
        rows = [planes[p, j * each:(j + 1) * each] for p in range(5)]
        pieces[j] = jnp.concatenate(rows, 0).astype(bf16)


def pieces_sum_kernel(pieces, out):
    f32, bf16 = jnp.float32, jnp.bfloat16
    total = pieces[0].astype(f32)
    for j in range(1, pieces.shape[0]):
        total = total + pieces[j].astype(f32)
    total = total.astype(bf16)
    for j in range(out.shape[0]):
        out[j] = total


def grids_kernel(own, other, parts, grid_left, forward, inverse_left, inverse, _, out, planes, cat, tall, hat):
    f32, bf16 = jnp.float32, jnp.bfloat16
    row_index, _ = place()
    core = row_index % 2
    chip = (row_index // 2).astype(f32)
    count = own.shape[0]
    each = SG // count
    for pieces, half in ((own, core), (other, 1 - core)):
        at = pl.ds(pl.multiple_of(half * HALF, HALF), HALF)
        for j in range(count):
            some = pieces[j].astype(f32)
            for p in range(5):
                planes[p, j * each:(j + 1) * each, at] = some[p * each:(p + 1) * each]
    cat[:, :SG] = planes[0].astype(bf16)
    cat[:, SG:] = planes[1].astype(bf16)
    wide = jnp.dot(cat[...], forward[...], preferred_element_type=f32).astype(bf16)
    tall[:SG] = wide[:, :SG]
    tall[SG:] = wide[:, SG:]
    model = jnp.dot(grid_left[...], tall[...], preferred_element_type=f32) * (1.0 / SG)
    hat_real, hat_imag = model[:SG], model[SG:]
    cat[:, :SG] = (planes[2] - planes[4] * hat_real).astype(bf16)
    cat[:, SG:] = (planes[3] - planes[4] * hat_imag).astype(bf16)
    hat[:, :SG] = hat_real.astype(bf16)
    hat[:, SG:] = hat_imag.astype(bf16)
    wide = jnp.dot(cat[...], inverse[...], preferred_element_type=f32)
    for k in range(2):
        some = wide[:, k * SG:(k + 1) * SG]
        tall[k * SG:(k + 1) * SG, :HALF] = jnp.where(core == 0, some[:, :HALF], some[:, HALF:]).astype(bf16)
    back = jnp.dot(inverse_left[...], tall[:, :HALF], preferred_element_type=f32) * (1.0 / SG)
    back = back.astype(bf16)
    counter = sublanes(SG).astype(f32)
    vis_each = (parts.shape[1] - 2 * SG) // 2
    for k in range(parts.shape[0]):
        out[k, :2 * SG] = back
        ask = vis_rows(parts[k, 2 * SG:2 * SG + vis_each].astype(f32))
        u_here = jnp.where(ask[0:1] == chip, ask[1:2], -1.0)
        hot = jnp.where(u_here == counter, 1.0, 0.0).astype(bf16)
        pick = ask[2:3] == counter
        line = lax.dot_general(hat[...], hot, (((0,), (0,)), ((), ())), preferred_element_type=f32)
        rows = []
        for part in range(2):
            value = jnp.sum(jnp.where(pick, line[part * SG:(part + 1) * SG], 0.0), axis=0, keepdims=True)
            rows += [value[:, i * LANES:(i + 1) * LANES] for i in range(value.shape[1] // LANES)]
        rows.append(jnp.zeros((16 - len(rows), LANES), f32))
        out[k, 2 * SG:] = jnp.concatenate(rows, 0).astype(bf16)


def back_tables_kernel(rows_count, cols_count, side, offsets_row, offsets_col, row_tab, col_tab):
    bf16 = jnp.bfloat16
    row_index, col_index = place()
    unit = sublanes(16)
    row_step = SKY // (rows_count * side)
    row_base = row_index * (SKY // rows_count)
    for r in range(NR):
        freq = offsets_row[r] + lanes(SG)
        coarse = wave((row_base + 16 * row_step * sublanes(side // 16)) * freq)
        fine = wave((row_step * unit) * freq)

        def store(at, cos, sin, r=r):
            row_tab[at:at + 16, 2 * r * SG:(2 * r + 1) * SG] = cos.astype(bf16)
            row_tab[at:at + 16, (2 * r + 1) * SG:(2 * r + 2) * SG] = sin.astype(bf16)

        spread(coarse, fine, store)
    col_step = SKY // (cols_count * side)
    pos = col_index * (SKY // cols_count) + col_step * lanes(side)
    fine = wave(unit * pos)
    for c in range(NC):
        coarse = wave((offsets_col[c] + 16 * unit) * pos)

        def store(at, cos, sin, c=c):
            left = (at // HALF * 2 * NC + 2 * c) * HALF + at % HALF
            col_tab[left:left + 16] = cos.astype(bf16)
            col_tab[left + HALF:left + HALF + 16] = (-sin).astype(bf16)

        spread(coarse, fine, store)


def half_image(back, half, row_tab, col_tab, right, both):
    f32, bf16 = jnp.float32, jnp.bfloat16
    for c in range(NC):
        for r in range(NR):
            real = back[r * NC + c, :SG]
            imag = back[r * NC + c, SG:2 * SG]
            top, at = 2 * r * SG, 2 * c * HALF
            right[top:top + SG, at:at + HALF] = real
            right[top:top + SG, at + HALF:at + 2 * HALF] = imag
            right[top + SG:top + 2 * SG, at:at + HALF] = -imag
            right[top + SG:top + 2 * SG, at + HALF:at + 2 * HALF] = real
    both[...] = jnp.dot(row_tab[...], right[...], preferred_element_type=f32).astype(bf16)
    depth = 2 * NC * HALF
    rows = pl.ds(pl.multiple_of(half * depth, depth), depth)
    return lambda at: jnp.dot(both[at], col_tab[rows], preferred_element_type=f32)


def own_image_kernel(back, row_tab, col_tab, observed, out, residual, right, both):
    f32 = jnp.float32
    row_index, _ = place()
    model = jnp.zeros((16, LANES), f32)
    for s in range(NR * NC):
        model = model + back[s, 2 * SG:].astype(f32)
    count = observed.shape[1] // LANES
    for part in range(2):
        for i in range(count):
            at = slice(i * LANES, (i + 1) * LANES)
            residual[part:part + 1, at] = observed[part:part + 1, at] - model[part * count + i:part * count + i + 1]
    part = half_image(back, row_index % 2, row_tab, col_tab, right, both)
    out[...] = part(slice(0, out.shape[0]))


def image_kernel(scale, back, first, row_tab, col_tab, out, right, both, image, sems):
    row_index, _ = place()
    part = half_image(back, 1 - row_index % 2, row_tab, col_tab, right, both)
    chunks = sems.shape[0]
    step = image.shape[0] // chunks
    writes = []
    for n in range(chunks):
        at = slice(n * step, (n + 1) * step)
        image[at] = (first[at] + part(at)) * scale
        write = pltpu.make_async_copy(image.at[at], out.at[at], sems.at[n])
        write.start()
        writes.append(write)
    for write in writes:
        write.wait()


def call(kernel, out_shape, name, spaces, scratch=(), cost=0, outs=None, room=24):
    kinds = {"s": pltpu.SMEM, "v": pltpu.VMEM, "a": pl.ANY}
    several = isinstance(out_shape, tuple)
    outs = outs or "v" * (len(out_shape) if several else 1)
    out_specs = tuple(pl.BlockSpec(memory_space=kinds[kind]) for kind in outs)
    return pl.pallas_call(
        kernel,
        out_shape=out_shape,
        in_specs=[pl.BlockSpec(memory_space=kinds[kind]) for kind in spaces],
        out_specs=out_specs if several else out_specs[0],
        scratch_shapes=list(scratch),
        compiler_params=pltpu.CompilerParams(vmem_limit_bytes=room * 2**20),
        cost_estimate=pl.CostEstimate(flops=cost, bytes_accessed=2**20, transcendentals=0),
        name=name,
    )


def grid_tables():
    counter = np.arange(SG)
    angles = (counter[:, None] * counter[None, :] % SG).astype(np.float64) * (2.0 * math.pi / SG)
    return np.cos(angles).astype(ml_dtypes.bfloat16), np.sin(angles).astype(ml_dtypes.bfloat16)


def exchange(blocks, axes, groups):
    return lax.all_to_all(blocks, axes, 0, 0, tiled=True, axis_index_groups=groups)


def shape(*dims, dtype=jnp.bfloat16):
    return jax.ShapeDtypeStruct(dims, dtype)


def shards(facet, row_offsets, col_offsets, vis_subgrid, vis_u, vis_v, observed):
    f32, bf16 = jnp.float32, jnp.bfloat16
    rows_count, cols_count = lax.axis_size("frow"), lax.axis_size("fcol")
    side = facet.shape[0]
    n_vis = vis_u.shape[0]
    chips = rows_count // 2
    each = SG // cols_count
    x_groups = [[2 * chip + core for chip in range(chips)] for core in range(2)]
    swap = [(index, index ^ 1) for index in range(rows_count)]
    scale_in = 1.0 / (side * math.sqrt(rows_count * cols_count))
    scale_out = 1.0 / (SG * math.sqrt(NR * NC))
    line = (1, n_vis)

    half_shape = shape(side + 16, 4 * HALF)
    own, send = call(
        functools.partial(columns_kernel, cols_count), (half_shape, half_shape), "columns", "saaaaa",
        scratch=[
            pltpu.VMEM((side, 8 * HALF), bf16), pltpu.VMEM((side, side), bf16), pltpu.VMEM((3,) + line, jnp.int32),
            pltpu.VMEM((2, n_vis), f32), pltpu.SemaphoreType.DMA((5,)),
        ],
        cost=10**9, room=60,
    )(col_offsets, facet, vis_subgrid.reshape(line), vis_u.reshape(line), vis_v.reshape(line), observed)
    other = lax.ppermute(send, "frow", swap)
    row_tab = call(
        functools.partial(row_tables_kernel, rows_count, side), shape(4, SG, 2 * side), "row_tables", "s", cost=10**9
    )(row_offsets)
    vis_rows_count = 8 * 2 * n_vis // LANES
    parts = call(
        functools.partial(contributions_kernel, scale_in), shape(NR * NC, 2 * SG + vis_rows_count, HALF),
        "contributions", "vvv", scratch=[pltpu.VMEM((2 * side, 4 * HALF), bf16)], cost=2 * 10**9,
    )(own, other, row_tab)
    parts = exchange(parts, "frow", x_groups)

    pieces = call(
        gridding_kernel, shape(cols_count, 5 * each, HALF), "gridding", "v",
        scratch=[pltpu.VMEM((5, SG, HALF), f32)], cost=10**9,
    )(parts)
    pieces = exchange(pieces, "fcol", None)
    pieces = call(pieces_sum_kernel, shape(cols_count, 5 * each, HALF), "pieces_sum", "v", cost=10**6)(pieces)
    pieces = exchange(pieces, "fcol", None)
    pieces_other = lax.ppermute(pieces, "frow", swap)

    back_row, back_col = call(
        functools.partial(back_tables_kernel, rows_count, cols_count, side),
        (shape(side, 4 * SG), shape(4 * SG, side)), "back_tables", "ss", cost=10**9,
    )(row_offsets, col_offsets)
    kcos, ksin = grid_tables()
    block = [np.concatenate(pair, 1) for pair in ((kcos, ksin), (-ksin, kcos), (kcos, -ksin), (ksin, kcos))]
    forward_block = np.concatenate([block[0], block[1]], 0)
    inverse_block = np.concatenate([block[2], block[3]], 0)
    back = call(
        grids_kernel, shape(chips, 2 * SG + 16, HALF), "grids", "vvvvvvva",
        scratch=[
            pltpu.VMEM((5, SG, SG), f32), pltpu.VMEM((SG, 2 * SG), bf16), pltpu.VMEM((2 * SG, SG), bf16),
            pltpu.VMEM((SG, 2 * SG), bf16),
        ],
        cost=10**9,
    )(pieces, pieces_other, parts, inverse_block, forward_block, forward_block, inverse_block, back_col)
    back = exchange(back, "frow", x_groups)
    back_other = lax.ppermute(back, "frow", swap)

    work = [pltpu.VMEM((4 * SG, 2 * SG), bf16), pltpu.VMEM((side, 2 * SG), bf16)]
    first, residual = call(
        own_image_kernel, (shape(side, side, dtype=f32), shape(2, n_vis, dtype=f32)), "own_image", "vvvv",
        scratch=work, cost=10**9,
    )(back, back_row, back_col, observed)
    image = call(
        functools.partial(image_kernel, scale_out), shape(side, side, dtype=f32), "image", "vvvv", outs="a",
        scratch=work + [pltpu.VMEM((side, side), f32), pltpu.SemaphoreType.DMA((4,))], cost=10**9,
    )(back_other, first, back_row, back_col)
    return (image, residual)


def solution(mesh):
    in_specs = (
        P("frow", "fcol"),
        P(),
        P(),
        P(("frow", "fcol")),
        P(("frow", "fcol")),
        P(("frow", "fcol")),
        P(None, ("frow", "fcol")),
    )
    out_specs = (P("frow", "fcol"), P(None, ("frow", "fcol")))
    return jax.shard_map(shards, mesh=mesh, in_specs=in_specs, out_specs=out_specs, check_vma=False)
```

```python
import functools
import math

import jax
import jax.numpy as jnp
import ml_dtypes
import numpy as np
from jax import lax
from jax.experimental import pallas as pl
from jax.experimental.pallas import tpu as pltpu
from jax.sharding import PartitionSpec as P

SKY = 65536
SG = 256
NR = 2
NC = 2
HALF = SG // 2
LANES = 128


def wave(count):
    count = count & (SKY - 1)
    turned = count + SKY // 8
    near = (turned & (SKY // 4 - 1)) - SKY // 8
    quarter = lax.shift_right_logical(turned, 14) & 3
    t = near.astype(jnp.float32) * (2.0 * math.pi / SKY)
    q = t * t
    sin = t * (1.0 + q * (-1.0 / 6 + q * (1.0 / 120 + q * (-1.0 / 5040 + q * (1.0 / 362880)))))
    cos = 1.0 + q * (-0.5 + q * (1.0 / 24 + q * (-1.0 / 720 + q * (1.0 / 40320))))
    odd = (quarter & 1) == 1
    one, two = jnp.where(odd, sin, cos), jnp.where(odd, cos, sin)
    return (
        jnp.where((quarter == 1) | (quarter == 2), -one, one),
        jnp.where(quarter >= 2, -two, two),
    )


def lanes(n):
    return lax.broadcasted_iota(jnp.int32, (1, n), 1)


def sublanes(n):
    return lax.broadcasted_iota(jnp.int32, (n, 1), 0)


def spread(coarse, fine, store):
    for k in range(coarse[0].shape[0]):
        c, s = coarse[0][k:k + 1], coarse[1][k:k + 1]
        store(k * 16, c * fine[0] - s * fine[1], s * fine[0] + c * fine[1])


def place():
    return lax.axis_index("frow"), lax.axis_index("fcol")


def columns_kernel(cols_count, offsets, facet, subgrid, u, v, observed, own, send, col_tab, image, indices, seen, sems):
    f32, bf16 = jnp.float32, jnp.bfloat16
    side = facet.shape[0]
    copies = [
        pltpu.make_async_copy(facet, image, sems.at[0]),
        pltpu.make_async_copy(subgrid, indices.at[0], sems.at[1]),
        pltpu.make_async_copy(u, indices.at[1], sems.at[2]),
        pltpu.make_async_copy(v, indices.at[2], sems.at[3]),
        pltpu.make_async_copy(observed, seen, sems.at[4]),
    ]
    for copy in copies:
        copy.start()
    row_index, col_index = place()
    core = row_index % 2
    unit = sublanes(16)
    col_step = SKY // (cols_count * side)
    col_base = col_index * (SKY // cols_count)
    for c in range(NC):
        freq = offsets[c] + lanes(SG)
        coarse = wave((col_base + 16 * col_step * sublanes(side // 16)) * freq)
        fine = wave((col_step * unit) * freq)

        def store(at, cos, sin, c=c):
            for h in range(2):
                half = slice(h * HALF, (h + 1) * HALF)
                left = (2 * h + c) * SG
                col_tab[at:at + 16, left:left + HALF] = cos[:, half].astype(bf16)
                col_tab[at:at + 16, left + HALF:left + SG] = sin[:, half].astype(bf16)

        spread(coarse, fine, store)
    for copy in copies:
        copy.wait()
    vis = jnp.concatenate([indices[n].astype(f32) for n in range(3)] + [seen[...], jnp.zeros((3, side), f32)], 0)
    vis = jnp.concatenate([vis[:, :side // 2], vis[:, side // 2:]], 0).astype(bf16)
    for out, half in ((send, 1 - core), (own, core)):
        tab = col_tab[:, pl.ds(pl.multiple_of(half * 2 * SG, 2 * SG), 2 * SG)]
        out[:side] = jnp.dot(image[...], tab, preferred_element_type=f32).astype(bf16)
        out[side:, :side // 2] = vis
        out[side:, side // 2:] = vis


def row_tables_kernel(rows_count, side, offsets, row_tab):
    bf16 = jnp.bfloat16
    row_index, _ = place()
    unit = sublanes(16)
    row_step = SKY // (rows_count * side)
    for f in range(2):
        pos = (row_index ^ f) * (SKY // rows_count) + row_step * lanes(side)
        fine = wave(unit * pos)
        for r in range(NR):
            coarse = wave((offsets[r] + 16 * unit) * pos)

            def store(at, cos, sin, r=r, f=f):
                row_tab[2 * r, at:at + 16, f * side:(f + 1) * side] = cos.astype(bf16)
                row_tab[2 * r + 1, at:at + 16, f * side:(f + 1) * side] = sin.astype(bf16)

            spread(coarse, fine, store)


def contributions_kernel(scale, own, other, row_tab, *refs):
    f32, bf16 = jnp.float32, jnp.bfloat16
    outs, right = refs[:-1], refs[-1]
    chip = place()[0] // 2
    side = row_tab.shape[2] // 2
    vis = []
    for f, half in enumerate((own, other)):
        right[f * side:(f + 1) * side] = half[:side]
        some = half[side:]
        vis += [some[:, k * LANES:(k + 1) * LANES] for k in range(side // 2 // LANES)]
    for n, out in enumerate(outs):
        for k, some in enumerate(vis):
            at = 2 * SG + 16 * k
            out[at:at + 16] = some
        r, c = split_number(chip + n)
        some = right[:, pl.ds(pl.multiple_of(c * SG, SG), SG)]
        with_cos = jnp.dot(row_tab[2 * r], some, preferred_element_type=f32)
        with_sin = jnp.dot(row_tab[2 * r + 1], some, preferred_element_type=f32)
        out[:SG] = ((with_cos[:, :HALF] - with_sin[:, HALF:]) * scale).astype(bf16)
        out[SG:2 * SG] = (-(with_cos[:, HALF:] + with_sin[:, :HALF]) * scale).astype(bf16)


def split_number(number):
    number = lax.rem(number, NR * NC)
    return number // NC, lax.rem(number, NC)


def vis_rows(block):
    count = block.shape[0] // 16
    return jnp.concatenate(
        [block[16 * k + 8 * part:16 * k + 8 * part + 8] for part in range(2) for k in range(count)], 1
    )


def gridding_kernel(*refs):
    f32, bf16 = jnp.float32, jnp.bfloat16
    parts, (pieces, planes) = refs[:-2], refs[-2:]
    row_index, _ = place()
    chip = (row_index // 2).astype(f32)
    v_at = (sublanes(HALF) + (row_index % 2) * HALF).astype(f32)
    counter = sublanes(SG).astype(f32)
    count = len(parts)
    total = jnp.zeros((SG, 3 * HALF), f32)
    for k in range(count):
        one = vis_rows(parts[k][2 * SG:].astype(f32))
        u_here = jnp.where(one[0:1] == chip, one[1:2], -1.0)
        hot = jnp.where(u_here == counter, 1.0, 0.0).astype(bf16)
        pick = one[2:3] == v_at
        right = jnp.concatenate(
            [jnp.where(pick, one[3:4], 0.0), jnp.where(pick, one[4:5], 0.0), jnp.where(pick, 1.0, 0.0)], 0
        ).astype(bf16)
        total = total + lax.dot_general(hot, right, (((1,), (1,)), ((), ())), preferred_element_type=f32)
    for p in range(2):
        some = parts[0][p * SG:(p + 1) * SG].astype(f32)
        for k in range(1, count):
            some = some + parts[k][p * SG:(p + 1) * SG].astype(f32)
        planes[p] = some
    for p in range(3):
        planes[2 + p] = total[:, p * HALF:(p + 1) * HALF]
    each = SG // pieces.shape[0]
    for j in range(pieces.shape[0]):
        rows = [planes[p, j * each:(j + 1) * each] for p in range(5)]
        pieces[j] = jnp.concatenate(rows, 0).astype(bf16)


def pieces_sum_kernel(pieces, out):
    f32, bf16 = jnp.float32, jnp.bfloat16
    total = pieces[0].astype(f32)
    for j in range(1, pieces.shape[0]):
        total = total + pieces[j].astype(f32)
    total = total.astype(bf16)
    for j in range(out.shape[0]):
        out[j] = total


def grids_kernel(chips, own, other, *refs):
    f32, bf16 = jnp.float32, jnp.bfloat16
    parts, (grid_left, forward, inverse_left, inverse, _) = refs[:chips], refs[chips:chips + 5]
    outs, rest, (planes, cat, tall, hat) = refs[chips + 5:-5], refs[-5], refs[-4:]
    row_index, _ = place()
    core = row_index % 2
    chip = (row_index // 2).astype(f32)
    count = own.shape[0]
    each = SG // count
    for pieces, half in ((own, core), (other, 1 - core)):
        at = pl.ds(pl.multiple_of(half * HALF, HALF), HALF)
        for j in range(count):
            some = pieces[j].astype(f32)
            for p in range(5):
                planes[p, j * each:(j + 1) * each, at] = some[p * each:(p + 1) * each]
    cat[:, :SG] = planes[0].astype(bf16)
    cat[:, SG:] = planes[1].astype(bf16)
    wide = jnp.dot(cat[...], forward[...], preferred_element_type=f32).astype(bf16)
    tall[:SG] = wide[:, :SG]
    tall[SG:] = wide[:, SG:]
    model = jnp.dot(grid_left[...], tall[...], preferred_element_type=f32) * (1.0 / SG)
    hat_real, hat_imag = model[:SG], model[SG:]
    cat[:, :SG] = (planes[2] - planes[4] * hat_real).astype(bf16)
    cat[:, SG:] = (planes[3] - planes[4] * hat_imag).astype(bf16)
    hat[:, :SG] = hat_real.astype(bf16)
    hat[:, SG:] = hat_imag.astype(bf16)
    wide = jnp.dot(cat[...], inverse[...], preferred_element_type=f32)
    for k in range(2):
        tall[k * SG:(k + 1) * SG] = wide[:, k * SG:(k + 1) * SG].astype(bf16)
    back = jnp.dot(inverse_left[...], tall[...], preferred_element_type=f32) * (1.0 / SG)
    rest[...] = jnp.where(core == 0, back[:, HALF:], back[:, :HALF]).astype(bf16)
    back = jnp.where(core == 0, back[:, :HALF], back[:, HALF:]).astype(bf16)
    counter = sublanes(SG).astype(f32)
    vis_each = (parts[0].shape[0] - 2 * SG) // 2
    for k, out in enumerate(outs):
        out[:2 * SG] = back
        ask = vis_rows(parts[-k % chips][2 * SG:2 * SG + vis_each].astype(f32))
        u_here = jnp.where(ask[0:1] == chip, ask[1:2], -1.0)
        hot = jnp.where(u_here == counter, 1.0, 0.0).astype(bf16)
        pick = ask[2:3] == counter
        line = lax.dot_general(hat[...], hot, (((0,), (0,)), ((), ())), preferred_element_type=f32)
        rows = []
        for part in range(2):
            value = jnp.sum(jnp.where(pick, line[part * SG:(part + 1) * SG], 0.0), axis=0, keepdims=True)
            rows += [value[:, i * LANES:(i + 1) * LANES] for i in range(value.shape[1] // LANES)]
        rows.append(jnp.zeros((16 - len(rows), LANES), f32))
        out[2 * SG:] = jnp.concatenate(rows, 0).astype(bf16)


def back_tables_kernel(rows_count, cols_count, side, offsets_row, offsets_col, row_tab, col_tab):
    bf16 = jnp.bfloat16
    row_index, col_index = place()
    unit = sublanes(16)
    row_step = SKY // (rows_count * side)
    row_base = row_index * (SKY // rows_count)
    for r in range(NR):
        freq = offsets_row[r] + lanes(SG)
        coarse = wave((row_base + 16 * row_step * sublanes(side // 16)) * freq)
        fine = wave((row_step * unit) * freq)

        def store(at, cos, sin, r=r):
            row_tab[at:at + 16, 2 * r * SG:(2 * r + 1) * SG] = cos.astype(bf16)
            row_tab[at:at + 16, (2 * r + 1) * SG:(2 * r + 2) * SG] = sin.astype(bf16)

        spread(coarse, fine, store)
    col_step = SKY // (cols_count * side)
    pos = col_index * (SKY // cols_count) + col_step * lanes(side)
    fine = wave(unit * pos)
    for c in range(NC):
        coarse = wave((offsets_col[c] + 16 * unit) * pos)

        def store(at, cos, sin, c=c):
            left = (at // HALF * 2 * NC + 2 * c) * HALF + at % HALF
            col_tab[left:left + 16] = cos.astype(bf16)
            col_tab[left + HALF:left + HALF + 16] = (-sin).astype(bf16)

        spread(coarse, fine, store)


def half_image(blocks, half, row_tab, col_tab, right, both):
    f32, bf16 = jnp.float32, jnp.bfloat16
    chip = place()[0] // 2
    for k, block in enumerate(blocks):
        r, c = split_number(chip + len(blocks) - k)
        real, imag = block[:SG], block[SG:2 * SG]
        top = [pl.ds(pl.multiple_of((2 * r + n) * SG, SG), SG) for n in range(2)]
        at = [pl.ds(pl.multiple_of((2 * c + n) * HALF, HALF), HALF) for n in range(2)]
        right[top[0], at[0]] = real
        right[top[0], at[1]] = imag
        right[top[1], at[0]] = -imag
        right[top[1], at[1]] = real
    both[...] = jnp.dot(row_tab[...], right[...], preferred_element_type=f32).astype(bf16)
    depth = 2 * NC * HALF
    rows = pl.ds(pl.multiple_of(half * depth, depth), depth)
    return lambda at: jnp.dot(both[at], col_tab[rows], preferred_element_type=f32)


def own_image_kernel(*refs):
    blocks, (row_tab, col_tab, observed, out, residual, right, both) = refs[:-7], refs[-7:]
    f32 = jnp.float32
    row_index, _ = place()
    model = jnp.zeros((16, LANES), f32)
    for block in blocks:
        model = model + block[2 * SG:].astype(f32)
    count = observed.shape[1] // LANES
    for part in range(2):
        for i in range(count):
            at = slice(i * LANES, (i + 1) * LANES)
            residual[part:part + 1, at] = observed[part:part + 1, at] - model[part * count + i:part * count + i + 1]
    part = half_image(blocks, row_index % 2, row_tab, col_tab, right, both)
    out[...] = part(slice(0, out.shape[0]))


def image_kernel(scale, *refs):
    blocks, (first, row_tab, col_tab, out, right, both, image, sems) = refs[:-8], refs[-8:]
    row_index, _ = place()
    part = half_image(blocks, 1 - row_index % 2, row_tab, col_tab, right, both)
    chunks = sems.shape[0]
    step = image.shape[0] // chunks
    writes = []
    for n in range(chunks):
        at = slice(n * step, (n + 1) * step)
        image[at] = (first[at] + part(at)) * scale
        write = pltpu.make_async_copy(image.at[at], out.at[at], sems.at[n])
        write.start()
        writes.append(write)
    for write in writes:
        write.wait()


def call(kernel, out_shape, name, spaces, scratch=(), cost=0, outs=None, room=24):
    kinds = {"s": pltpu.SMEM, "v": pltpu.VMEM, "a": pl.ANY}
    several = isinstance(out_shape, tuple)
    outs = outs or "v" * (len(out_shape) if several else 1)
    out_specs = tuple(pl.BlockSpec(memory_space=kinds[kind]) for kind in outs)
    return pl.pallas_call(
        kernel,
        out_shape=out_shape,
        in_specs=[pl.BlockSpec(memory_space=kinds[kind]) for kind in spaces],
        out_specs=out_specs if several else out_specs[0],
        scratch_shapes=list(scratch),
        compiler_params=pltpu.CompilerParams(vmem_limit_bytes=room * 2**20),
        cost_estimate=pl.CostEstimate(flops=cost, bytes_accessed=2**20, transcendentals=0),
        name=name,
    )


def grid_tables():
    counter = np.arange(SG)
    angles = (counter[:, None] * counter[None, :] % SG).astype(np.float64) * (2.0 * math.pi / SG)
    return np.cos(angles).astype(ml_dtypes.bfloat16), np.sin(angles).astype(ml_dtypes.bfloat16)


def exchange(blocks, axes, groups):
    return lax.all_to_all(blocks, axes, 0, 0, tiled=True, axis_index_groups=groups)


def shape(*dims, dtype=jnp.bfloat16):
    return jax.ShapeDtypeStruct(dims, dtype)


def shards(facet, row_offsets, col_offsets, vis_subgrid, vis_u, vis_v, observed):
    f32, bf16 = jnp.float32, jnp.bfloat16
    rows_count, cols_count = lax.axis_size("frow"), lax.axis_size("fcol")
    side = facet.shape[0]
    n_vis = vis_u.shape[0]
    chips = rows_count // 2
    each = SG // cols_count
    swap = [(index, index ^ 1) for index in range(rows_count)]
    turns = [[(index, (index + 2 * k) % rows_count) for index in range(rows_count)] for k in range(chips)]
    scale_in = 1.0 / (side * math.sqrt(rows_count * cols_count))
    scale_out = 1.0 / (SG * math.sqrt(NR * NC))
    line = (1, n_vis)

    half_shape = shape(side + 16, 4 * HALF)
    own, send = call(
        functools.partial(columns_kernel, cols_count), (half_shape, half_shape), "columns", "saaaaa",
        scratch=[
            pltpu.VMEM((side, 8 * HALF), bf16), pltpu.VMEM((side, side), bf16), pltpu.VMEM((3,) + line, jnp.int32),
            pltpu.VMEM((2, n_vis), f32), pltpu.SemaphoreType.DMA((5,)),
        ],
        cost=10**9, room=60,
    )(col_offsets, facet, vis_subgrid.reshape(line), vis_u.reshape(line), vis_v.reshape(line), observed)
    other = lax.ppermute(send, "frow", swap)
    row_tab = call(
        functools.partial(row_tables_kernel, rows_count, side), shape(4, SG, 2 * side), "row_tables", "s", cost=10**9
    )(row_offsets)
    vis_rows_count = 8 * 2 * n_vis // LANES
    parts = call(
        functools.partial(contributions_kernel, scale_in), (shape(2 * SG + vis_rows_count, HALF),) * chips,
        "contributions", "vvv", scratch=[pltpu.VMEM((2 * side, 4 * HALF), bf16)], cost=2 * 10**9,
    )(own, other, row_tab)
    parts = [parts[0]] + [lax.ppermute(parts[k], "frow", turns[k]) for k in range(1, chips)]

    pieces = call(
        gridding_kernel, shape(cols_count, 5 * each, HALF), "gridding", "v" * chips,
        scratch=[pltpu.VMEM((5, SG, HALF), f32)], cost=10**9,
    )(*parts)
    pieces = exchange(pieces, "fcol", None)
    pieces = call(pieces_sum_kernel, shape(cols_count, 5 * each, HALF), "pieces_sum", "v", cost=10**6)(pieces)
    pieces = exchange(pieces, "fcol", None)
    pieces_other = lax.ppermute(pieces, "frow", swap)

    back_row, back_col = call(
        functools.partial(back_tables_kernel, rows_count, cols_count, side),
        (shape(side, 4 * SG), shape(4 * SG, side)), "back_tables", "ss", cost=10**9,
    )(row_offsets, col_offsets)
    kcos, ksin = grid_tables()
    block = [np.concatenate(pair, 1) for pair in ((kcos, ksin), (-ksin, kcos), (kcos, -ksin), (ksin, kcos))]
    forward_block = np.concatenate([block[0], block[1]], 0)
    inverse_block = np.concatenate([block[2], block[3]], 0)
    *back, rest = call(
        functools.partial(grids_kernel, chips), (shape(2 * SG + 16, HALF),) * chips + (shape(2 * SG, HALF),), "grids",
        "v" * (6 + chips) + "a",
        scratch=[
            pltpu.VMEM((5, SG, SG), f32), pltpu.VMEM((SG, 2 * SG), bf16), pltpu.VMEM((2 * SG, SG), bf16),
            pltpu.VMEM((SG, 2 * SG), bf16),
        ],
        cost=10**9,
    )(pieces, pieces_other, *parts, inverse_block, forward_block, forward_block, inverse_block, back_col)
    back = [back[0]] + [lax.ppermute(back[k], "frow", turns[k]) for k in range(1, chips)]
    back_other = [rest] + [lax.ppermute(back[k], "frow", swap) for k in range(1, chips)]

    work = [pltpu.VMEM((4 * SG, 2 * SG), bf16), pltpu.VMEM((side, 2 * SG), bf16)]
    first, residual = call(
        own_image_kernel, (shape(side, side, dtype=f32), shape(2, n_vis, dtype=f32)), "own_image", "vvv" + "v" * chips,
        scratch=work, cost=10**9,
    )(*back, back_row, back_col, observed)
    image = call(
        functools.partial(image_kernel, scale_out), shape(side, side, dtype=f32), "image", "vvv" + "v" * chips, outs="a",
        scratch=work + [pltpu.VMEM((side, side), f32), pltpu.SemaphoreType.DMA((4,))], cost=10**9,
    )(*back_other, first, back_row, back_col)
    return (image, residual)


def solution(mesh):
    in_specs = (
        P("frow", "fcol"),
        P(),
        P(),
        P(("frow", "fcol")),
        P(("frow", "fcol")),
        P(("frow", "fcol")),
        P(None, ("frow", "fcol")),
    )
    out_specs = (P("frow", "fcol"), P(None, ("frow", "fcol")))
    return jax.shard_map(shards, mesh=mesh, in_specs=in_specs, out_specs=out_specs, check_vma=False)
```

```python
import functools
import math

import jax
import jax.numpy as jnp
import ml_dtypes
import numpy as np
from jax import lax
from jax.experimental import pallas as pl
from jax.experimental.pallas import tpu as pltpu
from jax.sharding import PartitionSpec as P

SKY = 65536
SG = 256
NR = 2
NC = 2
HALF = SG // 2
LANES = 128


def wave(count):
    count = count & (SKY - 1)
    turned = count + SKY // 8
    near = (turned & (SKY // 4 - 1)) - SKY // 8
    quarter = lax.shift_right_logical(turned, 14) & 3
    t = near.astype(jnp.float32) * (2.0 * math.pi / SKY)
    q = t * t
    sin = t * (1.0 + q * (-1.0 / 6 + q * (1.0 / 120 + q * (-1.0 / 5040 + q * (1.0 / 362880)))))
    cos = 1.0 + q * (-0.5 + q * (1.0 / 24 + q * (-1.0 / 720 + q * (1.0 / 40320))))
    odd = (quarter & 1) == 1
    one, two = jnp.where(odd, sin, cos), jnp.where(odd, cos, sin)
    return (
        jnp.where((quarter == 1) | (quarter == 2), -one, one),
        jnp.where(quarter >= 2, -two, two),
    )


def lanes(n):
    return lax.broadcasted_iota(jnp.int32, (1, n), 1)


def sublanes(n):
    return lax.broadcasted_iota(jnp.int32, (n, 1), 0)


def spread(coarse, fine, store):
    for k in range(coarse[0].shape[0]):
        c, s = coarse[0][k:k + 1], coarse[1][k:k + 1]
        store(k * 16, c * fine[0] - s * fine[1], s * fine[0] + c * fine[1])


def place():
    return lax.axis_index("frow"), lax.axis_index("fcol")


def half_columns(cols_count, offsets, half, side, col_tab):
    bf16 = jnp.bfloat16
    col_index = place()[1]
    unit = sublanes(16)
    col_step = SKY // (cols_count * side)
    col_base = col_index * (SKY // cols_count)
    freq = [offsets[c] + half * HALF + lanes(HALF) for c in range(NC)]
    freq = jnp.concatenate(freq, 1)
    coarse = wave((col_base + 16 * col_step * sublanes(side // 16)) * freq)
    fine = wave((col_step * unit) * freq)

    def store(at, cos, sin):
        for c in range(NC):
            some = slice(c * HALF, (c + 1) * HALF)
            col_tab[at:at + 16, 2 * c * HALF:(2 * c + 1) * HALF] = cos[:, some].astype(bf16)
            col_tab[at:at + 16, (2 * c + 1) * HALF:(2 * c + 2) * HALF] = sin[:, some].astype(bf16)

    spread(coarse, fine, store)


def send_columns_kernel(cols_count, offsets, facet, subgrid, u, v, observed, send, vis, col_tab, image, indices, seen, sems):
    f32, bf16 = jnp.float32, jnp.bfloat16
    side = facet.shape[0]
    copies = [
        pltpu.make_async_copy(facet, image, sems.at[0]),
        pltpu.make_async_copy(subgrid, indices.at[0], sems.at[1]),
        pltpu.make_async_copy(u, indices.at[1], sems.at[2]),
        pltpu.make_async_copy(v, indices.at[2], sems.at[3]),
        pltpu.make_async_copy(observed, seen, sems.at[4]),
    ]
    for copy in copies:
        copy.start()
    half_columns(cols_count, offsets, 1 - place()[0] % 2, side, col_tab)
    for copy in copies:
        copy.wait()
    some = jnp.concatenate([indices[n].astype(f32) for n in range(3)] + [seen[...], jnp.zeros((3, side), f32)], 0)
    some = jnp.concatenate([some[:, :side // 2], some[:, side // 2:]], 0).astype(bf16)
    vis[...] = some
    send[side:, :side // 2] = some
    send[side:, side // 2:] = some
    send[:side] = jnp.dot(image[...], col_tab[...], preferred_element_type=f32).astype(bf16)


def own_columns_kernel(cols_count, offsets, facet, own, col_tab):
    half_columns(cols_count, offsets, place()[0] % 2, facet.shape[0], col_tab)
    own[...] = jnp.dot(facet[...], col_tab[...], preferred_element_type=jnp.float32).astype(jnp.bfloat16)


def row_tables_kernel(rows_count, side, offsets, row_tab):
    bf16 = jnp.bfloat16
    row_index, _ = place()
    unit = sublanes(16)
    row_step = SKY // (rows_count * side)
    for f in range(2):
        pos = (row_index ^ f) * (SKY // rows_count) + row_step * lanes(side)
        fine = wave(unit * pos)
        for r in range(NR):
            coarse = wave((offsets[r] + 16 * unit) * pos)

            def store(at, cos, sin, r=r, f=f):
                row_tab[2 * r, at:at + 16, f * side:(f + 1) * side] = cos.astype(bf16)
                row_tab[2 * r + 1, at:at + 16, f * side:(f + 1) * side] = sin.astype(bf16)

            spread(coarse, fine, store)


def contributions_kernel(scale, own, own_vis, other, row_tab, *refs):
    f32, bf16 = jnp.float32, jnp.bfloat16
    outs, right = refs[:-1], refs[-1]
    chip = place()[0] // 2
    side = row_tab.shape[2] // 2
    vis = []
    right[:side] = own[...]
    right[side:] = other[:side]
    for some in (own_vis[...], other[side:]):
        vis += [some[:, k * LANES:(k + 1) * LANES] for k in range(side // 2 // LANES)]
    for n, out in enumerate(outs):
        for k, some in enumerate(vis):
            at = 2 * SG + 16 * k
            out[at:at + 16] = some
        r, c = split_number(chip + n)
        some = right[:, pl.ds(pl.multiple_of(c * SG, SG), SG)]
        with_cos = jnp.dot(row_tab[2 * r], some, preferred_element_type=f32)
        with_sin = jnp.dot(row_tab[2 * r + 1], some, preferred_element_type=f32)
        out[:SG] = ((with_cos[:, :HALF] - with_sin[:, HALF:]) * scale).astype(bf16)
        out[SG:2 * SG] = (-(with_cos[:, HALF:] + with_sin[:, :HALF]) * scale).astype(bf16)


def split_number(number):
    number = lax.rem(number, NR * NC)
    return number // NC, lax.rem(number, NC)


def vis_rows(block):
    count = block.shape[0] // 16
    return jnp.concatenate(
        [block[16 * k + 8 * part:16 * k + 8 * part + 8] for part in range(2) for k in range(count)], 1
    )


def gridding_kernel(*refs):
    f32, bf16 = jnp.float32, jnp.bfloat16
    parts, (pieces, planes) = refs[:-2], refs[-2:]
    row_index, _ = place()
    chip = (row_index // 2).astype(f32)
    v_at = (sublanes(HALF) + (row_index % 2) * HALF).astype(f32)
    counter = sublanes(SG).astype(f32)
    count = len(parts)
    total = jnp.zeros((SG, 3 * HALF), f32)
    for k in range(count):
        one = vis_rows(parts[k][2 * SG:].astype(f32))
        u_here = jnp.where(one[0:1] == chip, one[1:2], -1.0)
        hot = jnp.where(u_here == counter, 1.0, 0.0).astype(bf16)
        pick = one[2:3] == v_at
        right = jnp.concatenate(
            [jnp.where(pick, one[3:4], 0.0), jnp.where(pick, one[4:5], 0.0), jnp.where(pick, 1.0, 0.0)], 0
        ).astype(bf16)
        total = total + lax.dot_general(hot, right, (((1,), (1,)), ((), ())), preferred_element_type=f32)
    for p in range(2):
        some = parts[0][p * SG:(p + 1) * SG].astype(f32)
        for k in range(1, count):
            some = some + parts[k][p * SG:(p + 1) * SG].astype(f32)
        planes[p] = some
    for p in range(3):
        planes[2 + p] = total[:, p * HALF:(p + 1) * HALF]
    each = SG // pieces.shape[0]
    for j in range(pieces.shape[0]):
        rows = [planes[p, j * each:(j + 1) * each] for p in range(5)]
        pieces[j] = jnp.concatenate(rows, 0).astype(bf16)


def pieces_sum_kernel(pieces, out):
    f32, bf16 = jnp.float32, jnp.bfloat16
    total = pieces[0].astype(f32)
    for j in range(1, pieces.shape[0]):
        total = total + pieces[j].astype(f32)
    total = total.astype(bf16)
    for j in range(out.shape[0]):
        out[j] = total


def grids_kernel(chips, own, other, *refs):
    f32, bf16 = jnp.float32, jnp.bfloat16
    parts, (grid_left, forward, inverse_left, inverse, _) = refs[:chips], refs[chips:chips + 5]
    outs, rest, (planes, cat, tall, hat) = refs[chips + 5:-5], refs[-5], refs[-4:]
    row_index, _ = place()
    core = row_index % 2
    chip = (row_index // 2).astype(f32)
    count = own.shape[0]
    each = SG // count
    for pieces, half in ((own, core), (other, 1 - core)):
        at = pl.ds(pl.multiple_of(half * HALF, HALF), HALF)
        for j in range(count):
            some = pieces[j].astype(f32)
            for p in range(5):
                planes[p, j * each:(j + 1) * each, at] = some[p * each:(p + 1) * each]
    cat[:, :SG] = planes[0].astype(bf16)
    cat[:, SG:] = planes[1].astype(bf16)
    wide = jnp.dot(cat[...], forward[...], preferred_element_type=f32).astype(bf16)
    tall[:SG] = wide[:, :SG]
    tall[SG:] = wide[:, SG:]
    model = jnp.dot(grid_left[...], tall[...], preferred_element_type=f32) * (1.0 / SG)
    hat_real, hat_imag = model[:SG], model[SG:]
    cat[:, :SG] = (planes[2] - planes[4] * hat_real).astype(bf16)
    cat[:, SG:] = (planes[3] - planes[4] * hat_imag).astype(bf16)
    hat[:, :SG] = hat_real.astype(bf16)
    hat[:, SG:] = hat_imag.astype(bf16)
    wide = jnp.dot(cat[...], inverse[...], preferred_element_type=f32)
    for k in range(2):
        tall[k * SG:(k + 1) * SG] = wide[:, k * SG:(k + 1) * SG].astype(bf16)
    back = jnp.dot(inverse_left[...], tall[...], preferred_element_type=f32) * (1.0 / SG)
    rest[...] = jnp.where(core == 0, back[:, HALF:], back[:, :HALF]).astype(bf16)
    back = jnp.where(core == 0, back[:, :HALF], back[:, HALF:]).astype(bf16)
    counter = sublanes(SG).astype(f32)
    vis_each = (parts[0].shape[0] - 2 * SG) // 2
    for k, out in enumerate(outs):
        out[:2 * SG] = back
        ask = vis_rows(parts[-k % chips][2 * SG:2 * SG + vis_each].astype(f32))
        u_here = jnp.where(ask[0:1] == chip, ask[1:2], -1.0)
        hot = jnp.where(u_here == counter, 1.0, 0.0).astype(bf16)
        pick = ask[2:3] == counter
        line = lax.dot_general(hat[...], hot, (((0,), (0,)), ((), ())), preferred_element_type=f32)
        rows = []
        for part in range(2):
            value = jnp.sum(jnp.where(pick, line[part * SG:(part + 1) * SG], 0.0), axis=0, keepdims=True)
            rows += [value[:, i * LANES:(i + 1) * LANES] for i in range(value.shape[1] // LANES)]
        rows.append(jnp.zeros((16 - len(rows), LANES), f32))
        out[2 * SG:] = jnp.concatenate(rows, 0).astype(bf16)


def back_tables_kernel(rows_count, cols_count, side, offsets_row, offsets_col, row_tab, col_tab):
    bf16 = jnp.bfloat16
    row_index, col_index = place()
    unit = sublanes(16)
    row_step = SKY // (rows_count * side)
    row_base = row_index * (SKY // rows_count)
    for r in range(NR):
        freq = offsets_row[r] + lanes(SG)
        coarse = wave((row_base + 16 * row_step * sublanes(side // 16)) * freq)
        fine = wave((row_step * unit) * freq)

        def store(at, cos, sin, r=r):
            row_tab[at:at + 16, 2 * r * SG:(2 * r + 1) * SG] = cos.astype(bf16)
            row_tab[at:at + 16, (2 * r + 1) * SG:(2 * r + 2) * SG] = sin.astype(bf16)

        spread(coarse, fine, store)
    col_step = SKY // (cols_count * side)
    pos = col_index * (SKY // cols_count) + col_step * lanes(side)
    fine = wave(unit * pos)
    for c in range(NC):
        coarse = wave((offsets_col[c] + 16 * unit) * pos)

        def store(at, cos, sin, c=c):
            left = (at // HALF * 2 * NC + 2 * c) * HALF + at % HALF
            col_tab[left:left + 16] = cos.astype(bf16)
            col_tab[left + HALF:left + HALF + 16] = (-sin).astype(bf16)

        spread(coarse, fine, store)


def block_part(block, number, row_tab):
    r, _ = split_number(number)
    real, imag = block[:SG], block[SG:2 * SG]
    right = jnp.concatenate([jnp.concatenate([real, imag], 1), jnp.concatenate([-imag, real], 1)], 0)
    left = row_tab[:, pl.ds(pl.multiple_of(2 * r * SG, 2 * SG), 2 * SG)]
    return jnp.dot(left, right, preferred_element_type=jnp.float32)


def first_part_kernel(number, own, rest, row_tab, out):
    chip = place()[0] // 2
    for half, block in enumerate((own, rest)):
        out[:, half * SG:(half + 1) * SG] = block_part(block, chip + number, row_tab)


def image_kernel(scale, chips, *refs):
    f32, bf16 = jnp.float32, jnp.bfloat16
    blocks, others, firsts, refs = refs[:chips], refs[chips:chips + 2], refs[chips + 2:chips + 4], refs[chips + 4:]
    row_tab, col_tab, observed, out, residual, both, image, seen, sems = refs
    row_index, _ = place()
    core, chip = row_index % 2, row_index // 2
    model = jnp.zeros((16, LANES), f32)
    for block in blocks:
        model = model + block[2 * SG:].astype(f32)
    count = observed.shape[1] // LANES
    for part in range(2):
        for i in range(count):
            at = slice(i * LANES, (i + 1) * LANES)
            seen[part:part + 1, at] = observed[part:part + 1, at] - model[part * count + i:part * count + i + 1]
    writes = [pltpu.make_async_copy(seen, residual, sems.at[0])]
    writes[0].start()
    for k in range(2, chips):
        c = split_number(chip + chips - k)[1]
        for n, block in enumerate((blocks[k], others[k - 2])):
            half = core if n == 0 else 1 - core
            at = pl.ds(pl.multiple_of((half * NC + c) * SG, SG), SG)
            part = firsts[k - 2][:, n * SG:(n + 1) * SG] + block_part(block, chip + chips - k, row_tab)
            both[:, at] = part.astype(bf16)
    chunks = sems.shape[0] - 1
    step = image.shape[0] // chunks
    for n in range(chunks):
        at = slice(n * step, (n + 1) * step)
        image[at] = jnp.dot(both[at], col_tab[...], preferred_element_type=f32) * scale
        write = pltpu.make_async_copy(image.at[at], out.at[at], sems.at[1 + n])
        write.start()
        writes.append(write)
    for write in writes:
        write.wait()


def call(kernel, out_shape, name, spaces, scratch=(), cost=0, outs=None, room=24):
    kinds = {"s": pltpu.SMEM, "v": pltpu.VMEM, "a": pl.ANY}
    several = isinstance(out_shape, tuple)
    outs = outs or "v" * (len(out_shape) if several else 1)
    out_specs = tuple(pl.BlockSpec(memory_space=kinds[kind]) for kind in outs)
    return pl.pallas_call(
        kernel,
        out_shape=out_shape,
        in_specs=[pl.BlockSpec(memory_space=kinds[kind]) for kind in spaces],
        out_specs=out_specs if several else out_specs[0],
        scratch_shapes=list(scratch),
        compiler_params=pltpu.CompilerParams(vmem_limit_bytes=room * 2**20),
        cost_estimate=pl.CostEstimate(flops=cost, bytes_accessed=2**20, transcendentals=0),
        name=name,
    )


def grid_tables():
    counter = np.arange(SG)
    angles = (counter[:, None] * counter[None, :] % SG).astype(np.float64) * (2.0 * math.pi / SG)
    return np.cos(angles).astype(ml_dtypes.bfloat16), np.sin(angles).astype(ml_dtypes.bfloat16)


def exchange(blocks, axes, groups):
    return lax.all_to_all(blocks, axes, 0, 0, tiled=True, axis_index_groups=groups)


def shape(*dims, dtype=jnp.bfloat16):
    return jax.ShapeDtypeStruct(dims, dtype)


def shards(facet, row_offsets, col_offsets, vis_subgrid, vis_u, vis_v, observed):
    f32, bf16 = jnp.float32, jnp.bfloat16
    rows_count, cols_count = lax.axis_size("frow"), lax.axis_size("fcol")
    side = facet.shape[0]
    n_vis = vis_u.shape[0]
    chips = rows_count // 2
    each = SG // cols_count
    swap = [(index, index ^ 1) for index in range(rows_count)]
    turns = [[(index, (index + 2 * k) % rows_count) for index in range(rows_count)] for k in range(chips)]

    def turned(blocks):
        moved = {k: lax.ppermute(blocks[k], "frow", turns[k]) for k in (2, 1, 3)}
        return [blocks[0]] + [moved[k] for k in range(1, chips)]

    scale_in = 1.0 / (side * math.sqrt(rows_count * cols_count))
    scale_out = 1.0 / (SG * math.sqrt(NR * NC))
    line = (1, n_vis)

    send, vis = call(
        functools.partial(send_columns_kernel, cols_count), (shape(side + 16, 4 * HALF), shape(16, n_vis // 2)),
        "send_columns", "saaaaa",
        scratch=[
            pltpu.VMEM((side, 4 * HALF), bf16), pltpu.VMEM((side, side), bf16), pltpu.VMEM((3,) + line, jnp.int32),
            pltpu.VMEM((2, n_vis), f32), pltpu.SemaphoreType.DMA((5,)),
        ],
        cost=10**9, room=60,
    )(col_offsets, facet, vis_subgrid.reshape(line), vis_u.reshape(line), vis_v.reshape(line), observed)
    other = lax.ppermute(send, "frow", swap)
    own = call(
        functools.partial(own_columns_kernel, cols_count), shape(side, 4 * HALF), "own_columns", "sv",
        scratch=[pltpu.VMEM((side, 4 * HALF), bf16)], cost=10**9,
    )(col_offsets, facet)
    row_tab = call(
        functools.partial(row_tables_kernel, rows_count, side), shape(4, SG, 2 * side), "row_tables", "s", cost=10**9
    )(row_offsets)
    vis_rows_count = 8 * 2 * n_vis // LANES
    parts = call(
        functools.partial(contributions_kernel, scale_in), (shape(2 * SG + vis_rows_count, HALF),) * chips,
        "contributions", "vvvv", scratch=[pltpu.VMEM((2 * side, 4 * HALF), bf16)], cost=2 * 10**9,
    )(own, vis, other, row_tab)
    parts = turned(parts)

    pieces = call(
        gridding_kernel, shape(cols_count, 5 * each, HALF), "gridding", "v" * chips,
        scratch=[pltpu.VMEM((5, SG, HALF), f32)], cost=10**9,
    )(*parts)
    pieces = exchange(pieces, "fcol", None)
    pieces = call(pieces_sum_kernel, shape(cols_count, 5 * each, HALF), "pieces_sum", "v", cost=10**6)(pieces)
    pieces = exchange(pieces, "fcol", None)
    pieces_other = lax.ppermute(pieces, "frow", swap)

    back_row, back_col = call(
        functools.partial(back_tables_kernel, rows_count, cols_count, side),
        (shape(side, 4 * SG), shape(4 * SG, side)), "back_tables", "ss", cost=10**9,
    )(row_offsets, col_offsets)
    kcos, ksin = grid_tables()
    block = [np.concatenate(pair, 1) for pair in ((kcos, ksin), (-ksin, kcos), (kcos, -ksin), (ksin, kcos))]
    forward_block = np.concatenate([block[0], block[1]], 0)
    inverse_block = np.concatenate([block[2], block[3]], 0)
    *back, rest = call(
        functools.partial(grids_kernel, chips), (shape(2 * SG + 16, HALF),) * chips + (shape(2 * SG, HALF),), "grids",
        "v" * (6 + chips) + "a",
        scratch=[
            pltpu.VMEM((5, SG, SG), f32), pltpu.VMEM((SG, 2 * SG), bf16), pltpu.VMEM((2 * SG, SG), bf16),
            pltpu.VMEM((SG, 2 * SG), bf16),
        ],
        cost=10**9,
    )(pieces, pieces_other, *parts, inverse_block, forward_block, forward_block, inverse_block, back_col)
    back = turned(back)

    def first_part(number, mine, other):
        kernel = functools.partial(first_part_kernel, number)
        return call(kernel, shape(side, 2 * SG, dtype=f32), "first_part", "vvv", cost=10**9)(mine, other, back_row)

    firsts = [first_part(chips, back[0], rest)]
    back[1], firsts[0] = lax.optimization_barrier((back[1], firsts[0]))
    rest = [lax.ppermute(block, "frow", swap) for block in back[1:]]
    firsts.append(first_part(chips - 1, back[1], rest[0]))
    return call(
        functools.partial(image_kernel, scale_out, chips),
        (shape(side, side, dtype=f32), shape(2, n_vis, dtype=f32)), "image", "v" * (chips + 7), outs="aa",
        scratch=[
            pltpu.VMEM((side, 4 * SG), bf16), pltpu.VMEM((side, side), f32), pltpu.VMEM((2, n_vis), f32),
            pltpu.SemaphoreType.DMA((5,)),
        ],
        cost=10**9,
    )(*back, *rest[1:], *firsts, back_row, back_col, observed)


def solution(mesh):
    in_specs = (
        P("frow", "fcol"),
        P(),
        P(),
        P(("frow", "fcol")),
        P(("frow", "fcol")),
        P(("frow", "fcol")),
        P(None, ("frow", "fcol")),
    )
    out_specs = (P("frow", "fcol"), P(None, ("frow", "fcol")))
    return jax.shard_map(shards, mesh=mesh, in_specs=in_specs, out_specs=out_specs, check_vma=False)
```

```python
import functools
import math

import jax
import jax.numpy as jnp
import ml_dtypes
import numpy as np
from jax import lax
from jax.experimental import pallas as pl
from jax.experimental.pallas import tpu as pltpu
from jax.sharding import PartitionSpec as P

SKY = 65536
SG = 256
NR = 2
NC = 2
HALF = SG // 2
LANES = 128


def wave(count):
    count = count & (SKY - 1)
    turned = count + SKY // 8
    near = (turned & (SKY // 4 - 1)) - SKY // 8
    quarter = lax.shift_right_logical(turned, 14) & 3
    t = near.astype(jnp.float32) * (2.0 * math.pi / SKY)
    q = t * t
    sin = t * (1.0 + q * (-1.0 / 6 + q * (1.0 / 120 + q * (-1.0 / 5040 + q * (1.0 / 362880)))))
    cos = 1.0 + q * (-0.5 + q * (1.0 / 24 + q * (-1.0 / 720 + q * (1.0 / 40320))))
    odd = (quarter & 1) == 1
    one, two = jnp.where(odd, sin, cos), jnp.where(odd, cos, sin)
    return (
        jnp.where((quarter == 1) | (quarter == 2), -one, one),
        jnp.where(quarter >= 2, -two, two),
    )


def lanes(n):
    return lax.broadcasted_iota(jnp.int32, (1, n), 1)


def sublanes(n):
    return lax.broadcasted_iota(jnp.int32, (n, 1), 0)


def spread(coarse, fine, store):
    for k in range(coarse[0].shape[0]):
        c, s = coarse[0][k:k + 1], coarse[1][k:k + 1]
        store(k * 16, c * fine[0] - s * fine[1], s * fine[0] + c * fine[1])


def place():
    return lax.axis_index("frow"), lax.axis_index("fcol")


def half_columns(cols_count, offsets, half, side, col_tab):
    bf16 = jnp.bfloat16
    col_index = place()[1]
    unit = sublanes(16)
    col_step = SKY // (cols_count * side)
    col_base = col_index * (SKY // cols_count)
    freq = [offsets[c] + half * HALF + lanes(HALF) for c in range(NC)]
    freq = jnp.concatenate(freq, 1)
    coarse = wave((col_base + 16 * col_step * sublanes(side // 16)) * freq)
    fine = wave((col_step * unit) * freq)

    def store(at, cos, sin):
        for c in range(NC):
            some = slice(c * HALF, (c + 1) * HALF)
            col_tab[at:at + 16, 2 * c * HALF:(2 * c + 1) * HALF] = cos[:, some].astype(bf16)
            col_tab[at:at + 16, (2 * c + 1) * HALF:(2 * c + 2) * HALF] = sin[:, some].astype(bf16)

    spread(coarse, fine, store)


def send_columns_kernel(cols_count, offsets, facet, subgrid, u, v, observed, send, vis, *scratch):
    col_tab, image, indices, seen, first, made, tail, sems = scratch
    f32, bf16 = jnp.float32, jnp.bfloat16
    side = facet.shape[0]
    pairs = [
        (offsets, first), (facet, image), (subgrid, indices.at[0]), (u, indices.at[1]), (v, indices.at[2]), (observed, seen),
    ]
    copies = [pltpu.make_async_copy(source, target, sems.at[n]) for n, (source, target) in enumerate(pairs)]
    for copy in copies:
        copy.start()
    copies[0].wait()
    half_columns(cols_count, first, 1 - place()[0] % 2, side, col_tab)
    for copy in copies[2:]:
        copy.wait()
    some = jnp.concatenate([indices[n].astype(f32) for n in range(3)] + [seen[...], jnp.zeros((3, side), f32)], 0)
    some = jnp.concatenate([some[:, :side // 2], some[:, side // 2:]], 0).astype(bf16)
    tail[:, :side // 2] = some
    tail[:, side // 2:] = some
    writes = [
        pltpu.make_async_copy(tail.at[:, pl.ds(0, side // 2)], vis, sems.at[6]),
        pltpu.make_async_copy(tail, send.at[pl.ds(side, 16)], sems.at[7]),
    ]
    for write in writes:
        write.start()
    copies[1].wait()
    step = side // 2
    for n in range(2):
        at = pl.ds(n * step, step)
        made[at] = jnp.dot(image[at], col_tab[...], preferred_element_type=f32).astype(bf16)
        write = pltpu.make_async_copy(made.at[at], send.at[at], sems.at[8 + n])
        write.start()
        writes.append(write)
    for write in writes:
        write.wait()


def own_columns_kernel(cols_count, offsets, facet, own, col_tab):
    half_columns(cols_count, offsets, place()[0] % 2, facet.shape[0], col_tab)
    own[...] = jnp.dot(facet[...], col_tab[...], preferred_element_type=jnp.float32).astype(jnp.bfloat16)


def row_tables_kernel(rows_count, side, offsets, row_tab):
    bf16 = jnp.bfloat16
    row_index, _ = place()
    unit = sublanes(16)
    row_step = SKY // (rows_count * side)
    for f in range(2):
        pos = (row_index ^ f) * (SKY // rows_count) + row_step * lanes(side)
        fine = wave(unit * pos)
        for r in range(NR):
            coarse = wave((offsets[r] + 16 * unit) * pos)

            def store(at, cos, sin, r=r, f=f):
                row_tab[2 * r, at:at + 16, f * side:(f + 1) * side] = cos.astype(bf16)
                row_tab[2 * r + 1, at:at + 16, f * side:(f + 1) * side] = sin.astype(bf16)

            spread(coarse, fine, store)


def contributions_kernel(scale, own, own_vis, other, row_tab, *refs):
    f32, bf16 = jnp.float32, jnp.bfloat16
    outs, right = refs[:-1], refs[-1]
    chip = place()[0] // 2
    side = row_tab.shape[2] // 2
    vis = []
    right[:side] = own[...]
    right[side:] = other[:side]
    for some in (own_vis[...], other[side:]):
        vis += [some[:, k * LANES:(k + 1) * LANES] for k in range(side // 2 // LANES)]
    for n, out in enumerate(outs):
        for k, some in enumerate(vis):
            at = 2 * SG + 16 * k
            out[at:at + 16] = some
        r, c = split_number(chip + n)
        some = right[:, pl.ds(pl.multiple_of(c * SG, SG), SG)]
        with_cos = jnp.dot(row_tab[2 * r], some, preferred_element_type=f32)
        with_sin = jnp.dot(row_tab[2 * r + 1], some, preferred_element_type=f32)
        out[:SG] = ((with_cos[:, :HALF] - with_sin[:, HALF:]) * scale).astype(bf16)
        out[SG:2 * SG] = (-(with_cos[:, HALF:] + with_sin[:, :HALF]) * scale).astype(bf16)


def split_number(number):
    number = lax.rem(number, NR * NC)
    return number // NC, lax.rem(number, NC)


def vis_rows(block):
    count = block.shape[0] // 16
    return jnp.concatenate(
        [block[16 * k + 8 * part:16 * k + 8 * part + 8] for part in range(2) for k in range(count)], 1
    )


def grid_sums(parts):
    f32, bf16 = jnp.float32, jnp.bfloat16
    row_index, _ = place()
    chip = (row_index // 2).astype(f32)
    v_at = (sublanes(HALF) + (row_index % 2) * HALF).astype(f32)
    counter = sublanes(SG).astype(f32)
    total = jnp.zeros((SG, 3 * HALF), f32)
    planes = [jnp.zeros((SG, HALF), f32)] * 2
    for part in parts:
        one = vis_rows(part[2 * SG:].astype(f32))
        u_here = jnp.where(one[0:1] == chip, one[1:2], -1.0)
        hot = jnp.where(u_here == counter, 1.0, 0.0).astype(bf16)
        pick = one[2:3] == v_at
        right = jnp.concatenate(
            [jnp.where(pick, one[3:4], 0.0), jnp.where(pick, one[4:5], 0.0), jnp.where(pick, 1.0, 0.0)], 0
        ).astype(bf16)
        total = total + lax.dot_general(hot, right, (((1,), (1,)), ((), ())), preferred_element_type=f32)
        planes = [planes[p] + part[p * SG:(p + 1) * SG].astype(f32) for p in range(2)]
    return planes + [total[:, p * HALF:(p + 1) * HALF] for p in range(3)]


def first_sums_kernel(*refs):
    for p, plane in enumerate(grid_sums(refs[:-1])):
        refs[-1][p] = plane


def gridding_kernel(*refs):
    parts, (first, pieces, planes) = refs[:-3], refs[-3:]
    for p, plane in enumerate(grid_sums(parts)):
        planes[p] = first[p] + plane
    each = SG // pieces.shape[0]
    for j in range(pieces.shape[0]):
        rows = [planes[p, j * each:(j + 1) * each] for p in range(5)]
        pieces[j] = jnp.concatenate(rows, 0).astype(jnp.bfloat16)


def pieces_sum_kernel(pieces, out):
    f32, bf16 = jnp.float32, jnp.bfloat16
    total = pieces[0].astype(f32)
    for j in range(1, pieces.shape[0]):
        total = total + pieces[j].astype(f32)
    total = total.astype(bf16)
    for j in range(out.shape[0]):
        out[j] = total


def grids_kernel(chips, near, *refs):
    f32, bf16 = jnp.float32, jnp.bfloat16
    own, other, refs = refs[:near], refs[near:2 * near], refs[2 * near:]
    parts, (grid_left, forward, inverse_left, inverse, _) = refs[:chips], refs[chips:chips + 5]
    outs, rest, (planes, cat, tall, hat) = refs[chips + 5:-5], refs[-5], refs[-4:]
    row_index, col_index = place()
    core = row_index % 2
    chip = (row_index // 2).astype(f32)
    count = own[0].shape[0]
    each = SG // (count * near)
    for blocks, half in ((own, core), (other, 1 - core)):
        at = pl.ds(pl.multiple_of(half * HALF, HALF), HALF)
        for k, pieces in enumerate(blocks):
            line = lax.rem(col_index + near - k, near)
            for j in range(count):
                some = pieces[j].astype(f32)
                rows = pl.ds(pl.multiple_of((j * near + line) * each, each), each)
                for p in range(5):
                    planes[p, rows, at] = some[p * each:(p + 1) * each]
    cat[:, :SG] = planes[0].astype(bf16)
    cat[:, SG:] = planes[1].astype(bf16)
    wide = jnp.dot(cat[...], forward[...], preferred_element_type=f32).astype(bf16)
    tall[:SG] = wide[:, :SG]
    tall[SG:] = wide[:, SG:]
    model = jnp.dot(grid_left[...], tall[...], preferred_element_type=f32) * (1.0 / SG)
    hat_real, hat_imag = model[:SG], model[SG:]
    cat[:, :SG] = (planes[2] - planes[4] * hat_real).astype(bf16)
    cat[:, SG:] = (planes[3] - planes[4] * hat_imag).astype(bf16)
    hat[:, :SG] = hat_real.astype(bf16)
    hat[:, SG:] = hat_imag.astype(bf16)
    wide = jnp.dot(cat[...], inverse[...], preferred_element_type=f32)
    for k in range(2):
        tall[k * SG:(k + 1) * SG] = wide[:, k * SG:(k + 1) * SG].astype(bf16)
    back = jnp.dot(inverse_left[...], tall[...], preferred_element_type=f32) * (1.0 / SG)
    rest[...] = jnp.where(core == 0, back[:, HALF:], back[:, :HALF]).astype(bf16)
    back = jnp.where(core == 0, back[:, :HALF], back[:, HALF:]).astype(bf16)
    counter = sublanes(SG).astype(f32)
    vis_each = (parts[0].shape[0] - 2 * SG) // 2
    for k, out in enumerate(outs):
        out[:2 * SG] = back
        ask = vis_rows(parts[-k % chips][2 * SG:2 * SG + vis_each].astype(f32))
        u_here = jnp.where(ask[0:1] == chip, ask[1:2], -1.0)
        hot = jnp.where(u_here == counter, 1.0, 0.0).astype(bf16)
        pick = ask[2:3] == counter
        line = lax.dot_general(hat[...], hot, (((0,), (0,)), ((), ())), preferred_element_type=f32)
        rows = []
        for part in range(2):
            value = jnp.sum(jnp.where(pick, line[part * SG:(part + 1) * SG], 0.0), axis=0, keepdims=True)
            rows += [value[:, i * LANES:(i + 1) * LANES] for i in range(value.shape[1] // LANES)]
        rows.append(jnp.zeros((16 - len(rows), LANES), f32))
        out[2 * SG:] = jnp.concatenate(rows, 0).astype(bf16)


def back_tables_kernel(rows_count, cols_count, side, offsets_row, offsets_col, row_tab, col_tab):
    bf16 = jnp.bfloat16
    row_index, col_index = place()
    unit = sublanes(16)
    row_step = SKY // (rows_count * side)
    row_base = row_index * (SKY // rows_count)
    for r in range(NR):
        freq = offsets_row[r] + lanes(SG)
        coarse = wave((row_base + 16 * row_step * sublanes(side // 16)) * freq)
        fine = wave((row_step * unit) * freq)

        def store(at, cos, sin, r=r):
            row_tab[at:at + 16, 2 * r * SG:(2 * r + 1) * SG] = cos.astype(bf16)
            row_tab[at:at + 16, (2 * r + 1) * SG:(2 * r + 2) * SG] = sin.astype(bf16)

        spread(coarse, fine, store)
    col_step = SKY // (cols_count * side)
    pos = col_index * (SKY // cols_count) + col_step * lanes(side)
    fine = wave(unit * pos)
    for c in range(NC):
        coarse = wave((offsets_col[c] + 16 * unit) * pos)

        def store(at, cos, sin, c=c):
            left = (at // HALF * 2 * NC + 2 * c) * HALF + at % HALF
            col_tab[left:left + 16] = cos.astype(bf16)
            col_tab[left + HALF:left + HALF + 16] = (-sin).astype(bf16)

        spread(coarse, fine, store)


def block_part(block, number, row_tab):
    r, _ = split_number(number)
    real, imag = block[:SG], block[SG:2 * SG]
    right = jnp.concatenate([jnp.concatenate([real, imag], 1), jnp.concatenate([-imag, real], 1)], 0)
    left = row_tab[:, pl.ds(pl.multiple_of(2 * r * SG, 2 * SG), 2 * SG)]
    return jnp.dot(left, right, preferred_element_type=jnp.float32)


def first_part_kernel(number, own, rest, row_tab, out):
    chip = place()[0] // 2
    for half, block in enumerate((own, rest)):
        out[:, half * SG:(half + 1) * SG] = block_part(block, chip + number, row_tab)


def image_kernel(scale, chips, *refs):
    f32, bf16 = jnp.float32, jnp.bfloat16
    blocks, others, firsts, refs = refs[:chips], refs[chips:chips + 2], refs[chips + 2:chips + 4], refs[chips + 4:]
    row_tab, col_tab, observed, out, residual, both, image, seen, sems = refs
    row_index, _ = place()
    core, chip = row_index % 2, row_index // 2
    model = jnp.zeros((16, LANES), f32)
    for block in blocks:
        model = model + block[2 * SG:].astype(f32)
    count = observed.shape[1] // LANES
    for part in range(2):
        for i in range(count):
            at = slice(i * LANES, (i + 1) * LANES)
            seen[part:part + 1, at] = observed[part:part + 1, at] - model[part * count + i:part * count + i + 1]
    writes = [pltpu.make_async_copy(seen, residual, sems.at[0])]
    writes[0].start()
    for k in range(2, chips):
        c = split_number(chip + chips - k)[1]
        for n, block in enumerate((blocks[k], others[k - 2])):
            half = core if n == 0 else 1 - core
            at = pl.ds(pl.multiple_of((half * NC + c) * SG, SG), SG)
            part = firsts[k - 2][:, n * SG:(n + 1) * SG] + block_part(block, chip + chips - k, row_tab)
            both[:, at] = part.astype(bf16)
    chunks = sems.shape[0] - 1
    step = image.shape[0] // chunks
    for n in range(chunks):
        at = slice(n * step, (n + 1) * step)
        image[at] = jnp.dot(both[at], col_tab[...], preferred_element_type=f32) * scale
        write = pltpu.make_async_copy(image.at[at], out.at[at], sems.at[1 + n])
        write.start()
        writes.append(write)
    for write in writes:
        write.wait()


def call(kernel, out_shape, name, spaces, scratch=(), cost=0, outs=None, room=24):
    kinds = {"s": pltpu.SMEM, "v": pltpu.VMEM, "a": pl.ANY}
    several = isinstance(out_shape, tuple)
    outs = outs or "v" * (len(out_shape) if several else 1)
    out_specs = tuple(pl.BlockSpec(memory_space=kinds[kind]) for kind in outs)
    return pl.pallas_call(
        kernel,
        out_shape=out_shape,
        in_specs=[pl.BlockSpec(memory_space=kinds[kind]) for kind in spaces],
        out_specs=out_specs if several else out_specs[0],
        scratch_shapes=list(scratch),
        compiler_params=pltpu.CompilerParams(vmem_limit_bytes=room * 2**20),
        cost_estimate=pl.CostEstimate(flops=cost, bytes_accessed=2**20, transcendentals=0),
        name=name,
    )


def grid_tables():
    counter = np.arange(SG)
    angles = (counter[:, None] * counter[None, :] % SG).astype(np.float64) * (2.0 * math.pi / SG)
    return np.cos(angles).astype(ml_dtypes.bfloat16), np.sin(angles).astype(ml_dtypes.bfloat16)


def exchange(blocks, axes, groups):
    return lax.all_to_all(blocks, axes, 0, 0, tiled=True, axis_index_groups=groups)


def shape(*dims, dtype=jnp.bfloat16):
    return jax.ShapeDtypeStruct(dims, dtype)


def shards(facet, row_offsets, col_offsets, vis_subgrid, vis_u, vis_v, observed):
    f32, bf16 = jnp.float32, jnp.bfloat16
    rows_count, cols_count = lax.axis_size("frow"), lax.axis_size("fcol")
    side = facet.shape[0]
    n_vis = vis_u.shape[0]
    chips = rows_count // 2
    each = SG // cols_count
    swap = [(index, index ^ 1) for index in range(rows_count)]
    turns = [[(index, (index + 2 * k) % rows_count) for index in range(rows_count)] for k in range(chips)]

    def turned(blocks):
        moved = {k: lax.ppermute(blocks[k], "frow", turns[k]) for k in (2, 1, 3)}
        return [blocks[0]] + [moved[k] for k in range(1, chips)]

    scale_in = 1.0 / (side * math.sqrt(rows_count * cols_count))
    scale_out = 1.0 / (SG * math.sqrt(NR * NC))
    near = 4
    line = (1, n_vis)

    send, vis = call(
        functools.partial(send_columns_kernel, cols_count), (shape(side + 16, 4 * HALF), shape(16, n_vis // 2)),
        "send_columns", "aaaaaa",
        scratch=[
            pltpu.VMEM((side, 4 * HALF), bf16), pltpu.VMEM((side, side), bf16), pltpu.VMEM((3,) + line, jnp.int32),
            pltpu.VMEM((2, n_vis), f32), pltpu.SMEM((NC,), jnp.int32), pltpu.VMEM((side, 4 * HALF), bf16),
            pltpu.VMEM((16, n_vis), bf16), pltpu.SemaphoreType.DMA((10,)),
        ],
        cost=10**9, room=60, outs="aa",
    )(col_offsets, facet, vis_subgrid.reshape(line), vis_u.reshape(line), vis_v.reshape(line), observed)
    other = lax.ppermute(send, "frow", swap)
    own = call(
        functools.partial(own_columns_kernel, cols_count), shape(side, 4 * HALF), "own_columns", "sv",
        scratch=[pltpu.VMEM((side, 4 * HALF), bf16)], cost=10**9,
    )(col_offsets, facet)
    row_tab = call(
        functools.partial(row_tables_kernel, rows_count, side), shape(4, SG, 2 * side), "row_tables", "s", cost=10**9
    )(row_offsets)
    vis_rows_count = 8 * 2 * n_vis // LANES
    parts = call(
        functools.partial(contributions_kernel, scale_in), (shape(2 * SG + vis_rows_count, HALF),) * chips,
        "contributions", "vvvv", scratch=[pltpu.VMEM((2 * side, 4 * HALF), bf16)], cost=2 * 10**9,
    )(own, vis, other, row_tab)
    parts = turned(parts)

    sums = call(first_sums_kernel, shape(5, SG, HALF, dtype=f32), "first_sums", "vv", cost=10**9)(*parts[:2])
    pieces = call(
        gridding_kernel, shape(cols_count, 5 * each, HALF), "gridding", "v" * (chips - 1),
        scratch=[pltpu.VMEM((5, SG, HALF), f32)], cost=10**9,
    )(*parts[2:], sums)
    pieces = exchange(pieces, "fcol", None)
    far = cols_count // near
    pieces = call(pieces_sum_kernel, shape(far, 5 * each, HALF), "pieces_sum", "v", cost=10**6)(pieces)
    pieces = exchange(pieces, "fcol", [[near * step + line for step in range(far)] for line in range(near)])
    lines = [[(index, index // near * near + (index + k) % near) for index in range(cols_count)] for k in range(near)]
    pieces = [pieces] + [lax.ppermute(pieces, "fcol", lines[k]) for k in range(1, near)]
    pieces_other = [lax.ppermute(block, "frow", swap) for block in pieces]

    back_row, back_col = call(
        functools.partial(back_tables_kernel, rows_count, cols_count, side),
        (shape(side, 4 * SG), shape(4 * SG, side)), "back_tables", "ss", cost=10**9,
    )(row_offsets, col_offsets)
    kcos, ksin = grid_tables()
    block = [np.concatenate(pair, 1) for pair in ((kcos, ksin), (-ksin, kcos), (kcos, -ksin), (ksin, kcos))]
    forward_block = np.concatenate([block[0], block[1]], 0)
    inverse_block = np.concatenate([block[2], block[3]], 0)
    *back, rest = call(
        functools.partial(grids_kernel, chips, near), (shape(2 * SG + 16, HALF),) * chips + (shape(2 * SG, HALF),), "grids",
        "v" * (4 + chips + 2 * near) + "a",
        scratch=[
            pltpu.VMEM((5, SG, SG), f32), pltpu.VMEM((SG, 2 * SG), bf16), pltpu.VMEM((2 * SG, SG), bf16),
            pltpu.VMEM((SG, 2 * SG), bf16),
        ],
        cost=10**9,
    )(*pieces, *pieces_other, *parts, inverse_block, forward_block, forward_block, inverse_block, back_col)
    back = turned(back)

    def first_part(number, mine, other):
        kernel = functools.partial(first_part_kernel, number)
        return call(kernel, shape(side, 2 * SG, dtype=f32), "first_part", "vvv", cost=10**9)(mine, other, back_row)

    firsts = [first_part(chips, back[0], rest)]
    back[1], firsts[0] = lax.optimization_barrier((back[1], firsts[0]))
    rest = [lax.ppermute(block, "frow", swap) for block in back[1:]]
    firsts.append(first_part(chips - 1, back[1], rest[0]))
    return call(
        functools.partial(image_kernel, scale_out, chips),
        (shape(side, side, dtype=f32), shape(2, n_vis, dtype=f32)), "image", "v" * (chips + 7), outs="aa",
        scratch=[
            pltpu.VMEM((side, 4 * SG), bf16), pltpu.VMEM((side, side), f32), pltpu.VMEM((2, n_vis), f32),
            pltpu.SemaphoreType.DMA((5,)),
        ],
        cost=10**9,
    )(*back, *rest[1:], *firsts, back_row, back_col, observed)


def solution(mesh):
    in_specs = (
        P("frow", "fcol"),
        P(),
        P(),
        P(("frow", "fcol")),
        P(("frow", "fcol")),
        P(("frow", "fcol")),
        P(None, ("frow", "fcol")),
    )
    out_specs = (P("frow", "fcol"), P(None, ("frow", "fcol")))
    return jax.shard_map(shards, mesh=mesh, in_specs=in_specs, out_specs=out_specs, check_vma=False)
```

```python
import functools
import math

import jax
import jax.numpy as jnp
import ml_dtypes
import numpy as np
from jax import lax
from jax.experimental import pallas as pl
from jax.experimental.pallas import tpu as pltpu
from jax.sharding import PartitionSpec as P

SKY = 65536
SG = 256
NR = 2
NC = 2
HALF = SG // 2
LANES = 128


def wave(count):
    count = count & (SKY - 1)
    turned = count + SKY // 8
    near = (turned & (SKY // 4 - 1)) - SKY // 8
    quarter = lax.shift_right_logical(turned, 14) & 3
    t = near.astype(jnp.float32) * (2.0 * math.pi / SKY)
    q = t * t
    sin = t * (1.0 + q * (-1.0 / 6 + q * (1.0 / 120 + q * (-1.0 / 5040 + q * (1.0 / 362880)))))
    cos = 1.0 + q * (-0.5 + q * (1.0 / 24 + q * (-1.0 / 720 + q * (1.0 / 40320))))
    odd = (quarter & 1) == 1
    one, two = jnp.where(odd, sin, cos), jnp.where(odd, cos, sin)
    return (
        jnp.where((quarter == 1) | (quarter == 2), -one, one),
        jnp.where(quarter >= 2, -two, two),
    )


def lanes(n):
    return lax.broadcasted_iota(jnp.int32, (1, n), 1)


def sublanes(n):
    return lax.broadcasted_iota(jnp.int32, (n, 1), 0)


def spread(coarse, fine, store):
    for k in range(coarse[0].shape[0]):
        c, s = coarse[0][k:k + 1], coarse[1][k:k + 1]
        store(k * 16, c * fine[0] - s * fine[1], s * fine[0] + c * fine[1])


def place():
    return lax.axis_index("frow"), lax.axis_index("fcol")


def half_columns(cols_count, offsets, half, side, col_tab):
    bf16 = jnp.bfloat16
    col_index = place()[1]
    unit = sublanes(16)
    col_step = SKY // (cols_count * side)
    col_base = col_index * (SKY // cols_count)
    freq = [offsets[c] + half * HALF + lanes(HALF) for c in range(NC)]
    freq = jnp.concatenate(freq, 1)
    coarse = wave((col_base + 16 * col_step * sublanes(side // 16)) * freq)
    fine = wave((col_step * unit) * freq)

    def store(at, cos, sin):
        for c in range(NC):
            some = slice(c * HALF, (c + 1) * HALF)
            col_tab[at:at + 16, 2 * c * HALF:(2 * c + 1) * HALF] = cos[:, some].astype(bf16)
            col_tab[at:at + 16, (2 * c + 1) * HALF:(2 * c + 2) * HALF] = sin[:, some].astype(bf16)

    spread(coarse, fine, store)


def send_columns_kernel(cols_count, offsets, facet, subgrid, u, v, observed, send, vis, *scratch):
    col_tab, image, indices, seen, first, made, tail, sems = scratch
    f32, bf16 = jnp.float32, jnp.bfloat16
    side = facet.shape[0]
    pairs = [
        (offsets, first), (facet, image), (subgrid, indices.at[0]), (u, indices.at[1]), (v, indices.at[2]), (observed, seen),
    ]
    copies = [pltpu.make_async_copy(source, target, sems.at[n]) for n, (source, target) in enumerate(pairs)]
    for copy in copies:
        copy.start()
    copies[0].wait()
    half_columns(cols_count, first, 1 - place()[0] % 2, side, col_tab)
    for copy in copies[2:]:
        copy.wait()
    some = jnp.concatenate([indices[n].astype(f32) for n in range(3)] + [seen[...], jnp.zeros((3, side), f32)], 0)
    some = jnp.concatenate([some[:, :side // 2], some[:, side // 2:]], 0).astype(bf16)
    tail[:, :side // 2] = some
    tail[:, side // 2:] = some
    writes = [
        pltpu.make_async_copy(tail.at[:, pl.ds(0, side // 2)], vis, sems.at[6]),
        pltpu.make_async_copy(tail, send.at[pl.ds(side, 16)], sems.at[7]),
    ]
    for write in writes:
        write.start()
    copies[1].wait()
    step = side // 2
    for n in range(2):
        at = pl.ds(n * step, step)
        made[at] = jnp.dot(image[at], col_tab[...], preferred_element_type=f32).astype(bf16)
        write = pltpu.make_async_copy(made.at[at], send.at[at], sems.at[8 + n])
        write.start()
        writes.append(write)
    for write in writes:
        write.wait()


def own_tables_kernel(rows_count, cols_count, offsets, col_offsets, facet, own, row_tab, col_tab):
    bf16 = jnp.bfloat16
    row_index, _ = place()
    side = facet.shape[0]
    half_columns(cols_count, col_offsets, row_index % 2, side, col_tab)
    own[...] = jnp.dot(facet[...], col_tab[...], preferred_element_type=jnp.float32).astype(bf16)
    unit = sublanes(16)
    row_step = SKY // (rows_count * side)
    for f in range(2):
        pos = (row_index ^ f) * (SKY // rows_count) + row_step * lanes(side)
        fine = wave(unit * pos)
        for r in range(NR):
            coarse = wave((offsets[r] + 16 * unit) * pos)

            def store(at, cos, sin, r=r, f=f):
                row_tab[2 * r, at:at + 16, f * side:(f + 1) * side] = cos.astype(bf16)
                row_tab[2 * r + 1, at:at + 16, f * side:(f + 1) * side] = sin.astype(bf16)

            spread(coarse, fine, store)


def contributions_kernel(scale, own, own_vis, other, row_tab, *refs):
    f32, bf16 = jnp.float32, jnp.bfloat16
    outs, right = refs[:-1], refs[-1]
    chip = place()[0] // 2
    side = row_tab.shape[2] // 2
    vis = []
    right[:side] = own[...]
    right[side:] = other[:side]
    for some in (own_vis[...], other[side:]):
        vis += [some[:, k * LANES:(k + 1) * LANES] for k in range(side // 2 // LANES)]
    for n, out in enumerate(outs):
        for k, some in enumerate(vis):
            at = 2 * SG + 16 * k
            out[at:at + 16] = some
        r, c = split_number(chip + n)
        some = right[:, pl.ds(pl.multiple_of(c * SG, SG), SG)]
        with_cos = jnp.dot(row_tab[2 * r], some, preferred_element_type=f32)
        with_sin = jnp.dot(row_tab[2 * r + 1], some, preferred_element_type=f32)
        out[:SG] = ((with_cos[:, :HALF] - with_sin[:, HALF:]) * scale).astype(bf16)
        out[SG:2 * SG] = (-(with_cos[:, HALF:] + with_sin[:, :HALF]) * scale).astype(bf16)


def split_number(number):
    number = lax.rem(number, NR * NC)
    return number // NC, lax.rem(number, NC)


def vis_rows(block):
    count = block.shape[0] // 16
    return jnp.concatenate(
        [block[16 * k + 8 * part:16 * k + 8 * part + 8] for part in range(2) for k in range(count)], 1
    )


def grid_sums(parts):
    f32, bf16 = jnp.float32, jnp.bfloat16
    row_index, _ = place()
    chip = (row_index // 2).astype(f32)
    v_at = (sublanes(HALF) + (row_index % 2) * HALF).astype(f32)
    counter = sublanes(SG).astype(f32)
    total = jnp.zeros((SG, 3 * HALF), f32)
    planes = [jnp.zeros((SG, HALF), f32)] * 2
    for part in parts:
        one = vis_rows(part[2 * SG:].astype(f32))
        u_here = jnp.where(one[0:1] == chip, one[1:2], -1.0)
        hot = jnp.where(u_here == counter, 1.0, 0.0).astype(bf16)
        pick = one[2:3] == v_at
        right = jnp.concatenate(
            [jnp.where(pick, one[3:4], 0.0), jnp.where(pick, one[4:5], 0.0), jnp.where(pick, 1.0, 0.0)], 0
        ).astype(bf16)
        total = total + lax.dot_general(hot, right, (((1,), (1,)), ((), ())), preferred_element_type=f32)
        planes = [planes[p] + part[p * SG:(p + 1) * SG].astype(f32) for p in range(2)]
    return planes + [total[:, p * HALF:(p + 1) * HALF] for p in range(3)]


def first_sums_kernel(*refs):
    for p, plane in enumerate(grid_sums(refs[:-1])):
        refs[-1][p] = plane


def gridding_kernel(*refs):
    parts, (first, _, pieces, planes) = refs[:-4], refs[-4:]
    for p, plane in enumerate(grid_sums(parts)):
        planes[p] = first[p] + plane
    each = SG // pieces.shape[0]
    for j in range(pieces.shape[0]):
        rows = [planes[p, j * each:(j + 1) * each] for p in range(5)]
        pieces[j] = jnp.concatenate(rows, 0).astype(jnp.bfloat16)


def pieces_sum_kernel(pieces, out):
    f32, bf16 = jnp.float32, jnp.bfloat16
    total = pieces[0].astype(f32)
    for j in range(1, pieces.shape[0]):
        total = total + pieces[j].astype(f32)
    total = total.astype(bf16)
    for j in range(out.shape[0]):
        out[j] = total


def grids_kernel(chips, own, other, *refs):
    f32, bf16 = jnp.float32, jnp.bfloat16
    parts, (grid_left, forward, inverse_left, inverse) = refs[:chips], refs[chips:chips + 4]
    outs, rest, (planes, cat, tall, hat) = refs[chips + 4:-5], refs[-5], refs[-4:]
    row_index, _ = place()
    core = row_index % 2
    chip = (row_index // 2).astype(f32)
    count = own.shape[0]
    each = SG // count
    for pieces, half in ((own, core), (other, 1 - core)):
        at = pl.ds(pl.multiple_of(half * HALF, HALF), HALF)
        for j in range(count):
            some = pieces[j].astype(f32)
            for p in range(5):
                planes[p, j * each:(j + 1) * each, at] = some[p * each:(p + 1) * each]
    cat[:, :SG] = planes[0].astype(bf16)
    cat[:, SG:] = planes[1].astype(bf16)
    wide = jnp.dot(cat[...], forward[...], preferred_element_type=f32).astype(bf16)
    tall[:SG] = wide[:, :SG]
    tall[SG:] = wide[:, SG:]
    model = jnp.dot(grid_left[...], tall[...], preferred_element_type=f32) * (1.0 / SG)
    hat_real, hat_imag = model[:SG], model[SG:]
    cat[:, :SG] = (planes[2] - planes[4] * hat_real).astype(bf16)
    cat[:, SG:] = (planes[3] - planes[4] * hat_imag).astype(bf16)
    hat[:, :SG] = hat_real.astype(bf16)
    hat[:, SG:] = hat_imag.astype(bf16)
    wide = jnp.dot(cat[...], inverse[...], preferred_element_type=f32)
    for k in range(2):
        tall[k * SG:(k + 1) * SG] = wide[:, k * SG:(k + 1) * SG].astype(bf16)
    back = jnp.dot(inverse_left[...], tall[...], preferred_element_type=f32) * (1.0 / SG)
    rest[...] = jnp.where(core == 0, back[:, HALF:], back[:, :HALF]).astype(bf16)
    back = jnp.where(core == 0, back[:, :HALF], back[:, HALF:]).astype(bf16)
    counter = sublanes(SG).astype(f32)
    vis_each = (parts[0].shape[0] - 2 * SG) // 2
    for k, out in enumerate(outs):
        out[:2 * SG] = back
        ask = vis_rows(parts[-k % chips][2 * SG:2 * SG + vis_each].astype(f32))
        u_here = jnp.where(ask[0:1] == chip, ask[1:2], -1.0)
        hot = jnp.where(u_here == counter, 1.0, 0.0).astype(bf16)
        pick = ask[2:3] == counter
        line = lax.dot_general(hat[...], hot, (((0,), (0,)), ((), ())), preferred_element_type=f32)
        rows = []
        for part in range(2):
            value = jnp.sum(jnp.where(pick, line[part * SG:(part + 1) * SG], 0.0), axis=0, keepdims=True)
            rows += [value[:, i * LANES:(i + 1) * LANES] for i in range(value.shape[1] // LANES)]
        rows.append(jnp.zeros((16 - len(rows), LANES), f32))
        out[2 * SG:] = jnp.concatenate(rows, 0).astype(bf16)


def back_tables_kernel(rows_count, cols_count, side, offsets_row, offsets_col, row_tab, col_tab):
    bf16 = jnp.bfloat16
    row_index, col_index = place()
    unit = sublanes(16)
    row_step = SKY // (rows_count * side)
    row_base = row_index * (SKY // rows_count)
    for r in range(NR):
        freq = offsets_row[r] + lanes(SG)
        coarse = wave((row_base + 16 * row_step * sublanes(side // 16)) * freq)
        fine = wave((row_step * unit) * freq)

        def store(at, cos, sin, r=r):
            row_tab[at:at + 16, 2 * r * SG:(2 * r + 1) * SG] = cos.astype(bf16)
            row_tab[at:at + 16, (2 * r + 1) * SG:(2 * r + 2) * SG] = sin.astype(bf16)

        spread(coarse, fine, store)
    col_step = SKY // (cols_count * side)
    pos = col_index * (SKY // cols_count) + col_step * lanes(side)
    fine = wave(unit * pos)
    for c in range(NC):
        coarse = wave((offsets_col[c] + 16 * unit) * pos)

        def store(at, cos, sin, c=c):
            left = (at // HALF * 2 * NC + 2 * c) * HALF + at % HALF
            col_tab[left:left + 16] = cos.astype(bf16)
            col_tab[left + HALF:left + HALF + 16] = (-sin).astype(bf16)

        spread(coarse, fine, store)


def block_part(block, number, row_tab):
    r, _ = split_number(number)
    real, imag = block[:SG], block[SG:2 * SG]
    right = jnp.concatenate([jnp.concatenate([real, imag], 1), jnp.concatenate([-imag, real], 1)], 0)
    left = row_tab[:, pl.ds(pl.multiple_of(2 * r * SG, 2 * SG), 2 * SG)]
    return jnp.dot(left, right, preferred_element_type=jnp.float32)


def first_part_kernel(number, own, rest, row_tab, out):
    chip = place()[0] // 2
    for half, block in enumerate((own, rest)):
        out[:, half * SG:(half + 1) * SG] = block_part(block, chip + number, row_tab)


def image_kernel(scale, chips, *refs):
    f32, bf16 = jnp.float32, jnp.bfloat16
    blocks, others, firsts, refs = refs[:chips], refs[chips:chips + 2], refs[chips + 2:chips + 4], refs[chips + 4:]
    row_tab, col_tab, observed, out, residual, both, image, seen, sems = refs
    row_index, _ = place()
    core, chip = row_index % 2, row_index // 2
    model = jnp.zeros((16, LANES), f32)
    for block in blocks:
        model = model + block[2 * SG:].astype(f32)
    count = observed.shape[1] // LANES
    for part in range(2):
        for i in range(count):
            at = slice(i * LANES, (i + 1) * LANES)
            seen[part:part + 1, at] = observed[part:part + 1, at] - model[part * count + i:part * count + i + 1]
    writes = [pltpu.make_async_copy(seen, residual, sems.at[0])]
    writes[0].start()
    for k in range(2, chips):
        c = split_number(chip + chips - k)[1]
        for n, block in enumerate((blocks[k], others[k - 2])):
            half = core if n == 0 else 1 - core
            at = pl.ds(pl.multiple_of((half * NC + c) * SG, SG), SG)
            part = firsts[k - 2][:, n * SG:(n + 1) * SG] + block_part(block, chip + chips - k, row_tab)
            both[:, at] = part.astype(bf16)
    chunks = sems.shape[0] - 1
    step = image.shape[0] // chunks
    for n in range(chunks):
        at = slice(n * step, (n + 1) * step)
        image[at] = jnp.dot(both[at], col_tab[...], preferred_element_type=f32) * scale
        write = pltpu.make_async_copy(image.at[at], out.at[at], sems.at[1 + n])
        write.start()
        writes.append(write)
    for write in writes:
        write.wait()


def call(kernel, out_shape, name, spaces, scratch=(), cost=0, outs=None, room=24):
    kinds = {"s": pltpu.SMEM, "v": pltpu.VMEM, "a": pl.ANY}
    several = isinstance(out_shape, tuple)
    outs = outs or "v" * (len(out_shape) if several else 1)
    out_specs = tuple(pl.BlockSpec(memory_space=kinds[kind]) for kind in outs)
    return pl.pallas_call(
        kernel,
        out_shape=out_shape,
        in_specs=[pl.BlockSpec(memory_space=kinds[kind]) for kind in spaces],
        out_specs=out_specs if several else out_specs[0],
        scratch_shapes=list(scratch),
        compiler_params=pltpu.CompilerParams(vmem_limit_bytes=room * 2**20),
        cost_estimate=pl.CostEstimate(flops=cost, bytes_accessed=2**20, transcendentals=0),
        name=name,
    )


def grid_tables():
    counter = np.arange(SG)
    angles = (counter[:, None] * counter[None, :] % SG).astype(np.float64) * (2.0 * math.pi / SG)
    return np.cos(angles).astype(ml_dtypes.bfloat16), np.sin(angles).astype(ml_dtypes.bfloat16)


def exchange(blocks, axes, groups):
    return lax.all_to_all(blocks, axes, 0, 0, tiled=True, axis_index_groups=groups)


def shape(*dims, dtype=jnp.bfloat16):
    return jax.ShapeDtypeStruct(dims, dtype)


def shards(facet, row_offsets, col_offsets, vis_subgrid, vis_u, vis_v, observed):
    f32, bf16 = jnp.float32, jnp.bfloat16
    rows_count, cols_count = lax.axis_size("frow"), lax.axis_size("fcol")
    side = facet.shape[0]
    n_vis = vis_u.shape[0]
    chips = rows_count // 2
    each = SG // cols_count
    swap = [(index, index ^ 1) for index in range(rows_count)]
    turns = [[(index, (index + 2 * k) % rows_count) for index in range(rows_count)] for k in range(chips)]

    def turned(blocks):
        moved = {k: lax.ppermute(blocks[k], "frow", turns[k]) for k in (2, 1, 3)}
        return [blocks[0]] + [moved[k] for k in range(1, chips)]

    scale_in = 1.0 / (side * math.sqrt(rows_count * cols_count))
    scale_out = 1.0 / (SG * math.sqrt(NR * NC))
    line = (1, n_vis)

    send, vis = call(
        functools.partial(send_columns_kernel, cols_count), (shape(side + 16, 4 * HALF), shape(16, n_vis // 2)),
        "send_columns", "aaaaaa",
        scratch=[
            pltpu.VMEM((side, 4 * HALF), bf16), pltpu.VMEM((side, side), bf16), pltpu.VMEM((3,) + line, jnp.int32),
            pltpu.VMEM((2, n_vis), f32), pltpu.SMEM((NC,), jnp.int32), pltpu.VMEM((side, 4 * HALF), bf16),
            pltpu.VMEM((16, n_vis), bf16), pltpu.SemaphoreType.DMA((10,)),
        ],
        cost=10**9, room=60, outs="aa",
    )(col_offsets, facet, vis_subgrid.reshape(line), vis_u.reshape(line), vis_v.reshape(line), observed)
    other = lax.ppermute(send, "frow", swap)
    own, row_tab = call(
        functools.partial(own_tables_kernel, rows_count, cols_count),
        (shape(side, 4 * HALF), shape(4, SG, 2 * side)), "own_tables", "ssv",
        scratch=[pltpu.VMEM((side, 4 * HALF), bf16)], cost=10**9,
    )(row_offsets, col_offsets, facet)
    vis_rows_count = 8 * 2 * n_vis // LANES
    parts = call(
        functools.partial(contributions_kernel, scale_in), (shape(2 * SG + vis_rows_count, HALF),) * chips,
        "contributions", "vvvv", scratch=[pltpu.VMEM((2 * side, 4 * HALF), bf16)], cost=2 * 10**9,
    )(own, vis, other, row_tab)
    parts = turned(parts)

    sums = call(first_sums_kernel, shape(5, SG, HALF, dtype=f32), "first_sums", "vv", cost=10**9)(*parts[:2])
    back_row, back_col = call(
        functools.partial(back_tables_kernel, rows_count, cols_count, side),
        (shape(side, 4 * SG), shape(4 * SG, side)), "back_tables", "ss", cost=10**9,
    )(row_offsets, col_offsets)
    pieces = call(
        gridding_kernel, shape(cols_count, 5 * each, HALF), "gridding", "v" * (chips - 1) + "a",
        scratch=[pltpu.VMEM((5, SG, HALF), f32)], cost=10**9,
    )(*parts[2:], sums, back_col)
    pieces = exchange(pieces, "fcol", None)
    pieces = call(pieces_sum_kernel, shape(cols_count, 5 * each, HALF), "pieces_sum", "v", cost=10**6)(pieces)
    pieces = exchange(pieces, "fcol", None)
    pieces_other = lax.ppermute(pieces, "frow", swap)

    kcos, ksin = grid_tables()
    block = [np.concatenate(pair, 1) for pair in ((kcos, ksin), (-ksin, kcos), (kcos, -ksin), (ksin, kcos))]
    forward_block = np.concatenate([block[0], block[1]], 0)
    inverse_block = np.concatenate([block[2], block[3]], 0)
    *back, rest = call(
        functools.partial(grids_kernel, chips), (shape(2 * SG + 16, HALF),) * chips + (shape(2 * SG, HALF),), "grids",
        "v" * (6 + chips),
        scratch=[
            pltpu.VMEM((5, SG, SG), f32), pltpu.VMEM((SG, 2 * SG), bf16), pltpu.VMEM((2 * SG, SG), bf16),
            pltpu.VMEM((SG, 2 * SG), bf16),
        ],
        cost=10**9,
    )(pieces, pieces_other, *parts, inverse_block, forward_block, forward_block, inverse_block)
    back = turned(back)

    def first_part(number, mine, other):
        kernel = functools.partial(first_part_kernel, number)
        return call(kernel, shape(side, 2 * SG, dtype=f32), "first_part", "vvv", cost=10**9)(mine, other, back_row)

    firsts = [first_part(chips, back[0], rest)]
    back[1], firsts[0] = lax.optimization_barrier((back[1], firsts[0]))
    rest = [lax.ppermute(block, "frow", swap) for block in back[1:]]
    firsts.append(first_part(chips - 1, back[1], rest[0]))
    return call(
        functools.partial(image_kernel, scale_out, chips),
        (shape(side, side, dtype=f32), shape(2, n_vis, dtype=f32)), "image", "v" * (chips + 7), outs="aa",
        scratch=[
            pltpu.VMEM((side, 4 * SG), bf16), pltpu.VMEM((side, side), f32), pltpu.VMEM((2, n_vis), f32),
            pltpu.SemaphoreType.DMA((5,)),
        ],
        cost=10**9,
    )(*back, *rest[1:], *firsts, back_row, back_col, observed)


def solution(mesh):
    in_specs = (
        P("frow", "fcol"),
        P(),
        P(),
        P(("frow", "fcol")),
        P(("frow", "fcol")),
        P(("frow", "fcol")),
        P(None, ("frow", "fcol")),
    )
    out_specs = (P("frow", "fcol"), P(None, ("frow", "fcol")))
    return jax.shard_map(shards, mesh=mesh, in_specs=in_specs, out_specs=out_specs, check_vma=False)
```

```python
import functools
import math

import jax
import jax.numpy as jnp
import ml_dtypes
import numpy as np
from jax import lax
from jax.experimental import pallas as pl
from jax.experimental.pallas import tpu as pltpu
from jax.sharding import PartitionSpec as P

SKY = 65536
SG = 256
NR = 2
NC = 2
HALF = SG // 2
LANES = 128


def wave(count):
    count = count & (SKY - 1)
    turned = count + SKY // 8
    near = (turned & (SKY // 4 - 1)) - SKY // 8
    quarter = lax.shift_right_logical(turned, 14) & 3
    t = near.astype(jnp.float32) * (2.0 * math.pi / SKY)
    q = t * t
    sin = t * (1.0 + q * (-1.0 / 6 + q * (1.0 / 120 + q * (-1.0 / 5040 + q * (1.0 / 362880)))))
    cos = 1.0 + q * (-0.5 + q * (1.0 / 24 + q * (-1.0 / 720 + q * (1.0 / 40320))))
    odd = (quarter & 1) == 1
    one, two = jnp.where(odd, sin, cos), jnp.where(odd, cos, sin)
    return (
        jnp.where((quarter == 1) | (quarter == 2), -one, one),
        jnp.where(quarter >= 2, -two, two),
    )


def lanes(n):
    return lax.broadcasted_iota(jnp.int32, (1, n), 1)


def sublanes(n):
    return lax.broadcasted_iota(jnp.int32, (n, 1), 0)


def spread(coarse, fine, store):
    for k in range(coarse[0].shape[0]):
        c, s = coarse[0][k:k + 1], coarse[1][k:k + 1]
        store(k * 16, c * fine[0] - s * fine[1], s * fine[0] + c * fine[1])


def place():
    return lax.axis_index("frow"), lax.axis_index("fcol")


def half_columns(cols_count, offsets, half, side, col_tab):
    bf16 = jnp.bfloat16
    col_index = place()[1]
    unit = sublanes(16)
    col_step = SKY // (cols_count * side)
    col_base = col_index * (SKY // cols_count)
    freq = [offsets[c] + half * HALF + lanes(HALF) for c in range(NC)]
    freq = jnp.concatenate(freq, 1)
    coarse = wave((col_base + 16 * col_step * sublanes(side // 16)) * freq)
    fine = wave((col_step * unit) * freq)

    def store(at, cos, sin):
        for c in range(NC):
            some = slice(c * HALF, (c + 1) * HALF)
            col_tab[at:at + 16, 2 * c * HALF:(2 * c + 1) * HALF] = cos[:, some].astype(bf16)
            col_tab[at:at + 16, (2 * c + 1) * HALF:(2 * c + 2) * HALF] = sin[:, some].astype(bf16)

    spread(coarse, fine, store)


def send_columns_kernel(cols_count, offsets, facet, subgrid, u, v, observed, send, vis, *scratch):
    col_tab, image, indices, seen, first, made, tail, sems = scratch
    f32, bf16 = jnp.float32, jnp.bfloat16
    side = facet.shape[0]
    pairs = [
        (offsets, first), (facet, image), (subgrid, indices.at[0]), (u, indices.at[1]), (v, indices.at[2]), (observed, seen),
    ]
    copies = [pltpu.make_async_copy(source, target, sems.at[n]) for n, (source, target) in enumerate(pairs)]
    for copy in copies:
        copy.start()
    copies[0].wait()
    half_columns(cols_count, first, 1 - place()[0] % 2, side, col_tab)
    for copy in copies[2:]:
        copy.wait()
    some = jnp.concatenate([indices[n].astype(f32) for n in range(3)] + [seen[...], jnp.zeros((3, side), f32)], 0)
    some = jnp.concatenate([some[:, :side // 2], some[:, side // 2:]], 0).astype(bf16)
    tail[:, :side // 2] = some
    tail[:, side // 2:] = some
    writes = [
        pltpu.make_async_copy(tail.at[:, pl.ds(0, side // 2)], vis, sems.at[6]),
        pltpu.make_async_copy(tail, send.at[pl.ds(side, 16)], sems.at[7]),
    ]
    for write in writes:
        write.start()
    copies[1].wait()
    step = side // 2
    for n in range(2):
        at = pl.ds(n * step, step)
        made[at] = jnp.dot(image[at], col_tab[...], preferred_element_type=f32).astype(bf16)
        write = pltpu.make_async_copy(made.at[at], send.at[at], sems.at[8 + n])
        write.start()
        writes.append(write)
    for write in writes:
        write.wait()


def own_tables_kernel(rows_count, cols_count, offsets, col_offsets, facet, own, row_tab, col_tab):
    bf16 = jnp.bfloat16
    row_index, _ = place()
    side = facet.shape[0]
    half_columns(cols_count, col_offsets, row_index % 2, side, col_tab)
    own[...] = jnp.dot(facet[...], col_tab[...], preferred_element_type=jnp.float32).astype(bf16)
    unit = sublanes(16)
    row_step = SKY // (rows_count * side)
    for f in range(2):
        pos = (row_index ^ f) * (SKY // rows_count) + row_step * lanes(side)
        fine = wave(unit * pos)
        for r in range(NR):
            coarse = wave((offsets[r] + 16 * unit) * pos)

            def store(at, cos, sin, r=r, f=f):
                row_tab[2 * r, at:at + 16, f * side:(f + 1) * side] = cos.astype(bf16)
                row_tab[2 * r + 1, at:at + 16, f * side:(f + 1) * side] = sin.astype(bf16)

            spread(coarse, fine, store)


def contributions_kernel(scale, own, own_vis, other, row_tab, *refs):
    f32, bf16 = jnp.float32, jnp.bfloat16
    outs, right = refs[:-1], refs[-1]
    chip = place()[0] // 2
    side = row_tab.shape[2] // 2
    vis = []
    right[:side] = own[...]
    right[side:] = other[:side]
    for some in (own_vis[...], other[side:]):
        vis += [some[:, k * LANES:(k + 1) * LANES] for k in range(side // 2 // LANES)]
    for n, out in enumerate(outs):
        for k, some in enumerate(vis):
            at = 2 * SG + 16 * k
            out[at:at + 16] = some
        r, c = split_number(chip + n)
        some = right[:, pl.ds(pl.multiple_of(c * SG, SG), SG)]
        with_cos = jnp.dot(row_tab[2 * r], some, preferred_element_type=f32)
        with_sin = jnp.dot(row_tab[2 * r + 1], some, preferred_element_type=f32)
        out[:SG] = ((with_cos[:, :HALF] - with_sin[:, HALF:]) * scale).astype(bf16)
        out[SG:2 * SG] = (-(with_cos[:, HALF:] + with_sin[:, :HALF]) * scale).astype(bf16)


def split_number(number):
    number = lax.rem(number, NR * NC)
    return number // NC, lax.rem(number, NC)


def vis_rows(block):
    count = block.shape[0] // 16
    return jnp.concatenate(
        [block[16 * k + 8 * part:16 * k + 8 * part + 8] for part in range(2) for k in range(count)], 1
    )


def grid_sums(parts):
    f32, bf16 = jnp.float32, jnp.bfloat16
    row_index, _ = place()
    chip = (row_index // 2).astype(f32)
    v_at = (sublanes(HALF) + (row_index % 2) * HALF).astype(f32)
    counter = sublanes(SG).astype(f32)
    total = jnp.zeros((SG, 3 * HALF), f32)
    planes = [jnp.zeros((SG, HALF), f32)] * 2
    for part in parts:
        one = vis_rows(part[2 * SG:].astype(f32))
        u_here = jnp.where(one[0:1] == chip, one[1:2], -1.0)
        hot = jnp.where(u_here == counter, 1.0, 0.0).astype(bf16)
        pick = one[2:3] == v_at
        right = jnp.concatenate(
            [jnp.where(pick, one[3:4], 0.0), jnp.where(pick, one[4:5], 0.0), jnp.where(pick, 1.0, 0.0)], 0
        ).astype(bf16)
        total = total + lax.dot_general(hot, right, (((1,), (1,)), ((), ())), preferred_element_type=f32)
        planes = [planes[p] + part[p * SG:(p + 1) * SG].astype(f32) for p in range(2)]
    return planes + [total[:, p * HALF:(p + 1) * HALF] for p in range(3)]


def first_sums_kernel(*refs):
    for p, plane in enumerate(grid_sums(refs[:-1])):
        refs[-1][p] = plane


def gridding_kernel(*refs):
    parts, (first, _, pieces, planes) = refs[:-4], refs[-4:]
    for p, plane in enumerate(grid_sums(parts)):
        planes[p] = first[p] + plane
    each = SG // pieces.shape[0]
    for j in range(pieces.shape[0]):
        rows = [planes[p, j * each:(j + 1) * each] for p in range(5)]
        pieces[j] = jnp.concatenate(rows, 0).astype(jnp.bfloat16)


def pieces_sum_kernel(pieces, out):
    f32, bf16 = jnp.float32, jnp.bfloat16
    total = pieces[0].astype(f32)
    for j in range(1, pieces.shape[0]):
        total = total + pieces[j].astype(f32)
    total = total.astype(bf16)
    for j in range(out.shape[0]):
        out[j] = total


def grids_kernel(chips, own, other, *refs):
    f32, bf16 = jnp.float32, jnp.bfloat16
    parts, (grid_left, forward, inverse_left, inverse) = refs[:chips], refs[chips:chips + 4]
    outs, rest, (planes, cat, tall, hat) = refs[chips + 4:-5], refs[-5], refs[-4:]
    row_index, _ = place()
    core = row_index % 2
    chip = (row_index // 2).astype(f32)
    count = own.shape[0]
    each = SG // count
    for pieces, half in ((own, core), (other, 1 - core)):
        at = pl.ds(pl.multiple_of(half * HALF, HALF), HALF)
        for j in range(count):
            some = pieces[j].astype(f32)
            for p in range(5):
                planes[p, j * each:(j + 1) * each, at] = some[p * each:(p + 1) * each]
    cat[:, :SG] = planes[0].astype(bf16)
    cat[:, SG:] = planes[1].astype(bf16)
    wide = jnp.dot(cat[...], forward[...], preferred_element_type=f32).astype(bf16)
    tall[:SG] = wide[:, :SG]
    tall[SG:] = wide[:, SG:]
    model = jnp.dot(grid_left[...], tall[...], preferred_element_type=f32) * (1.0 / SG)
    hat_real, hat_imag = model[:SG], model[SG:]
    cat[:, :SG] = (planes[2] - planes[4] * hat_real).astype(bf16)
    cat[:, SG:] = (planes[3] - planes[4] * hat_imag).astype(bf16)
    hat[:, :SG] = hat_real.astype(bf16)
    hat[:, SG:] = hat_imag.astype(bf16)
    wide = jnp.dot(cat[...], inverse[...], preferred_element_type=f32)
    for k in range(2):
        tall[k * SG:(k + 1) * SG] = wide[:, k * SG:(k + 1) * SG].astype(bf16)
    back = jnp.dot(inverse_left[...], tall[...], preferred_element_type=f32) * (1.0 / SG)
    rest[...] = jnp.where(core == 0, back[:, HALF:], back[:, :HALF]).astype(bf16)
    back = jnp.where(core == 0, back[:, :HALF], back[:, HALF:]).astype(bf16)
    counter = sublanes(SG).astype(f32)
    vis_each = (parts[0].shape[0] - 2 * SG) // 2
    for k, out in enumerate(outs):
        out[:2 * SG] = back
        ask = vis_rows(parts[-k % chips][2 * SG:2 * SG + vis_each].astype(f32))
        u_here = jnp.where(ask[0:1] == chip, ask[1:2], -1.0)
        hot = jnp.where(u_here == counter, 1.0, 0.0).astype(bf16)
        pick = ask[2:3] == counter
        line = lax.dot_general(hat[...], hot, (((0,), (0,)), ((), ())), preferred_element_type=f32)
        rows = []
        for part in range(2):
            value = jnp.sum(jnp.where(pick, line[part * SG:(part + 1) * SG], 0.0), axis=0, keepdims=True)
            rows += [value[:, i * LANES:(i + 1) * LANES] for i in range(value.shape[1] // LANES)]
        rows.append(jnp.zeros((16 - len(rows), LANES), f32))
        out[2 * SG:] = jnp.concatenate(rows, 0).astype(bf16)


def back_tables_kernel(rows_count, cols_count, side, offsets_row, offsets_col, row_tab, col_tab):
    bf16 = jnp.bfloat16
    row_index, col_index = place()
    unit = sublanes(16)
    row_step = SKY // (rows_count * side)
    row_base = row_index * (SKY // rows_count)
    for r in range(NR):
        freq = offsets_row[r] + lanes(SG)
        coarse = wave((row_base + 16 * row_step * sublanes(side // 16)) * freq)
        fine = wave((row_step * unit) * freq)

        def store(at, cos, sin, r=r):
            row_tab[at:at + 16, 2 * r * SG:(2 * r + 1) * SG] = cos.astype(bf16)
            row_tab[at:at + 16, (2 * r + 1) * SG:(2 * r + 2) * SG] = sin.astype(bf16)

        spread(coarse, fine, store)
    col_step = SKY // (cols_count * side)
    pos = col_index * (SKY // cols_count) + col_step * lanes(side)
    fine = wave(unit * pos)
    for c in range(NC):
        coarse = wave((offsets_col[c] + 16 * unit) * pos)

        def store(at, cos, sin, c=c):
            left = (2 * c + at // HALF) * 2 * HALF + at % HALF
            col_tab[left:left + 16] = cos.astype(bf16)
            col_tab[left + HALF:left + HALF + 16] = (-sin).astype(bf16)

        spread(coarse, fine, store)


def block_part(block, number, row_tab):
    r, _ = split_number(number)
    real, imag = block[:SG], block[SG:2 * SG]
    right = jnp.concatenate([jnp.concatenate([real, imag], 1), jnp.concatenate([-imag, real], 1)], 0)
    left = row_tab[:, pl.ds(pl.multiple_of(2 * r * SG, 2 * SG), 2 * SG)]
    return jnp.dot(left, right, preferred_element_type=jnp.float32)


def first_part_kernel(own, rest, row_tab, out):
    chip = place()[0] // 2
    for n, block in enumerate((own, rest)):
        out[:, n * SG:(n + 1) * SG] = block_part(block, chip, row_tab)


def column_rows(number):
    depth = 2 * SG
    return pl.ds(pl.multiple_of(split_number(number)[1] * depth, depth), depth)


def half_lanes(n):
    half = place()[0] % 2
    return pl.ds(pl.multiple_of((half if n == 0 else 1 - half) * SG, SG), SG)


def own_column_kernel(chips, opposite, own, rest, first, row_tab, col_tab, out, both):
    chip = place()[0] // 2
    for n, block in enumerate((own, rest)):
        part = first[:, n * SG:(n + 1) * SG] + block_part(block, chip + chips - opposite, row_tab)
        both[:, half_lanes(n)] = part.astype(jnp.bfloat16)
    out[...] = jnp.dot(both[...], col_tab[column_rows(chip)], preferred_element_type=jnp.float32)


def image_kernel(scale, chips, *refs):
    f32, bf16 = jnp.float32, jnp.bfloat16
    blocks, others, refs = refs[:chips], refs[chips:chips + 2], refs[chips + 2:]
    first, row_tab, col_tab, observed, out, residual, both, image, seen, sems = refs
    chip = place()[0] // 2
    model = jnp.zeros((16, LANES), f32)
    for block in blocks:
        model = model + block[2 * SG:].astype(f32)
    count = observed.shape[1] // LANES
    for part in range(2):
        for i in range(count):
            at = slice(i * LANES, (i + 1) * LANES)
            seen[part:part + 1, at] = observed[part:part + 1, at] - model[part * count + i:part * count + i + 1]
    writes = [pltpu.make_async_copy(seen, residual, sems.at[0])]
    writes[0].start()
    for n, pair in enumerate(((blocks[1], blocks[3]), others)):
        part = block_part(pair[0], chip + chips - 1, row_tab) + block_part(pair[1], chip + chips - 3, row_tab)
        both[:, half_lanes(n)] = part.astype(bf16)
    chunks = sems.shape[0] - 1
    step = image.shape[0] // chunks
    for n in range(chunks):
        at = slice(n * step, (n + 1) * step)
        part = jnp.dot(both[at], col_tab[column_rows(chip + 1)], preferred_element_type=f32)
        image[at] = (first[at] + part) * scale
        write = pltpu.make_async_copy(image.at[at], out.at[at], sems.at[1 + n])
        write.start()
        writes.append(write)
    for write in writes:
        write.wait()


def call(kernel, out_shape, name, spaces, scratch=(), cost=0, outs=None, room=24):
    kinds = {"s": pltpu.SMEM, "v": pltpu.VMEM, "a": pl.ANY}
    several = isinstance(out_shape, tuple)
    outs = outs or "v" * (len(out_shape) if several else 1)
    out_specs = tuple(pl.BlockSpec(memory_space=kinds[kind]) for kind in outs)
    return pl.pallas_call(
        kernel,
        out_shape=out_shape,
        in_specs=[pl.BlockSpec(memory_space=kinds[kind]) for kind in spaces],
        out_specs=out_specs if several else out_specs[0],
        scratch_shapes=list(scratch),
        compiler_params=pltpu.CompilerParams(vmem_limit_bytes=room * 2**20),
        cost_estimate=pl.CostEstimate(flops=cost, bytes_accessed=2**20, transcendentals=0),
        name=name,
    )


def grid_tables():
    counter = np.arange(SG)
    angles = (counter[:, None] * counter[None, :] % SG).astype(np.float64) * (2.0 * math.pi / SG)
    return np.cos(angles).astype(ml_dtypes.bfloat16), np.sin(angles).astype(ml_dtypes.bfloat16)


def exchange(blocks, axes, groups):
    return lax.all_to_all(blocks, axes, 0, 0, tiled=True, axis_index_groups=groups)


def shape(*dims, dtype=jnp.bfloat16):
    return jax.ShapeDtypeStruct(dims, dtype)


def shards(facet, row_offsets, col_offsets, vis_subgrid, vis_u, vis_v, observed):
    f32, bf16 = jnp.float32, jnp.bfloat16
    rows_count, cols_count = lax.axis_size("frow"), lax.axis_size("fcol")
    side = facet.shape[0]
    n_vis = vis_u.shape[0]
    chips = rows_count // 2
    each = SG // cols_count
    swap = [(index, index ^ 1) for index in range(rows_count)]
    turns = [[(index, (index + 2 * k) % rows_count) for index in range(rows_count)] for k in range(chips)]

    def turned(blocks):
        moved = {k: lax.ppermute(blocks[k], "frow", turns[k]) for k in (2, 1, 3)}
        return [blocks[0]] + [moved[k] for k in range(1, chips)]

    scale_in = 1.0 / (side * math.sqrt(rows_count * cols_count))
    scale_out = 1.0 / (SG * math.sqrt(NR * NC))
    line = (1, n_vis)

    send, vis = call(
        functools.partial(send_columns_kernel, cols_count), (shape(side + 16, 4 * HALF), shape(16, n_vis // 2)),
        "send_columns", "aaaaaa",
        scratch=[
            pltpu.VMEM((side, 4 * HALF), bf16), pltpu.VMEM((side, side), bf16), pltpu.VMEM((3,) + line, jnp.int32),
            pltpu.VMEM((2, n_vis), f32), pltpu.SMEM((NC,), jnp.int32), pltpu.VMEM((side, 4 * HALF), bf16),
            pltpu.VMEM((16, n_vis), bf16), pltpu.SemaphoreType.DMA((10,)),
        ],
        cost=10**9, room=60, outs="aa",
    )(col_offsets, facet, vis_subgrid.reshape(line), vis_u.reshape(line), vis_v.reshape(line), observed)
    other = lax.ppermute(send, "frow", swap)
    own, row_tab = call(
        functools.partial(own_tables_kernel, rows_count, cols_count),
        (shape(side, 4 * HALF), shape(4, SG, 2 * side)), "own_tables", "ssv",
        scratch=[pltpu.VMEM((side, 4 * HALF), bf16)], cost=10**9,
    )(row_offsets, col_offsets, facet)
    vis_rows_count = 8 * 2 * n_vis // LANES
    parts = call(
        functools.partial(contributions_kernel, scale_in), (shape(2 * SG + vis_rows_count, HALF),) * chips,
        "contributions", "vvvv", scratch=[pltpu.VMEM((2 * side, 4 * HALF), bf16)], cost=2 * 10**9,
    )(own, vis, other, row_tab)
    parts = turned(parts)

    sums = call(first_sums_kernel, shape(5, SG, HALF, dtype=f32), "first_sums", "vv", cost=10**9)(parts[0], parts[2])
    back_row, back_col = call(
        functools.partial(back_tables_kernel, rows_count, cols_count, side),
        (shape(side, 4 * SG), shape(4 * SG, side)), "back_tables", "ss", cost=10**9,
    )(row_offsets, col_offsets)
    pieces = call(
        gridding_kernel, shape(cols_count, 5 * each, HALF), "gridding", "v" * (chips - 1) + "a",
        scratch=[pltpu.VMEM((5, SG, HALF), f32)], cost=10**9,
    )(parts[1], parts[3], sums, back_col)
    pieces = exchange(pieces, "fcol", None)
    pieces = call(pieces_sum_kernel, shape(cols_count, 5 * each, HALF), "pieces_sum", "v", cost=10**6)(pieces)
    pieces = exchange(pieces, "fcol", None)
    pieces_other = lax.ppermute(pieces, "frow", swap)

    kcos, ksin = grid_tables()
    block = [np.concatenate(pair, 1) for pair in ((kcos, ksin), (-ksin, kcos), (kcos, -ksin), (ksin, kcos))]
    forward_block = np.concatenate([block[0], block[1]], 0)
    inverse_block = np.concatenate([block[2], block[3]], 0)
    *back, rest = call(
        functools.partial(grids_kernel, chips), (shape(2 * SG + 16, HALF),) * chips + (shape(2 * SG, HALF),), "grids",
        "v" * (6 + chips),
        scratch=[
            pltpu.VMEM((5, SG, SG), f32), pltpu.VMEM((SG, 2 * SG), bf16), pltpu.VMEM((2 * SG, SG), bf16),
            pltpu.VMEM((SG, 2 * SG), bf16),
        ],
        cost=10**9,
    )(pieces, pieces_other, *parts, inverse_block, forward_block, forward_block, inverse_block)
    back = turned(back)

    both = pltpu.VMEM((side, 2 * SG), bf16)
    square = shape(side, side, dtype=f32)
    first = call(first_part_kernel, square, "first_part", "vvv", cost=10**9)(back[0], rest, back_row)
    back[2], first = lax.optimization_barrier((back[2], first))
    rest = {k: lax.ppermute(back[k], "frow", swap) for k in (2, 1, 3)}
    first = call(
        functools.partial(own_column_kernel, chips, 2), square, "own_column", "v" * 5, scratch=[both], cost=10**9
    )(back[2], rest[2], first, back_row, back_col)
    return call(
        functools.partial(image_kernel, scale_out, chips), (square, shape(2, n_vis, dtype=f32)), "image",
        "v" * (chips + 6), outs="aa",
        scratch=[both, pltpu.VMEM((side, side), f32), pltpu.VMEM((2, n_vis), f32), pltpu.SemaphoreType.DMA((5,))],
        cost=10**9,
    )(*back, rest[1], rest[3], first, back_row, back_col, observed)


def solution(mesh):
    in_specs = (
        P("frow", "fcol"),
        P(),
        P(),
        P(("frow", "fcol")),
        P(("frow", "fcol")),
        P(("frow", "fcol")),
        P(None, ("frow", "fcol")),
    )
    out_specs = (P("frow", "fcol"), P(None, ("frow", "fcol")))
    return jax.shard_map(shards, mesh=mesh, in_specs=in_specs, out_specs=out_specs, check_vma=False)
```

```python
import functools
import math

import jax
import jax.numpy as jnp
import ml_dtypes
import numpy as np
from jax import lax
from jax.experimental import pallas as pl
from jax.experimental.pallas import tpu as pltpu
from jax.sharding import PartitionSpec as P

SKY = 65536
SG = 256
NR = 2
NC = 2
HALF = SG // 2
LANES = 128


def wave(count):
    count = count & (SKY - 1)
    turned = count + SKY // 8
    near = (turned & (SKY // 4 - 1)) - SKY // 8
    quarter = lax.shift_right_logical(turned, 14) & 3
    t = near.astype(jnp.float32) * (2.0 * math.pi / SKY)
    q = t * t
    sin = t * (1.0 + q * (-1.0 / 6 + q * (1.0 / 120 + q * (-1.0 / 5040 + q * (1.0 / 362880)))))
    cos = 1.0 + q * (-0.5 + q * (1.0 / 24 + q * (-1.0 / 720 + q * (1.0 / 40320))))
    odd = (quarter & 1) == 1
    one, two = jnp.where(odd, sin, cos), jnp.where(odd, cos, sin)
    return (
        jnp.where((quarter == 1) | (quarter == 2), -one, one),
        jnp.where(quarter >= 2, -two, two),
    )


def lanes(n):
    return lax.broadcasted_iota(jnp.int32, (1, n), 1)


def sublanes(n):
    return lax.broadcasted_iota(jnp.int32, (n, 1), 0)


def spread(coarse, fine, store):
    for k in range(coarse[0].shape[0]):
        c, s = coarse[0][k:k + 1], coarse[1][k:k + 1]
        store(k * 16, c * fine[0] - s * fine[1], s * fine[0] + c * fine[1])


def place():
    return lax.axis_index("frow"), lax.axis_index("fcol")


def half_columns(cols_count, offsets, half, side, col_tab):
    bf16 = jnp.bfloat16
    col_index = place()[1]
    unit = sublanes(16)
    col_step = SKY // (cols_count * side)
    col_base = col_index * (SKY // cols_count)
    freq = [offsets[c] + half * HALF + lanes(HALF) for c in range(NC)]
    freq = jnp.concatenate(freq, 1)
    coarse = wave((col_base + 16 * col_step * sublanes(side // 16)) * freq)
    fine = wave((col_step * unit) * freq)

    def store(at, cos, sin):
        for c in range(NC):
            some = slice(c * HALF, (c + 1) * HALF)
            col_tab[at:at + 16, 2 * c * HALF:(2 * c + 1) * HALF] = cos[:, some].astype(bf16)
            col_tab[at:at + 16, (2 * c + 1) * HALF:(2 * c + 2) * HALF] = sin[:, some].astype(bf16)

    spread(coarse, fine, store)


def send_columns_kernel(cols_count, offsets, facet, subgrid, u, v, observed, send, vis, *scratch):
    col_tab, image, indices, seen, first, made, tail, sems = scratch
    f32, bf16 = jnp.float32, jnp.bfloat16
    side = facet.shape[0]
    pairs = [
        (offsets, first), (facet, image), (subgrid, indices.at[0]), (u, indices.at[1]), (v, indices.at[2]), (observed, seen),
    ]
    copies = [pltpu.make_async_copy(source, target, sems.at[n]) for n, (source, target) in enumerate(pairs)]
    for copy in copies:
        copy.start()
    copies[0].wait()
    half_columns(cols_count, first, 1 - place()[0] % 2, side, col_tab)
    for copy in copies[2:]:
        copy.wait()
    some = jnp.concatenate([indices[n].astype(f32) for n in range(3)] + [seen[...], jnp.zeros((3, side), f32)], 0)
    some = jnp.concatenate([some[:, :side // 2], some[:, side // 2:]], 0).astype(bf16)
    tail[:, :side // 2] = some
    tail[:, side // 2:] = some
    writes = [
        pltpu.make_async_copy(tail.at[:, pl.ds(0, side // 2)], vis, sems.at[6]),
        pltpu.make_async_copy(tail, send.at[pl.ds(side, 16)], sems.at[7]),
    ]
    for write in writes:
        write.start()
    copies[1].wait()
    step = side // 2
    for n in range(2):
        at = pl.ds(n * step, step)
        made[at] = jnp.dot(image[at], col_tab[...], preferred_element_type=f32).astype(bf16)
        write = pltpu.make_async_copy(made.at[at], send.at[at], sems.at[8 + n])
        write.start()
        writes.append(write)
    for write in writes:
        write.wait()


def own_tables_kernel(rows_count, cols_count, offsets, col_offsets, facet, own, row_tab, col_tab):
    bf16 = jnp.bfloat16
    row_index, _ = place()
    side = facet.shape[0]
    half_columns(cols_count, col_offsets, row_index % 2, side, col_tab)
    own[...] = jnp.dot(facet[...], col_tab[...], preferred_element_type=jnp.float32).astype(bf16)
    unit = sublanes(16)
    row_step = SKY // (rows_count * side)
    for f in range(2):
        pos = (row_index ^ f) * (SKY // rows_count) + row_step * lanes(side)
        fine = wave(unit * pos)
        for r in range(NR):
            coarse = wave((offsets[r] + 16 * unit) * pos)

            def store(at, cos, sin, r=r, f=f):
                row_tab[2 * r, at:at + 16, f * side:(f + 1) * side] = cos.astype(bf16)
                row_tab[2 * r + 1, at:at + 16, f * side:(f + 1) * side] = sin.astype(bf16)

            spread(coarse, fine, store)


def contribution_kernel(scale, number, own, own_vis, other, row_tab, out):
    f32, bf16 = jnp.float32, jnp.bfloat16
    side = own.shape[0]
    vis = []
    for some in (own_vis[...], other[side:]):
        vis += [some[:, k * LANES:(k + 1) * LANES] for k in range(side // 2 // LANES)]
    for k, some in enumerate(vis):
        at = 2 * SG + 16 * k
        out[at:at + 16] = some
    r, c = split_number(place()[0] // 2 + number)
    at = pl.ds(pl.multiple_of(c * SG, SG), SG)
    right = jnp.concatenate([own[:, at], other[:side, at]], 0)
    with_cos = jnp.dot(row_tab[2 * r], right, preferred_element_type=f32)
    with_sin = jnp.dot(row_tab[2 * r + 1], right, preferred_element_type=f32)
    out[:SG] = ((with_cos[:, :HALF] - with_sin[:, HALF:]) * scale).astype(bf16)
    out[SG:2 * SG] = (-(with_cos[:, HALF:] + with_sin[:, :HALF]) * scale).astype(bf16)


def split_number(number):
    number = lax.rem(number, NR * NC)
    return number // NC, lax.rem(number, NC)


def vis_rows(block):
    count = block.shape[0] // 16
    return jnp.concatenate(
        [block[16 * k + 8 * part:16 * k + 8 * part + 8] for part in range(2) for k in range(count)], 1
    )


def grid_sums(parts):
    f32, bf16 = jnp.float32, jnp.bfloat16
    row_index, _ = place()
    chip = (row_index // 2).astype(f32)
    v_at = (sublanes(HALF) + (row_index % 2) * HALF).astype(f32)
    counter = sublanes(SG).astype(f32)
    total = jnp.zeros((SG, 3 * HALF), f32)
    planes = [jnp.zeros((SG, HALF), f32)] * 2
    for part in parts:
        one = vis_rows(part[2 * SG:].astype(f32))
        u_here = jnp.where(one[0:1] == chip, one[1:2], -1.0)
        hot = jnp.where(u_here == counter, 1.0, 0.0).astype(bf16)
        pick = one[2:3] == v_at
        right = jnp.concatenate(
            [jnp.where(pick, one[3:4], 0.0), jnp.where(pick, one[4:5], 0.0), jnp.where(pick, 1.0, 0.0)], 0
        ).astype(bf16)
        total = total + lax.dot_general(hot, right, (((1,), (1,)), ((), ())), preferred_element_type=f32)
        planes = [planes[p] + part[p * SG:(p + 1) * SG].astype(f32) for p in range(2)]
    return planes + [total[:, p * HALF:(p + 1) * HALF] for p in range(3)]


def first_sums_kernel(*refs):
    for p, plane in enumerate(grid_sums(refs[:-1])):
        refs[-1][p] = plane


def gridding_kernel(*refs):
    parts, (first, _, pieces, planes) = refs[:-4], refs[-4:]
    for p, plane in enumerate(grid_sums(parts)):
        planes[p] = first[p] + plane
    each = SG // pieces.shape[0]
    for j in range(pieces.shape[0]):
        rows = [planes[p, j * each:(j + 1) * each] for p in range(5)]
        pieces[j] = jnp.concatenate(rows, 0).astype(jnp.bfloat16)


def pieces_sum_kernel(pieces, out):
    f32, bf16 = jnp.float32, jnp.bfloat16
    total = pieces[0].astype(f32)
    for j in range(1, pieces.shape[0]):
        total = total + pieces[j].astype(f32)
    total = total.astype(bf16)
    for j in range(out.shape[0]):
        out[j] = total


def lay_out(pieces, half, planes, lanes_at):
    f32, bf16 = jnp.float32, jnp.bfloat16
    each = SG // pieces.shape[0]
    for j in range(pieces.shape[0]):
        some = pieces[j].astype(f32)
        for p in range(5):
            planes[p, j * each:(j + 1) * each, lanes_at] = some[p * each:(p + 1) * each]

    def step(forward):
        rows = [pl.ds(pl.multiple_of(p * SG + half * HALF, HALF), HALF) for p in range(2)]
        left = jnp.concatenate([planes[p, :, lanes_at].astype(bf16) for p in range(2)], 1)
        right = jnp.concatenate([forward[at] for at in rows], 0)
        return jnp.dot(left, right, preferred_element_type=f32)

    return step


def own_half_kernel(pieces, forward, out, wide, planes):
    wide[...] = lay_out(pieces, place()[0] % 2, planes, slice(0, HALF))(forward)
    out[...] = planes[2:]


def grids_kernel(chips, own, own_wide, other, *refs):
    f32, bf16 = jnp.float32, jnp.bfloat16
    parts, (grid_left, forward, inverse_left, inverse) = refs[:chips], refs[chips:chips + 4]
    outs, rest, (planes, cat, tall, hat) = refs[chips + 4:-5], refs[-5], refs[-4:]
    row_index, _ = place()
    core = row_index % 2
    chip = (row_index // 2).astype(f32)
    at = [pl.ds(pl.multiple_of(half * HALF, HALF), HALF) for half in (core, 1 - core)]
    wide = (own_wide[...] + lay_out(other, 1 - core, planes, at[1])(forward)).astype(bf16)
    for p in range(3):
        planes[2 + p, :, at[0]] = own[p]
    tall[:SG] = wide[:, :SG]
    tall[SG:] = wide[:, SG:]
    model = jnp.dot(grid_left[...], tall[...], preferred_element_type=f32) * (1.0 / SG)
    hat_real, hat_imag = model[:SG], model[SG:]
    cat[:, :SG] = (planes[2] - planes[4] * hat_real).astype(bf16)
    cat[:, SG:] = (planes[3] - planes[4] * hat_imag).astype(bf16)
    hat[:, :SG] = hat_real.astype(bf16)
    hat[:, SG:] = hat_imag.astype(bf16)
    wide = jnp.dot(cat[...], inverse[...], preferred_element_type=f32)
    for k in range(2):
        tall[k * SG:(k + 1) * SG] = wide[:, k * SG:(k + 1) * SG].astype(bf16)
    back = jnp.dot(inverse_left[...], tall[...], preferred_element_type=f32) * (1.0 / SG)
    rest[...] = jnp.where(core == 0, back[:, HALF:], back[:, :HALF]).astype(bf16)
    back = jnp.where(core == 0, back[:, :HALF], back[:, HALF:]).astype(bf16)
    counter = sublanes(SG).astype(f32)
    vis_each = (parts[0].shape[0] - 2 * SG) // 2
    for k, out in enumerate(outs):
        out[:2 * SG] = back
        ask = vis_rows(parts[-k % chips][2 * SG:2 * SG + vis_each].astype(f32))
        u_here = jnp.where(ask[0:1] == chip, ask[1:2], -1.0)
        hot = jnp.where(u_here == counter, 1.0, 0.0).astype(bf16)
        pick = ask[2:3] == counter
        line = lax.dot_general(hat[...], hot, (((0,), (0,)), ((), ())), preferred_element_type=f32)
        rows = []
        for part in range(2):
            value = jnp.sum(jnp.where(pick, line[part * SG:(part + 1) * SG], 0.0), axis=0, keepdims=True)
            rows += [value[:, i * LANES:(i + 1) * LANES] for i in range(value.shape[1] // LANES)]
        rows.append(jnp.zeros((16 - len(rows), LANES), f32))
        out[2 * SG:] = jnp.concatenate(rows, 0).astype(bf16)


def back_tables_kernel(rows_count, cols_count, side, offsets_row, offsets_col, row_tab, col_tab):
    bf16 = jnp.bfloat16
    row_index, col_index = place()
    unit = sublanes(16)
    row_step = SKY // (rows_count * side)
    row_base = row_index * (SKY // rows_count)
    for r in range(NR):
        freq = offsets_row[r] + lanes(SG)
        coarse = wave((row_base + 16 * row_step * sublanes(side // 16)) * freq)
        fine = wave((row_step * unit) * freq)

        def store(at, cos, sin, r=r):
            row_tab[at:at + 16, 2 * r * SG:(2 * r + 1) * SG] = cos.astype(bf16)
            row_tab[at:at + 16, (2 * r + 1) * SG:(2 * r + 2) * SG] = sin.astype(bf16)

        spread(coarse, fine, store)
    col_step = SKY // (cols_count * side)
    pos = col_index * (SKY // cols_count) + col_step * lanes(side)
    fine = wave(unit * pos)
    for c in range(NC):
        coarse = wave((offsets_col[c] + 16 * unit) * pos)

        def store(at, cos, sin, c=c):
            left = (2 * c + at // HALF) * 2 * HALF + at % HALF
            col_tab[left:left + 16] = cos.astype(bf16)
            col_tab[left + HALF:left + HALF + 16] = (-sin).astype(bf16)

        spread(coarse, fine, store)


def block_part(block, number, row_tab):
    r, _ = split_number(number)
    real, imag = block[:SG], block[SG:2 * SG]
    right = jnp.concatenate([jnp.concatenate([real, imag], 1), jnp.concatenate([-imag, real], 1)], 0)
    left = row_tab[:, pl.ds(pl.multiple_of(2 * r * SG, 2 * SG), 2 * SG)]
    return jnp.dot(left, right, preferred_element_type=jnp.float32)


def first_part_kernel(own, rest, row_tab, out):
    chip = place()[0] // 2
    for n, block in enumerate((own, rest)):
        out[:, n * SG:(n + 1) * SG] = block_part(block, chip, row_tab)


def column_rows(number):
    depth = 2 * SG
    return pl.ds(pl.multiple_of(split_number(number)[1] * depth, depth), depth)


def half_lanes(n):
    half = place()[0] % 2
    return pl.ds(pl.multiple_of((half if n == 0 else 1 - half) * SG, SG), SG)


def own_column_kernel(chips, opposite, own, rest, first, row_tab, col_tab, out, both):
    chip = place()[0] // 2
    for n, block in enumerate((own, rest)):
        part = first[:, n * SG:(n + 1) * SG] + block_part(block, chip + chips - opposite, row_tab)
        both[:, half_lanes(n)] = part.astype(jnp.bfloat16)
    out[...] = jnp.dot(both[...], col_tab[column_rows(chip)], preferred_element_type=jnp.float32)


def image_kernel(scale, chips, *refs):
    f32, bf16 = jnp.float32, jnp.bfloat16
    blocks, others, refs = refs[:chips], refs[chips:chips + 2], refs[chips + 2:]
    first, row_tab, col_tab, observed, out, residual, both, image, seen, sems = refs
    chip = place()[0] // 2
    model = jnp.zeros((16, LANES), f32)
    for block in blocks:
        model = model + block[2 * SG:].astype(f32)
    count = observed.shape[1] // LANES
    for part in range(2):
        for i in range(count):
            at = slice(i * LANES, (i + 1) * LANES)
            seen[part:part + 1, at] = observed[part:part + 1, at] - model[part * count + i:part * count + i + 1]
    writes = [pltpu.make_async_copy(seen, residual, sems.at[0])]
    writes[0].start()
    for n, pair in enumerate(((blocks[1], blocks[3]), others)):
        part = block_part(pair[0], chip + chips - 1, row_tab) + block_part(pair[1], chip + chips - 3, row_tab)
        both[:, half_lanes(n)] = part.astype(bf16)
    chunks = sems.shape[0] - 1
    step = image.shape[0] // chunks
    for n in range(chunks):
        at = slice(n * step, (n + 1) * step)
        part = jnp.dot(both[at], col_tab[column_rows(chip + 1)], preferred_element_type=f32)
        image[at] = (first[at] + part) * scale
        write = pltpu.make_async_copy(image.at[at], out.at[at], sems.at[1 + n])
        write.start()
        writes.append(write)
    for write in writes:
        write.wait()


def call(kernel, out_shape, name, spaces, scratch=(), cost=0, outs=None, room=24):
    kinds = {"s": pltpu.SMEM, "v": pltpu.VMEM, "a": pl.ANY}
    several = isinstance(out_shape, tuple)
    outs = outs or "v" * (len(out_shape) if several else 1)
    out_specs = tuple(pl.BlockSpec(memory_space=kinds[kind]) for kind in outs)
    return pl.pallas_call(
        kernel,
        out_shape=out_shape,
        in_specs=[pl.BlockSpec(memory_space=kinds[kind]) for kind in spaces],
        out_specs=out_specs if several else out_specs[0],
        scratch_shapes=list(scratch),
        compiler_params=pltpu.CompilerParams(vmem_limit_bytes=room * 2**20),
        cost_estimate=pl.CostEstimate(flops=cost, bytes_accessed=2**20, transcendentals=0),
        name=name,
    )


def grid_tables():
    counter = np.arange(SG)
    angles = (counter[:, None] * counter[None, :] % SG).astype(np.float64) * (2.0 * math.pi / SG)
    return np.cos(angles).astype(ml_dtypes.bfloat16), np.sin(angles).astype(ml_dtypes.bfloat16)


def exchange(blocks, axes, groups):
    return lax.all_to_all(blocks, axes, 0, 0, tiled=True, axis_index_groups=groups)


def shape(*dims, dtype=jnp.bfloat16):
    return jax.ShapeDtypeStruct(dims, dtype)


def shards(facet, row_offsets, col_offsets, vis_subgrid, vis_u, vis_v, observed):
    f32, bf16 = jnp.float32, jnp.bfloat16
    rows_count, cols_count = lax.axis_size("frow"), lax.axis_size("fcol")
    side = facet.shape[0]
    n_vis = vis_u.shape[0]
    chips = rows_count // 2
    each = SG // cols_count
    swap = [(index, index ^ 1) for index in range(rows_count)]
    turns = [[(index, (index + 2 * k) % rows_count) for index in range(rows_count)] for k in range(chips)]

    def turned(blocks):
        moved = {k: lax.ppermute(blocks[k], "frow", turns[k]) for k in (2, 1, 3)}
        return [blocks[0]] + [moved[k] for k in range(1, chips)]

    scale_in = 1.0 / (side * math.sqrt(rows_count * cols_count))
    scale_out = 1.0 / (SG * math.sqrt(NR * NC))
    line = (1, n_vis)

    send, vis = call(
        functools.partial(send_columns_kernel, cols_count), (shape(side + 16, 4 * HALF), shape(16, n_vis // 2)),
        "send_columns", "aaaaaa",
        scratch=[
            pltpu.VMEM((side, 4 * HALF), bf16), pltpu.VMEM((side, side), bf16), pltpu.VMEM((3,) + line, jnp.int32),
            pltpu.VMEM((2, n_vis), f32), pltpu.SMEM((NC,), jnp.int32), pltpu.VMEM((side, 4 * HALF), bf16),
            pltpu.VMEM((16, n_vis), bf16), pltpu.SemaphoreType.DMA((10,)),
        ],
        cost=10**9, room=60, outs="aa",
    )(col_offsets, facet, vis_subgrid.reshape(line), vis_u.reshape(line), vis_v.reshape(line), observed)
    other = lax.ppermute(send, "frow", swap)
    own, row_tab = call(
        functools.partial(own_tables_kernel, rows_count, cols_count),
        (shape(side, 4 * HALF), shape(4, SG, 2 * side)), "own_tables", "ssv",
        scratch=[pltpu.VMEM((side, 4 * HALF), bf16)], cost=10**9,
    )(row_offsets, col_offsets, facet)
    vis_rows_count = 8 * 2 * n_vis // LANES
    parts = {}
    for k in (2, 1, 3, 0):
        parts[k] = call(
            functools.partial(contribution_kernel, scale_in, k), shape(2 * SG + vis_rows_count, HALF), "contribution",
            "vvvv", cost=5 * 10**8,
        )(own, vis, other, row_tab)
        own, parts[k] = lax.optimization_barrier((own, parts[k]))
    parts = turned(parts)

    sums = call(first_sums_kernel, shape(5, SG, HALF, dtype=f32), "first_sums", "vv", cost=10**9)(parts[0], parts[2])
    back_row, back_col = call(
        functools.partial(back_tables_kernel, rows_count, cols_count, side),
        (shape(side, 4 * SG), shape(4 * SG, side)), "back_tables", "ss", cost=10**9,
    )(row_offsets, col_offsets)
    pieces = call(
        gridding_kernel, shape(cols_count, 5 * each, HALF), "gridding", "v" * (chips - 1) + "a",
        scratch=[pltpu.VMEM((5, SG, HALF), f32)], cost=10**9,
    )(parts[1], parts[3], sums, back_col)
    pieces = exchange(pieces, "fcol", None)
    pieces = call(pieces_sum_kernel, shape(cols_count, 5 * each, HALF), "pieces_sum", "v", cost=10**6)(pieces)
    pieces = exchange(pieces, "fcol", None)
    pieces_other = lax.ppermute(pieces, "frow", swap)

    kcos, ksin = grid_tables()
    block = [np.concatenate(pair, 1) for pair in ((kcos, ksin), (-ksin, kcos), (kcos, -ksin), (ksin, kcos))]
    forward_block = np.concatenate([block[0], block[1]], 0)
    inverse_block = np.concatenate([block[2], block[3]], 0)
    own_planes, own_wide = call(
        own_half_kernel, (shape(3, SG, HALF, dtype=f32), shape(SG, 2 * SG, dtype=f32)), "own_half", "vv",
        scratch=[pltpu.VMEM((5, SG, HALF), f32)], cost=10**9,
    )(pieces, forward_block)
    *back, rest = call(
        functools.partial(grids_kernel, chips), (shape(2 * SG + 16, HALF),) * chips + (shape(2 * SG, HALF),), "grids",
        "v" * (7 + chips),
        scratch=[
            pltpu.VMEM((5, SG, SG), f32), pltpu.VMEM((SG, 2 * SG), bf16), pltpu.VMEM((2 * SG, SG), bf16),
            pltpu.VMEM((SG, 2 * SG), bf16),
        ],
        cost=10**9,
    )(own_planes, own_wide, pieces_other, *parts, inverse_block, forward_block, forward_block, inverse_block)
    back = turned(back)

    both = pltpu.VMEM((side, 2 * SG), bf16)
    square = shape(side, side, dtype=f32)
    first = call(first_part_kernel, square, "first_part", "vvv", cost=10**9)(back[0], rest, back_row)
    back[2], first = lax.optimization_barrier((back[2], first))
    rest = {k: lax.ppermute(back[k], "frow", swap) for k in (2, 1, 3)}
    first = call(
        functools.partial(own_column_kernel, chips, 2), square, "own_column", "v" * 5, scratch=[both], cost=10**9
    )(back[2], rest[2], first, back_row, back_col)
    return call(
        functools.partial(image_kernel, scale_out, chips), (square, shape(2, n_vis, dtype=f32)), "image",
        "v" * (chips + 6), outs="aa",
        scratch=[both, pltpu.VMEM((side, side), f32), pltpu.VMEM((2, n_vis), f32), pltpu.SemaphoreType.DMA((5,))],
        cost=10**9,
    )(*back, rest[1], rest[3], first, back_row, back_col, observed)


def solution(mesh):
    in_specs = (
        P("frow", "fcol"),
        P(),
        P(),
        P(("frow", "fcol")),
        P(("frow", "fcol")),
        P(("frow", "fcol")),
        P(None, ("frow", "fcol")),
    )
    out_specs = (P("frow", "fcol"), P(None, ("frow", "fcol")))
    return jax.shard_map(shards, mesh=mesh, in_specs=in_specs, out_specs=out_specs, check_vma=False)
```

```python
import functools
import math

import jax
import jax.numpy as jnp
import ml_dtypes
import numpy as np
from jax import lax
from jax.experimental import pallas as pl
from jax.experimental.pallas import tpu as pltpu
from jax.sharding import PartitionSpec as P

SKY = 65536
SG = 256
NR = 2
NC = 2
HALF = SG // 2
LANES = 128
BOTH = ("frow", "fcol")


def wave(count):
    count = count & (SKY - 1)
    turned = count + SKY // 8
    near = (turned & (SKY // 4 - 1)) - SKY // 8
    quarter = lax.shift_right_logical(turned, 14) & 3
    t = near.astype(jnp.float32) * (2.0 * math.pi / SKY)
    q = t * t
    sin = t * (1.0 + q * (-1.0 / 6 + q * (1.0 / 120 + q * (-1.0 / 5040 + q * (1.0 / 362880)))))
    cos = 1.0 + q * (-0.5 + q * (1.0 / 24 + q * (-1.0 / 720 + q * (1.0 / 40320))))
    odd = (quarter & 1) == 1
    one, two = jnp.where(odd, sin, cos), jnp.where(odd, cos, sin)
    return (
        jnp.where((quarter == 1) | (quarter == 2), -one, one),
        jnp.where(quarter >= 2, -two, two),
    )


def lanes(n):
    return lax.broadcasted_iota(jnp.int32, (1, n), 1)


def sublanes(n):
    return lax.broadcasted_iota(jnp.int32, (n, 1), 0)


def spread(coarse, fine, store):
    for k in range(coarse[0].shape[0]):
        c, s = coarse[0][k:k + 1], coarse[1][k:k + 1]
        store(k * 16, c * fine[0] - s * fine[1], s * fine[0] + c * fine[1])


def place():
    return lax.axis_index("frow"), lax.axis_index("fcol")


def served():
    row_index, col_index = place()
    return lax.rem(row_index // 2 + col_index, NR * NC)


def half_columns(cols_count, offsets, half, side, col_tab):
    bf16 = jnp.bfloat16
    col_index = place()[1]
    unit = sublanes(16)
    col_step = SKY // (cols_count * side)
    col_base = col_index * (SKY // cols_count)
    freq = [offsets[c] + half * HALF + lanes(HALF) for c in range(NC)]
    freq = jnp.concatenate(freq, 1)
    coarse = wave((col_base + 16 * col_step * sublanes(side // 16)) * freq)
    fine = wave((col_step * unit) * freq)

    def store(at, cos, sin):
        for c in range(NC):
            some = slice(c * HALF, (c + 1) * HALF)
            col_tab[at:at + 16, 2 * c * HALF:(2 * c + 1) * HALF] = cos[:, some].astype(bf16)
            col_tab[at:at + 16, (2 * c + 1) * HALF:(2 * c + 2) * HALF] = sin[:, some].astype(bf16)

    spread(coarse, fine, store)


def send_columns_kernel(cols_count, offsets, facet, subgrid, u, v, observed, send, vis, *scratch):
    col_tab, image, indices, seen, first, made, tail, sems = scratch
    f32, bf16 = jnp.float32, jnp.bfloat16
    side = facet.shape[0]
    pairs = [
        (offsets, first), (facet, image), (subgrid, indices.at[0]), (u, indices.at[1]), (v, indices.at[2]), (observed, seen),
    ]
    copies = [pltpu.make_async_copy(source, target, sems.at[n]) for n, (source, target) in enumerate(pairs)]
    for copy in copies:
        copy.start()
    copies[0].wait()
    half_columns(cols_count, first, 1 - place()[0] % 2, side, col_tab)
    for copy in copies[2:]:
        copy.wait()
    some = jnp.concatenate([indices[n].astype(f32) for n in range(3)] + [seen[...], jnp.zeros((3, side), f32)], 0)
    some = jnp.concatenate([some[:, :side // 2], some[:, side // 2:]], 0).astype(bf16)
    tail[:, :side // 2] = some
    tail[:, side // 2:] = some
    writes = [
        pltpu.make_async_copy(tail.at[:, pl.ds(0, side // 2)], vis, sems.at[6]),
        pltpu.make_async_copy(tail, send.at[pl.ds(side, 16)], sems.at[7]),
    ]
    for write in writes:
        write.start()
    copies[1].wait()
    step = side // 2
    for n in range(2):
        at = pl.ds(n * step, step)
        made[at] = jnp.dot(image[at], col_tab[...], preferred_element_type=f32).astype(bf16)
        write = pltpu.make_async_copy(made.at[at], send.at[at], sems.at[8 + n])
        write.start()
        writes.append(write)
    for write in writes:
        write.wait()


def own_tables_kernel(rows_count, cols_count, offsets, col_offsets, facet, own, row_tab, col_tab):
    bf16 = jnp.bfloat16
    row_index, _ = place()
    side = facet.shape[0]
    half_columns(cols_count, col_offsets, row_index % 2, side, col_tab)
    own[...] = jnp.dot(facet[...], col_tab[...], preferred_element_type=jnp.float32).astype(bf16)
    unit = sublanes(16)
    row_step = SKY // (rows_count * side)
    for f in range(2):
        pos = (row_index ^ f) * (SKY // rows_count) + row_step * lanes(side)
        fine = wave(unit * pos)
        for r in range(NR):
            coarse = wave((offsets[r] + 16 * unit) * pos)

            def store(at, cos, sin, r=r, f=f):
                row_tab[2 * r, at:at + 16, f * side:(f + 1) * side] = cos.astype(bf16)
                row_tab[2 * r + 1, at:at + 16, f * side:(f + 1) * side] = sin.astype(bf16)

            spread(coarse, fine, store)


def contribution_kernel(scale, number, own, own_vis, other, row_tab, out):
    f32, bf16 = jnp.float32, jnp.bfloat16
    side = own.shape[0]
    vis = []
    for some in (own_vis[...], other[side:]):
        vis += [some[:, k * LANES:(k + 1) * LANES] for k in range(side // 2 // LANES)]
    for k, some in enumerate(vis):
        at = 2 * SG + 16 * k
        out[at:at + 16] = some
    r, c = split_number(served() + number)
    at = pl.ds(pl.multiple_of(c * SG, SG), SG)
    right = jnp.concatenate([own[:, at], other[:side, at]], 0)
    with_cos = jnp.dot(row_tab[2 * r], right, preferred_element_type=f32)
    with_sin = jnp.dot(row_tab[2 * r + 1], right, preferred_element_type=f32)
    out[:SG] = ((with_cos[:, :HALF] - with_sin[:, HALF:]) * scale).astype(bf16)
    out[SG:2 * SG] = (-(with_cos[:, HALF:] + with_sin[:, :HALF]) * scale).astype(bf16)


def split_number(number):
    number = lax.rem(number, NR * NC)
    return number // NC, lax.rem(number, NC)


def vis_rows(block):
    count = block.shape[0] // 16
    return jnp.concatenate(
        [block[16 * k + 8 * part:16 * k + 8 * part + 8] for part in range(2) for k in range(count)], 1
    )


def grid_sums(parts):
    f32, bf16 = jnp.float32, jnp.bfloat16
    row_index, _ = place()
    chip = served().astype(f32)
    v_at = (sublanes(HALF) + (row_index % 2) * HALF).astype(f32)
    counter = sublanes(SG).astype(f32)
    total = jnp.zeros((SG, 3 * HALF), f32)
    planes = [jnp.zeros((SG, HALF), f32)] * 2
    for part in parts:
        one = vis_rows(part[2 * SG:].astype(f32))
        u_here = jnp.where(one[0:1] == chip, one[1:2], -1.0)
        hot = jnp.where(u_here == counter, 1.0, 0.0).astype(bf16)
        pick = one[2:3] == v_at
        right = jnp.concatenate(
            [jnp.where(pick, one[3:4], 0.0), jnp.where(pick, one[4:5], 0.0), jnp.where(pick, 1.0, 0.0)], 0
        ).astype(bf16)
        total = total + lax.dot_general(hot, right, (((1,), (1,)), ((), ())), preferred_element_type=f32)
        planes = [planes[p] + part[p * SG:(p + 1) * SG].astype(f32) for p in range(2)]
    return planes + [total[:, p * HALF:(p + 1) * HALF] for p in range(3)]


def first_sums_kernel(*refs):
    for p, plane in enumerate(grid_sums(refs[:-1])):
        refs[-1][p] = plane


def gridding_kernel(*refs):
    parts, (first, _, pieces, planes) = refs[:-4], refs[-4:]
    for p, plane in enumerate(grid_sums(parts)):
        planes[p] = first[p] + plane
    each = SG // pieces.shape[0]
    for j in range(pieces.shape[0]):
        rows = [planes[p, j * each:(j + 1) * each] for p in range(5)]
        pieces[j] = jnp.concatenate(rows, 0).astype(jnp.bfloat16)


def pieces_sum_kernel(pieces, out):
    f32, bf16 = jnp.float32, jnp.bfloat16
    total = pieces[0].astype(f32)
    for j in range(1, pieces.shape[0]):
        total = total + pieces[j].astype(f32)
    total = total.astype(bf16)
    for j in range(out.shape[0]):
        out[j] = total


def lay_out(pieces, half, planes, lanes_at):
    f32, bf16 = jnp.float32, jnp.bfloat16
    each = SG // pieces.shape[0]
    for j in range(pieces.shape[0]):
        some = pieces[j].astype(f32)
        for p in range(5):
            planes[p, j * each:(j + 1) * each, lanes_at] = some[p * each:(p + 1) * each]

    def step(forward):
        rows = [pl.ds(pl.multiple_of(p * SG + half * HALF, HALF), HALF) for p in range(2)]
        left = jnp.concatenate([planes[p, :, lanes_at].astype(bf16) for p in range(2)], 1)
        right = jnp.concatenate([forward[at] for at in rows], 0)
        return jnp.dot(left, right, preferred_element_type=f32)

    return step


def own_half_kernel(pieces, forward, out, wide, planes):
    wide[...] = lay_out(pieces, place()[0] % 2, planes, slice(0, HALF))(forward)
    out[...] = planes[2:]


def grids_kernel(chips, own, own_wide, other, *refs):
    f32, bf16 = jnp.float32, jnp.bfloat16
    parts, (grid_left, forward, inverse_left, inverse) = refs[:chips], refs[chips:chips + 4]
    outs, rest, (planes, cat, tall, hat) = refs[chips + 4:-5], refs[-5], refs[-4:]
    row_index, _ = place()
    core = row_index % 2
    chip = served().astype(f32)
    at = [pl.ds(pl.multiple_of(half * HALF, HALF), HALF) for half in (core, 1 - core)]
    wide = (own_wide[...] + lay_out(other, 1 - core, planes, at[1])(forward)).astype(bf16)
    for p in range(3):
        planes[2 + p, :, at[0]] = own[p]
    tall[:SG] = wide[:, :SG]
    tall[SG:] = wide[:, SG:]
    model = jnp.dot(grid_left[...], tall[...], preferred_element_type=f32) * (1.0 / SG)
    hat_real, hat_imag = model[:SG], model[SG:]
    cat[:, :SG] = (planes[2] - planes[4] * hat_real).astype(bf16)
    cat[:, SG:] = (planes[3] - planes[4] * hat_imag).astype(bf16)
    hat[:, :SG] = hat_real.astype(bf16)
    hat[:, SG:] = hat_imag.astype(bf16)
    wide = jnp.dot(cat[...], inverse[...], preferred_element_type=f32)
    for k in range(2):
        tall[k * SG:(k + 1) * SG] = wide[:, k * SG:(k + 1) * SG].astype(bf16)
    back = jnp.dot(inverse_left[...], tall[...], preferred_element_type=f32) * (1.0 / SG)
    rest[...] = jnp.where(core == 0, back[:, HALF:], back[:, :HALF]).astype(bf16)
    back = jnp.where(core == 0, back[:, :HALF], back[:, HALF:]).astype(bf16)
    counter = sublanes(SG).astype(f32)
    vis_each = (parts[0].shape[0] - 2 * SG) // 2
    for k, out in enumerate(outs):
        out[:2 * SG] = back
        ask = vis_rows(parts[-k % chips][2 * SG:2 * SG + vis_each].astype(f32))
        u_here = jnp.where(ask[0:1] == chip, ask[1:2], -1.0)
        hot = jnp.where(u_here == counter, 1.0, 0.0).astype(bf16)
        pick = ask[2:3] == counter
        line = lax.dot_general(hat[...], hot, (((0,), (0,)), ((), ())), preferred_element_type=f32)
        rows = []
        for part in range(2):
            value = jnp.sum(jnp.where(pick, line[part * SG:(part + 1) * SG], 0.0), axis=0, keepdims=True)
            rows += [value[:, i * LANES:(i + 1) * LANES] for i in range(value.shape[1] // LANES)]
        rows.append(jnp.zeros((16 - len(rows), LANES), f32))
        out[2 * SG:] = jnp.concatenate(rows, 0).astype(bf16)


def back_tables_kernel(rows_count, cols_count, side, offsets_row, offsets_col, row_tab, col_tab):
    bf16 = jnp.bfloat16
    row_index, col_index = place()
    unit = sublanes(16)
    row_step = SKY // (rows_count * side)
    row_base = row_index * (SKY // rows_count)
    for r in range(NR):
        freq = offsets_row[r] + lanes(SG)
        coarse = wave((row_base + 16 * row_step * sublanes(side // 16)) * freq)
        fine = wave((row_step * unit) * freq)

        def store(at, cos, sin, r=r):
            row_tab[at:at + 16, 2 * r * SG:(2 * r + 1) * SG] = cos.astype(bf16)
            row_tab[at:at + 16, (2 * r + 1) * SG:(2 * r + 2) * SG] = sin.astype(bf16)

        spread(coarse, fine, store)
    col_step = SKY // (cols_count * side)
    pos = col_index * (SKY // cols_count) + col_step * lanes(side)
    fine = wave(unit * pos)
    for c in range(NC):
        coarse = wave((offsets_col[c] + 16 * unit) * pos)

        def store(at, cos, sin, c=c):
            left = (2 * c + at // HALF) * 2 * HALF + at % HALF
            col_tab[left:left + 16] = cos.astype(bf16)
            col_tab[left + HALF:left + HALF + 16] = (-sin).astype(bf16)

        spread(coarse, fine, store)


def block_part(block, number, row_tab):
    r, _ = split_number(number)
    real, imag = block[:SG], block[SG:2 * SG]
    right = jnp.concatenate([jnp.concatenate([real, imag], 1), jnp.concatenate([-imag, real], 1)], 0)
    left = row_tab[:, pl.ds(pl.multiple_of(2 * r * SG, 2 * SG), 2 * SG)]
    return jnp.dot(left, right, preferred_element_type=jnp.float32)


def first_part_kernel(own, rest, row_tab, out):
    chip = served()
    for n, block in enumerate((own, rest)):
        out[:, n * SG:(n + 1) * SG] = block_part(block, chip, row_tab)


def column_rows(number):
    depth = 2 * SG
    return pl.ds(pl.multiple_of(split_number(number)[1] * depth, depth), depth)


def half_lanes(n):
    half = place()[0] % 2
    return pl.ds(pl.multiple_of((half if n == 0 else 1 - half) * SG, SG), SG)


def own_column_kernel(chips, opposite, own, rest, first, row_tab, col_tab, out, both):
    chip = served()
    for n, block in enumerate((own, rest)):
        part = first[:, n * SG:(n + 1) * SG] + block_part(block, chip + chips - opposite, row_tab)
        both[:, half_lanes(n)] = part.astype(jnp.bfloat16)
    out[...] = jnp.dot(both[...], col_tab[column_rows(chip)], preferred_element_type=jnp.float32)


def image_kernel(scale, chips, *refs):
    f32, bf16 = jnp.float32, jnp.bfloat16
    blocks, others, refs = refs[:chips], refs[chips:chips + 2], refs[chips + 2:]
    first, row_tab, col_tab, observed, out, residual, both, image, seen, sems = refs
    chip = served()
    model = jnp.zeros((16, LANES), f32)
    for block in blocks:
        model = model + block[2 * SG:].astype(f32)
    count = observed.shape[1] // LANES
    for part in range(2):
        for i in range(count):
            at = slice(i * LANES, (i + 1) * LANES)
            seen[part:part + 1, at] = observed[part:part + 1, at] - model[part * count + i:part * count + i + 1]
    writes = [pltpu.make_async_copy(seen, residual, sems.at[0])]
    writes[0].start()
    for n, pair in enumerate(((blocks[1], blocks[3]), others)):
        part = block_part(pair[0], chip + chips - 1, row_tab) + block_part(pair[1], chip + chips - 3, row_tab)
        both[:, half_lanes(n)] = part.astype(bf16)
    chunks = sems.shape[0] - 1
    step = image.shape[0] // chunks
    for n in range(chunks):
        at = slice(n * step, (n + 1) * step)
        part = jnp.dot(both[at], col_tab[column_rows(chip + 1)], preferred_element_type=f32)
        image[at] = (first[at] + part) * scale
        write = pltpu.make_async_copy(image.at[at], out.at[at], sems.at[1 + n])
        write.start()
        writes.append(write)
    for write in writes:
        write.wait()


def call(kernel, out_shape, name, spaces, scratch=(), cost=0, outs=None, room=24):
    kinds = {"s": pltpu.SMEM, "v": pltpu.VMEM, "a": pl.ANY}
    several = isinstance(out_shape, tuple)
    outs = outs or "v" * (len(out_shape) if several else 1)
    out_specs = tuple(pl.BlockSpec(memory_space=kinds[kind]) for kind in outs)
    return pl.pallas_call(
        kernel,
        out_shape=out_shape,
        in_specs=[pl.BlockSpec(memory_space=kinds[kind]) for kind in spaces],
        out_specs=out_specs if several else out_specs[0],
        scratch_shapes=list(scratch),
        compiler_params=pltpu.CompilerParams(vmem_limit_bytes=room * 2**20),
        cost_estimate=pl.CostEstimate(flops=cost, bytes_accessed=2**20, transcendentals=0),
        name=name,
    )


def grid_tables():
    counter = np.arange(SG)
    angles = (counter[:, None] * counter[None, :] % SG).astype(np.float64) * (2.0 * math.pi / SG)
    return np.cos(angles).astype(ml_dtypes.bfloat16), np.sin(angles).astype(ml_dtypes.bfloat16)


def exchange(blocks, axes, groups):
    return lax.all_to_all(blocks, axes, 0, 0, tiled=True, axis_index_groups=groups)


def shape(*dims, dtype=jnp.bfloat16):
    return jax.ShapeDtypeStruct(dims, dtype)


def shards(facet, row_offsets, col_offsets, vis_subgrid, vis_u, vis_v, observed):
    f32, bf16 = jnp.float32, jnp.bfloat16
    rows_count, cols_count = lax.axis_size("frow"), lax.axis_size("fcol")
    side = facet.shape[0]
    n_vis = vis_u.shape[0]
    chips = rows_count // 2
    each = SG // cols_count
    swap = [(index, index ^ 1) for index in range(rows_count)]
    line = NR * NC

    def turn(index, k):
        row, col = index // cols_count, index % cols_count
        if row % 2 == 0:
            row = (row + 2 * k) % rows_count
        else:
            col = col // line * line + (col + k) % line
        return row * cols_count + col

    turns = [[(index, turn(index, k)) for index in range(rows_count * cols_count)] for k in range(chips)]
    groups = [
        [((number - col) % line * 2 + core) * cols_count + col for col in range(cols_count)]
        for number in range(line) for core in range(2)
    ]

    def turned(blocks):
        moved = {k: lax.ppermute(blocks[k], BOTH, turns[k]) for k in (2, 1, 3)}
        return [blocks[0]] + [moved[k] for k in range(1, chips)]

    scale_in = 1.0 / (side * math.sqrt(rows_count * cols_count))
    scale_out = 1.0 / (SG * math.sqrt(NR * NC))
    flat = (1, n_vis)

    send, vis = call(
        functools.partial(send_columns_kernel, cols_count), (shape(side + 16, 4 * HALF), shape(16, n_vis // 2)),
        "send_columns", "aaaaaa",
        scratch=[
            pltpu.VMEM((side, 4 * HALF), bf16), pltpu.VMEM((side, side), bf16), pltpu.VMEM((3,) + flat, jnp.int32),
            pltpu.VMEM((2, n_vis), f32), pltpu.SMEM((NC,), jnp.int32), pltpu.VMEM((side, 4 * HALF), bf16),
            pltpu.VMEM((16, n_vis), bf16), pltpu.SemaphoreType.DMA((10,)),
        ],
        cost=10**9, room=60, outs="aa",
    )(col_offsets, facet, vis_subgrid.reshape(flat), vis_u.reshape(flat), vis_v.reshape(flat), observed)
    other = lax.ppermute(send, "frow", swap)
    own, row_tab = call(
        functools.partial(own_tables_kernel, rows_count, cols_count),
        (shape(side, 4 * HALF), shape(4, SG, 2 * side)), "own_tables", "ssv",
        scratch=[pltpu.VMEM((side, 4 * HALF), bf16)], cost=10**9,
    )(row_offsets, col_offsets, facet)
    vis_rows_count = 8 * 2 * n_vis // LANES
    parts = {}
    for k in (2, 1, 3, 0):
        parts[k] = call(
            functools.partial(contribution_kernel, scale_in, k), shape(2 * SG + vis_rows_count, HALF), "contribution",
            "vvvv", cost=5 * 10**8,
        )(own, vis, other, row_tab)
        own, parts[k] = lax.optimization_barrier((own, parts[k]))
    parts = turned(parts)

    sums = call(first_sums_kernel, shape(5, SG, HALF, dtype=f32), "first_sums", "vv", cost=10**9)(parts[0], parts[2])
    back_row, back_col = call(
        functools.partial(back_tables_kernel, rows_count, cols_count, side),
        (shape(side, 4 * SG), shape(4 * SG, side)), "back_tables", "ss", cost=10**9,
    )(row_offsets, col_offsets)
    pieces = call(
        gridding_kernel, shape(cols_count, 5 * each, HALF), "gridding", "v" * (chips - 1) + "a",
        scratch=[pltpu.VMEM((5, SG, HALF), f32)], cost=10**9,
    )(parts[1], parts[3], sums, back_col)
    pieces = exchange(pieces, BOTH, groups)
    pieces = call(pieces_sum_kernel, shape(cols_count, 5 * each, HALF), "pieces_sum", "v", cost=10**6)(pieces)
    pieces = exchange(pieces, BOTH, groups)
    pieces_other = lax.ppermute(pieces, "frow", swap)

    kcos, ksin = grid_tables()
    block = [np.concatenate(pair, 1) for pair in ((kcos, ksin), (-ksin, kcos), (kcos, -ksin), (ksin, kcos))]
    forward_block = np.concatenate([block[0], block[1]], 0)
    inverse_block = np.concatenate([block[2], block[3]], 0)
    own_planes, own_wide = call(
        own_half_kernel, (shape(3, SG, HALF, dtype=f32), shape(SG, 2 * SG, dtype=f32)), "own_half", "vv",
        scratch=[pltpu.VMEM((5, SG, HALF), f32)], cost=10**9,
    )(pieces, forward_block)
    *back, rest = call(
        functools.partial(grids_kernel, chips), (shape(2 * SG + 16, HALF),) * chips + (shape(2 * SG, HALF),), "grids",
        "v" * (7 + chips),
        scratch=[
            pltpu.VMEM((5, SG, SG), f32), pltpu.VMEM((SG, 2 * SG), bf16), pltpu.VMEM((2 * SG, SG), bf16),
            pltpu.VMEM((SG, 2 * SG), bf16),
        ],
        cost=10**9,
    )(own_planes, own_wide, pieces_other, *parts, inverse_block, forward_block, forward_block, inverse_block)
    back = turned(back)

    both = pltpu.VMEM((side, 2 * SG), bf16)
    square = shape(side, side, dtype=f32)
    first = call(first_part_kernel, square, "first_part", "vvv", cost=10**9)(back[0], rest, back_row)
    back[2], first = lax.optimization_barrier((back[2], first))
    rest = {k: lax.ppermute(back[k], "frow", swap) for k in (2, 1, 3)}
    first = call(
        functools.partial(own_column_kernel, chips, 2), square, "own_column", "v" * 5, scratch=[both], cost=10**9
    )(back[2], rest[2], first, back_row, back_col)
    return call(
        functools.partial(image_kernel, scale_out, chips), (square, shape(2, n_vis, dtype=f32)), "image",
        "v" * (chips + 6), outs="aa",
        scratch=[both, pltpu.VMEM((side, side), f32), pltpu.VMEM((2, n_vis), f32), pltpu.SemaphoreType.DMA((5,))],
        cost=10**9,
    )(*back, rest[1], rest[3], first, back_row, back_col, observed)


def solution(mesh):
    in_specs = (
        P("frow", "fcol"),
        P(),
        P(),
        P(("frow", "fcol")),
        P(("frow", "fcol")),
        P(("frow", "fcol")),
        P(None, ("frow", "fcol")),
    )
    out_specs = (P("frow", "fcol"), P(None, ("frow", "fcol")))
    return jax.shard_map(shards, mesh=mesh, in_specs=in_specs, out_specs=out_specs, check_vma=False)
```

```python
import functools
import math

import jax
import jax.numpy as jnp
import ml_dtypes
import numpy as np
from jax import lax
from jax.experimental import pallas as pl
from jax.experimental.pallas import tpu as pltpu
from jax.sharding import PartitionSpec as P

SKY = 65536
SG = 256
NR = 2
NC = 2
HALF = SG // 2
LANES = 128


def wave(count):
    count = count & (SKY - 1)
    turned = count + SKY // 8
    near = (turned & (SKY // 4 - 1)) - SKY // 8
    quarter = lax.shift_right_logical(turned, 14) & 3
    t = near.astype(jnp.float32) * (2.0 * math.pi / SKY)
    q = t * t
    sin = t * (1.0 + q * (-1.0 / 6 + q * (1.0 / 120 + q * (-1.0 / 5040 + q * (1.0 / 362880)))))
    cos = 1.0 + q * (-0.5 + q * (1.0 / 24 + q * (-1.0 / 720 + q * (1.0 / 40320))))
    odd = (quarter & 1) == 1
    one, two = jnp.where(odd, sin, cos), jnp.where(odd, cos, sin)
    return (
        jnp.where((quarter == 1) | (quarter == 2), -one, one),
        jnp.where(quarter >= 2, -two, two),
    )


def lanes(n):
    return lax.broadcasted_iota(jnp.int32, (1, n), 1)


def sublanes(n):
    return lax.broadcasted_iota(jnp.int32, (n, 1), 0)


def spread(coarse, fine, store):
    for k in range(coarse[0].shape[0]):
        c, s = coarse[0][k:k + 1], coarse[1][k:k + 1]
        store(k * 16, c * fine[0] - s * fine[1], s * fine[0] + c * fine[1])


def place():
    return lax.axis_index("frow"), lax.axis_index("fcol")


def half_columns(cols_count, offsets, half, side, col_tab):
    bf16 = jnp.bfloat16
    col_index = place()[1]
    unit = sublanes(16)
    col_step = SKY // (cols_count * side)
    col_base = col_index * (SKY // cols_count)
    freq = [offsets[c] + half * HALF + lanes(HALF) for c in range(NC)]
    freq = jnp.concatenate(freq, 1)
    coarse = wave((col_base + 16 * col_step * sublanes(side // 16)) * freq)
    fine = wave((col_step * unit) * freq)

    def store(at, cos, sin):
        for c in range(NC):
            some = slice(c * HALF, (c + 1) * HALF)
            col_tab[at:at + 16, 2 * c * HALF:(2 * c + 1) * HALF] = cos[:, some].astype(bf16)
            col_tab[at:at + 16, (2 * c + 1) * HALF:(2 * c + 2) * HALF] = sin[:, some].astype(bf16)

    spread(coarse, fine, store)


def send_columns_kernel(cols_count, offsets, facet, subgrid, u, v, observed, send, vis, *scratch):
    col_tab, image, indices, seen, first, made, tail, sems = scratch
    f32, bf16 = jnp.float32, jnp.bfloat16
    side = facet.shape[0]
    pairs = [
        (offsets, first), (facet, image), (subgrid, indices.at[0]), (u, indices.at[1]), (v, indices.at[2]), (observed, seen),
    ]
    copies = [pltpu.make_async_copy(source, target, sems.at[n]) for n, (source, target) in enumerate(pairs)]
    for copy in copies:
        copy.start()
    copies[0].wait()
    half_columns(cols_count, first, 1 - place()[0] % 2, side, col_tab)
    for copy in copies[2:]:
        copy.wait()
    some = jnp.concatenate([indices[n].astype(f32) for n in range(3)] + [seen[...], jnp.zeros((3, side), f32)], 0)
    some = jnp.concatenate([some[:, :side // 2], some[:, side // 2:]], 0).astype(bf16)
    tail[:, :side // 2] = some
    tail[:, side // 2:] = some
    writes = [
        pltpu.make_async_copy(tail.at[:, pl.ds(0, side // 2)], vis, sems.at[6]),
        pltpu.make_async_copy(tail, send.at[pl.ds(side, 16)], sems.at[7]),
    ]
    for write in writes:
        write.start()
    copies[1].wait()
    step = side // 2
    for n in range(2):
        at = pl.ds(n * step, step)
        made[at] = jnp.dot(image[at], col_tab[...], preferred_element_type=f32).astype(bf16)
        write = pltpu.make_async_copy(made.at[at], send.at[at], sems.at[8 + n])
        write.start()
        writes.append(write)
    for write in writes:
        write.wait()


def own_tables_kernel(rows_count, cols_count, offsets, col_offsets, facet, own, row_tab, col_tab):
    bf16 = jnp.bfloat16
    row_index, _ = place()
    side = facet.shape[0]
    half_columns(cols_count, col_offsets, row_index % 2, side, col_tab)
    own[...] = jnp.dot(facet[...], col_tab[...], preferred_element_type=jnp.float32).astype(bf16)
    unit = sublanes(16)
    row_step = SKY // (rows_count * side)
    for f in range(2):
        pos = (row_index ^ f) * (SKY // rows_count) + row_step * lanes(side)
        fine = wave(unit * pos)
        for r in range(NR):
            coarse = wave((offsets[r] + 16 * unit) * pos)

            def store(at, cos, sin, r=r, f=f):
                row_tab[2 * r, at:at + 16, f * side:(f + 1) * side] = cos.astype(bf16)
                row_tab[2 * r + 1, at:at + 16, f * side:(f + 1) * side] = sin.astype(bf16)

            spread(coarse, fine, store)


def contribution_kernel(scale, number, own, own_vis, other, row_tab, out):
    f32, bf16 = jnp.float32, jnp.bfloat16
    side = own.shape[0]
    vis = []
    for some in (own_vis[...], other[side:]):
        vis += [some[:, k * LANES:(k + 1) * LANES] for k in range(side // 2 // LANES)]
    for k, some in enumerate(vis):
        at = 2 * SG + 16 * k
        out[at:at + 16] = some
    r, c = split_number(place()[0] // 2 + number)
    at = pl.ds(pl.multiple_of(c * SG, SG), SG)
    right = jnp.concatenate([own[:, at], other[:side, at]], 0)
    with_cos = jnp.dot(row_tab[2 * r], right, preferred_element_type=f32)
    with_sin = jnp.dot(row_tab[2 * r + 1], right, preferred_element_type=f32)
    out[:SG] = ((with_cos[:, :HALF] - with_sin[:, HALF:]) * scale).astype(bf16)
    out[SG:2 * SG] = (-(with_cos[:, HALF:] + with_sin[:, :HALF]) * scale).astype(bf16)


def split_number(number):
    number = lax.rem(number, NR * NC)
    return number // NC, lax.rem(number, NC)


def vis_rows(block):
    count = block.shape[0] // 16
    return jnp.concatenate(
        [block[16 * k + 8 * part:16 * k + 8 * part + 8] for part in range(2) for k in range(count)], 1
    )


def grid_sums(parts):
    f32, bf16 = jnp.float32, jnp.bfloat16
    row_index, _ = place()
    chip = (row_index // 2).astype(f32)
    v_at = (sublanes(HALF) + (row_index % 2) * HALF).astype(f32)
    counter = sublanes(SG).astype(f32)
    total = jnp.zeros((SG, 3 * HALF), f32)
    planes = [jnp.zeros((SG, HALF), f32)] * 2
    for part in parts:
        one = vis_rows(part[2 * SG:].astype(f32))
        u_here = jnp.where(one[0:1] == chip, one[1:2], -1.0)
        hot = jnp.where(u_here == counter, 1.0, 0.0).astype(bf16)
        pick = one[2:3] == v_at
        right = jnp.concatenate(
            [jnp.where(pick, one[3:4], 0.0), jnp.where(pick, one[4:5], 0.0), jnp.where(pick, 1.0, 0.0)], 0
        ).astype(bf16)
        total = total + lax.dot_general(hot, right, (((1,), (1,)), ((), ())), preferred_element_type=f32)
        planes = [planes[p] + part[p * SG:(p + 1) * SG].astype(f32) for p in range(2)]
    return planes + [total[:, p * HALF:(p + 1) * HALF] for p in range(3)]


def first_sums_kernel(*refs):
    for p, plane in enumerate(grid_sums(refs[:-1])):
        refs[-1][p] = plane


def gridding_kernel(*refs):
    parts, (first, _, pieces, planes) = refs[:-4], refs[-4:]
    for p, plane in enumerate(grid_sums(parts)):
        planes[p] = first[p] + plane
    each = SG // pieces.shape[0]
    for j in range(pieces.shape[0]):
        rows = [planes[p, j * each:(j + 1) * each] for p in range(5)]
        pieces[j] = jnp.concatenate(rows, 0).astype(jnp.bfloat16)


def pieces_sum_kernel(pieces, out):
    f32, bf16 = jnp.float32, jnp.bfloat16
    total = pieces[0].astype(f32)
    for j in range(1, pieces.shape[0]):
        total = total + pieces[j].astype(f32)
    total = total.astype(bf16)
    for j in range(out.shape[0]):
        out[j] = total


def lay_out(pieces, half, planes, lanes_at):
    f32, bf16 = jnp.float32, jnp.bfloat16
    each = SG // pieces.shape[0]
    for j in range(pieces.shape[0]):
        some = pieces[j].astype(f32)
        for p in range(5):
            planes[p, j * each:(j + 1) * each, lanes_at] = some[p * each:(p + 1) * each]

    def step(forward):
        rows = [pl.ds(pl.multiple_of(p * SG + half * HALF, HALF), HALF) for p in range(2)]
        left = jnp.concatenate([planes[p, :, lanes_at].astype(bf16) for p in range(2)], 1)
        right = jnp.concatenate([forward[at] for at in rows], 0)
        return jnp.dot(left, right, preferred_element_type=f32)

    return step


def own_half_kernel(pieces, forward, out, wide, planes):
    wide[...] = lay_out(pieces, place()[0] % 2, planes, slice(0, HALF))(forward)
    out[...] = planes[2:]


def grids_kernel(own, own_wide, other, grid_left, forward, inverse_left, inverse, mine, rest, hat, planes, cat, tall):
    f32, bf16 = jnp.float32, jnp.bfloat16
    core = place()[0] % 2
    at = [pl.ds(pl.multiple_of(half * HALF, HALF), HALF) for half in (core, 1 - core)]
    wide = (own_wide[...] + lay_out(other, 1 - core, planes, at[1])(forward)).astype(bf16)
    for p in range(3):
        planes[2 + p, :, at[0]] = own[p]
    tall[:SG] = wide[:, :SG]
    tall[SG:] = wide[:, SG:]
    model = jnp.dot(grid_left[...], tall[...], preferred_element_type=f32) * (1.0 / SG)
    hat_real, hat_imag = model[:SG], model[SG:]
    cat[:, :SG] = (planes[2] - planes[4] * hat_real).astype(bf16)
    cat[:, SG:] = (planes[3] - planes[4] * hat_imag).astype(bf16)
    hat[:, :SG] = hat_real.astype(bf16)
    hat[:, SG:] = hat_imag.astype(bf16)
    wide = jnp.dot(cat[...], inverse[...], preferred_element_type=f32)
    for k in range(2):
        tall[k * SG:(k + 1) * SG] = wide[:, k * SG:(k + 1) * SG].astype(bf16)
    back = jnp.dot(inverse_left[...], tall[...], preferred_element_type=f32) * (1.0 / SG)
    rest[...] = jnp.where(core == 0, back[:, HALF:], back[:, :HALF]).astype(bf16)
    mine[...] = jnp.where(core == 0, back[:, :HALF], back[:, HALF:]).astype(bf16)


def answers_kernel(chips, hat, *refs):
    f32, bf16 = jnp.float32, jnp.bfloat16
    parts, outs = refs[:chips], refs[chips:]
    chip = (place()[0] // 2).astype(f32)
    counter = sublanes(SG).astype(f32)
    vis_each = (parts[0].shape[0] - 2 * SG) // 2
    for k, out in enumerate(outs):
        ask = vis_rows(parts[-k % chips][2 * SG:2 * SG + vis_each].astype(f32))
        u_here = jnp.where(ask[0:1] == chip, ask[1:2], -1.0)
        hot = jnp.where(u_here == counter, 1.0, 0.0).astype(bf16)
        pick = ask[2:3] == counter
        line = lax.dot_general(hat[...], hot, (((0,), (0,)), ((), ())), preferred_element_type=f32)
        rows = []
        for part in range(2):
            value = jnp.sum(jnp.where(pick, line[part * SG:(part + 1) * SG], 0.0), axis=0, keepdims=True)
            rows += [value[:, i * LANES:(i + 1) * LANES] for i in range(value.shape[1] // LANES)]
        rows.append(jnp.zeros((16 - len(rows), LANES), f32))
        out[...] = jnp.concatenate(rows, 0).astype(bf16)


def back_tables_kernel(rows_count, cols_count, side, offsets_row, offsets_col, row_tab, col_tab):
    bf16 = jnp.bfloat16
    row_index, col_index = place()
    unit = sublanes(16)
    row_step = SKY // (rows_count * side)
    row_base = row_index * (SKY // rows_count)
    for r in range(NR):
        freq = offsets_row[r] + lanes(SG)
        coarse = wave((row_base + 16 * row_step * sublanes(side // 16)) * freq)
        fine = wave((row_step * unit) * freq)

        def store(at, cos, sin, r=r):
            row_tab[at:at + 16, 2 * r * SG:(2 * r + 1) * SG] = cos.astype(bf16)
            row_tab[at:at + 16, (2 * r + 1) * SG:(2 * r + 2) * SG] = sin.astype(bf16)

        spread(coarse, fine, store)
    col_step = SKY // (cols_count * side)
    pos = col_index * (SKY // cols_count) + col_step * lanes(side)
    fine = wave(unit * pos)
    for c in range(NC):
        coarse = wave((offsets_col[c] + 16 * unit) * pos)

        def store(at, cos, sin, c=c):
            left = (2 * c + at // HALF) * 2 * HALF + at % HALF
            col_tab[left:left + 16] = cos.astype(bf16)
            col_tab[left + HALF:left + HALF + 16] = (-sin).astype(bf16)

        spread(coarse, fine, store)


def block_part(block, number, row_tab):
    r, _ = split_number(number)
    real, imag = block[:SG], block[SG:2 * SG]
    right = jnp.concatenate([jnp.concatenate([real, imag], 1), jnp.concatenate([-imag, real], 1)], 0)
    left = row_tab[:, pl.ds(pl.multiple_of(2 * r * SG, 2 * SG), 2 * SG)]
    return jnp.dot(left, right, preferred_element_type=jnp.float32)


def first_part_kernel(own, rest, row_tab, out):
    chip = place()[0] // 2
    for n, block in enumerate((own, rest)):
        out[:, n * SG:(n + 1) * SG] = block_part(block, chip, row_tab)


def column_rows(number):
    depth = 2 * SG
    return pl.ds(pl.multiple_of(split_number(number)[1] * depth, depth), depth)


def half_lanes(n):
    half = place()[0] % 2
    return pl.ds(pl.multiple_of((half if n == 0 else 1 - half) * SG, SG), SG)


def own_column_kernel(chips, opposite, own, rest, first, row_tab, col_tab, out, both):
    chip = place()[0] // 2
    for n, block in enumerate((own, rest)):
        part = first[:, n * SG:(n + 1) * SG] + block_part(block, chip + chips - opposite, row_tab)
        both[:, half_lanes(n)] = part.astype(jnp.bfloat16)
    out[...] = jnp.dot(both[...], col_tab[column_rows(chip)], preferred_element_type=jnp.float32)


def image_kernel(scale, chips, *refs):
    f32, bf16 = jnp.float32, jnp.bfloat16
    answers, blocks, others, refs = refs[:chips], refs[chips:chips + 2], refs[chips + 2:chips + 4], refs[chips + 4:]
    first, row_tab, col_tab, observed, out, residual, both, image, seen, sems = refs
    chip = place()[0] // 2
    model = jnp.zeros((16, LANES), f32)
    for answer in answers:
        model = model + answer[...].astype(f32)
    count = observed.shape[1] // LANES
    for part in range(2):
        for i in range(count):
            at = slice(i * LANES, (i + 1) * LANES)
            seen[part:part + 1, at] = observed[part:part + 1, at] - model[part * count + i:part * count + i + 1]
    writes = [pltpu.make_async_copy(seen, residual, sems.at[0])]
    writes[0].start()
    for n, pair in enumerate((blocks, others)):
        part = block_part(pair[0], chip + chips - 1, row_tab) + block_part(pair[1], chip + chips - 3, row_tab)
        both[:, half_lanes(n)] = part.astype(bf16)
    chunks = sems.shape[0] - 1
    step = image.shape[0] // chunks
    for n in range(chunks):
        at = slice(n * step, (n + 1) * step)
        part = jnp.dot(both[at], col_tab[column_rows(chip + 1)], preferred_element_type=f32)
        image[at] = (first[at] + part) * scale
        write = pltpu.make_async_copy(image.at[at], out.at[at], sems.at[1 + n])
        write.start()
        writes.append(write)
    for write in writes:
        write.wait()


def call(kernel, out_shape, name, spaces, scratch=(), cost=0, outs=None, room=24):
    kinds = {"s": pltpu.SMEM, "v": pltpu.VMEM, "a": pl.ANY}
    several = isinstance(out_shape, tuple)
    outs = outs or "v" * (len(out_shape) if several else 1)
    out_specs = tuple(pl.BlockSpec(memory_space=kinds[kind]) for kind in outs)
    return pl.pallas_call(
        kernel,
        out_shape=out_shape,
        in_specs=[pl.BlockSpec(memory_space=kinds[kind]) for kind in spaces],
        out_specs=out_specs if several else out_specs[0],
        scratch_shapes=list(scratch),
        compiler_params=pltpu.CompilerParams(vmem_limit_bytes=room * 2**20),
        cost_estimate=pl.CostEstimate(flops=cost, bytes_accessed=2**20, transcendentals=0),
        name=name,
    )


def grid_tables():
    counter = np.arange(SG)
    angles = (counter[:, None] * counter[None, :] % SG).astype(np.float64) * (2.0 * math.pi / SG)
    return np.cos(angles).astype(ml_dtypes.bfloat16), np.sin(angles).astype(ml_dtypes.bfloat16)


def exchange(blocks, axes, groups):
    return lax.all_to_all(blocks, axes, 0, 0, tiled=True, axis_index_groups=groups)


def shape(*dims, dtype=jnp.bfloat16):
    return jax.ShapeDtypeStruct(dims, dtype)


def shards(facet, row_offsets, col_offsets, vis_subgrid, vis_u, vis_v, observed):
    f32, bf16 = jnp.float32, jnp.bfloat16
    rows_count, cols_count = lax.axis_size("frow"), lax.axis_size("fcol")
    side = facet.shape[0]
    n_vis = vis_u.shape[0]
    chips = rows_count // 2
    each = SG // cols_count
    swap = [(index, index ^ 1) for index in range(rows_count)]
    turns = [[(index, (index + 2 * k) % rows_count) for index in range(rows_count)] for k in range(chips)]

    def turned(blocks):
        moved = {k: lax.ppermute(blocks[k], "frow", turns[k]) for k in (2, 1, 3)}
        return [blocks[0]] + [moved[k] for k in range(1, chips)]

    scale_in = 1.0 / (side * math.sqrt(rows_count * cols_count))
    scale_out = 1.0 / (SG * math.sqrt(NR * NC))
    line = (1, n_vis)

    send, vis = call(
        functools.partial(send_columns_kernel, cols_count), (shape(side + 16, 4 * HALF), shape(16, n_vis // 2)),
        "send_columns", "aaaaaa",
        scratch=[
            pltpu.VMEM((side, 4 * HALF), bf16), pltpu.VMEM((side, side), bf16), pltpu.VMEM((3,) + line, jnp.int32),
            pltpu.VMEM((2, n_vis), f32), pltpu.SMEM((NC,), jnp.int32), pltpu.VMEM((side, 4 * HALF), bf16),
            pltpu.VMEM((16, n_vis), bf16), pltpu.SemaphoreType.DMA((10,)),
        ],
        cost=10**9, room=60, outs="aa",
    )(col_offsets, facet, vis_subgrid.reshape(line), vis_u.reshape(line), vis_v.reshape(line), observed)
    other = lax.ppermute(send, "frow", swap)
    own, row_tab = call(
        functools.partial(own_tables_kernel, rows_count, cols_count),
        (shape(side, 4 * HALF), shape(4, SG, 2 * side)), "own_tables", "ssv",
        scratch=[pltpu.VMEM((side, 4 * HALF), bf16)], cost=10**9,
    )(row_offsets, col_offsets, facet)
    vis_rows_count = 8 * 2 * n_vis // LANES
    parts = {}
    for k in (2, 1, 3, 0):
        parts[k] = call(
            functools.partial(contribution_kernel, scale_in, k), shape(2 * SG + vis_rows_count, HALF), "contribution",
            "vvvv", cost=5 * 10**8,
        )(own, vis, other, row_tab)
        own, parts[k] = lax.optimization_barrier((own, parts[k]))
    parts = turned(parts)

    sums = call(first_sums_kernel, shape(5, SG, HALF, dtype=f32), "first_sums", "vv", cost=10**9)(parts[0], parts[2])
    back_row, back_col = call(
        functools.partial(back_tables_kernel, rows_count, cols_count, side),
        (shape(side, 4 * SG), shape(4 * SG, side)), "back_tables", "ss", cost=10**9,
    )(row_offsets, col_offsets)
    pieces = call(
        gridding_kernel, shape(cols_count, 5 * each, HALF), "gridding", "v" * (chips - 1) + "a",
        scratch=[pltpu.VMEM((5, SG, HALF), f32)], cost=10**9,
    )(parts[1], parts[3], sums, back_col)
    pieces = exchange(pieces, "fcol", None)
    pieces = call(pieces_sum_kernel, shape(cols_count, 5 * each, HALF), "pieces_sum", "v", cost=10**6)(pieces)
    pieces = exchange(pieces, "fcol", None)
    pieces_other = lax.ppermute(pieces, "frow", swap)

    kcos, ksin = grid_tables()
    block = [np.concatenate(pair, 1) for pair in ((kcos, ksin), (-ksin, kcos), (kcos, -ksin), (ksin, kcos))]
    forward_block = np.concatenate([block[0], block[1]], 0)
    inverse_block = np.concatenate([block[2], block[3]], 0)
    own_planes, own_wide = call(
        own_half_kernel, (shape(3, SG, HALF, dtype=f32), shape(SG, 2 * SG, dtype=f32)), "own_half", "vv",
        scratch=[pltpu.VMEM((5, SG, HALF), f32)], cost=10**9,
    )(pieces, forward_block)
    mine, rest, hat = call(
        grids_kernel, (shape(2 * SG, HALF), shape(2 * SG, HALF), shape(SG, 2 * SG)), "grids", "v" * 7,
        scratch=[
            pltpu.VMEM((5, SG, SG), f32), pltpu.VMEM((SG, 2 * SG), bf16), pltpu.VMEM((2 * SG, SG), bf16),
        ],
        cost=10**9,
    )(own_planes, own_wide, pieces_other, inverse_block, forward_block, forward_block, inverse_block)
    back = turned([mine] * chips)

    both = pltpu.VMEM((side, 2 * SG), bf16)
    square = shape(side, side, dtype=f32)
    first = call(first_part_kernel, square, "first_part", "vvv", cost=10**9)(back[0], rest, back_row)
    first, hat = lax.optimization_barrier((first, hat))
    *answers, = call(
        functools.partial(answers_kernel, chips), (shape(16, LANES),) * chips, "answers", "v" * (1 + chips), cost=10**9
    )(hat, *parts)
    answers = turned(answers)
    back[2], *answers = lax.optimization_barrier((back[2], *answers))
    rest = {k: lax.ppermute(back[k], "frow", swap) for k in (2, 1, 3)}
    first = call(
        functools.partial(own_column_kernel, chips, 2), square, "own_column", "v" * 5, scratch=[both], cost=10**9
    )(back[2], rest[2], first, back_row, back_col)
    return call(
        functools.partial(image_kernel, scale_out, chips), (square, shape(2, n_vis, dtype=f32)), "image",
        "v" * (chips + 8), outs="aa",
        scratch=[both, pltpu.VMEM((side, side), f32), pltpu.VMEM((2, n_vis), f32), pltpu.SemaphoreType.DMA((5,))],
        cost=10**9,
    )(*answers, back[1], back[3], rest[1], rest[3], first, back_row, back_col, observed)


def solution(mesh):
    in_specs = (
        P("frow", "fcol"),
        P(),
        P(),
        P(("frow", "fcol")),
        P(("frow", "fcol")),
        P(("frow", "fcol")),
        P(None, ("frow", "fcol")),
    )
    out_specs = (P("frow", "fcol"), P(None, ("frow", "fcol")))
    return jax.shard_map(shards, mesh=mesh, in_specs=in_specs, out_specs=out_specs, check_vma=False)
```

```python
import functools
import math

import jax
import jax.numpy as jnp
import ml_dtypes
import numpy as np
from jax import lax
from jax.experimental import pallas as pl
from jax.experimental.pallas import tpu as pltpu
from jax.sharding import PartitionSpec as P

SKY = 65536
SG = 256
NR = 2
NC = 2
HALF = SG // 2
LANES = 128
BOTH = ("frow", "fcol")


def wave(count):
    count = count & (SKY - 1)
    turned = count + SKY // 8
    near = (turned & (SKY // 4 - 1)) - SKY // 8
    quarter = lax.shift_right_logical(turned, 14) & 3
    t = near.astype(jnp.float32) * (2.0 * math.pi / SKY)
    q = t * t
    sin = t * (1.0 + q * (-1.0 / 6 + q * (1.0 / 120 + q * (-1.0 / 5040 + q * (1.0 / 362880)))))
    cos = 1.0 + q * (-0.5 + q * (1.0 / 24 + q * (-1.0 / 720 + q * (1.0 / 40320))))
    odd = (quarter & 1) == 1
    one, two = jnp.where(odd, sin, cos), jnp.where(odd, cos, sin)
    return (
        jnp.where((quarter == 1) | (quarter == 2), -one, one),
        jnp.where(quarter >= 2, -two, two),
    )


def lanes(n):
    return lax.broadcasted_iota(jnp.int32, (1, n), 1)


def sublanes(n):
    return lax.broadcasted_iota(jnp.int32, (n, 1), 0)


def spread(coarse, fine, store):
    for k in range(coarse[0].shape[0]):
        c, s = coarse[0][k:k + 1], coarse[1][k:k + 1]
        store(k * 16, c * fine[0] - s * fine[1], s * fine[0] + c * fine[1])


def place():
    return lax.axis_index("frow"), lax.axis_index("fcol")


def served():
    return lax.rem(place()[1], NR * NC)


def half_columns(cols_count, offsets, half, side, col_tab):
    bf16 = jnp.bfloat16
    col_index = place()[1]
    unit = sublanes(16)
    col_step = SKY // (cols_count * side)
    col_base = col_index * (SKY // cols_count)
    freq = [offsets[c] + half * HALF + lanes(HALF) for c in range(NC)]
    freq = jnp.concatenate(freq, 1)
    coarse = wave((col_base + 16 * col_step * sublanes(side // 16)) * freq)
    fine = wave((col_step * unit) * freq)

    def store(at, cos, sin):
        for c in range(NC):
            some = slice(c * HALF, (c + 1) * HALF)
            col_tab[at:at + 16, 2 * c * HALF:(2 * c + 1) * HALF] = cos[:, some].astype(bf16)
            col_tab[at:at + 16, (2 * c + 1) * HALF:(2 * c + 2) * HALF] = sin[:, some].astype(bf16)

    spread(coarse, fine, store)


def send_columns_kernel(cols_count, offsets, facet, subgrid, u, v, observed, send, vis, *scratch):
    col_tab, image, indices, seen, first, made, tail, sems = scratch
    f32, bf16 = jnp.float32, jnp.bfloat16
    side = facet.shape[0]
    pairs = [
        (offsets, first), (facet, image), (subgrid, indices.at[0]), (u, indices.at[1]), (v, indices.at[2]), (observed, seen),
    ]
    copies = [pltpu.make_async_copy(source, target, sems.at[n]) for n, (source, target) in enumerate(pairs)]
    for copy in copies:
        copy.start()
    copies[0].wait()
    half_columns(cols_count, first, 1 - place()[0] % 2, side, col_tab)
    for copy in copies[2:]:
        copy.wait()
    some = jnp.concatenate([indices[n].astype(f32) for n in range(3)] + [seen[...], jnp.zeros((3, side), f32)], 0)
    some = jnp.concatenate([some[:, :side // 2], some[:, side // 2:]], 0).astype(bf16)
    tail[:, :side // 2] = some
    tail[:, side // 2:] = some
    writes = [
        pltpu.make_async_copy(tail.at[:, pl.ds(0, side // 2)], vis, sems.at[6]),
        pltpu.make_async_copy(tail, send.at[pl.ds(side, 16)], sems.at[7]),
    ]
    for write in writes:
        write.start()
    copies[1].wait()
    step = side // 2
    for n in range(2):
        at = pl.ds(n * step, step)
        made[at] = jnp.dot(image[at], col_tab[...], preferred_element_type=f32).astype(bf16)
        write = pltpu.make_async_copy(made.at[at], send.at[at], sems.at[8 + n])
        write.start()
        writes.append(write)
    for write in writes:
        write.wait()


def own_tables_kernel(rows_count, cols_count, offsets, col_offsets, facet, own, row_tab, col_tab):
    bf16 = jnp.bfloat16
    row_index, _ = place()
    side = facet.shape[0]
    half_columns(cols_count, col_offsets, row_index % 2, side, col_tab)
    own[...] = jnp.dot(facet[...], col_tab[...], preferred_element_type=jnp.float32).astype(bf16)
    unit = sublanes(16)
    row_step = SKY // (rows_count * side)
    for f in range(2):
        pos = (row_index ^ f) * (SKY // rows_count) + row_step * lanes(side)
        fine = wave(unit * pos)
        for r in range(NR):
            coarse = wave((offsets[r] + 16 * unit) * pos)

            def store(at, cos, sin, r=r, f=f):
                row_tab[2 * r, at:at + 16, f * side:(f + 1) * side] = cos.astype(bf16)
                row_tab[2 * r + 1, at:at + 16, f * side:(f + 1) * side] = sin.astype(bf16)

            spread(coarse, fine, store)


def contribution_kernel(scale, number, own, own_vis, other, row_tab, out):
    f32, bf16 = jnp.float32, jnp.bfloat16
    side = own.shape[0]
    vis = []
    for some in (own_vis[...], other[side:]):
        vis += [some[:, k * LANES:(k + 1) * LANES] for k in range(side // 2 // LANES)]
    for k, some in enumerate(vis):
        at = 2 * SG + 16 * k
        out[at:at + 16] = some
    r, c = split_number(served() + number)
    at = pl.ds(pl.multiple_of(c * SG, SG), SG)
    right = jnp.concatenate([own[:, at], other[:side, at]], 0)
    with_cos = jnp.dot(row_tab[2 * r], right, preferred_element_type=f32)
    with_sin = jnp.dot(row_tab[2 * r + 1], right, preferred_element_type=f32)
    out[:SG] = ((with_cos[:, :HALF] - with_sin[:, HALF:]) * scale).astype(bf16)
    out[SG:2 * SG] = (-(with_cos[:, HALF:] + with_sin[:, :HALF]) * scale).astype(bf16)


def split_number(number):
    number = lax.rem(number, NR * NC)
    return number // NC, lax.rem(number, NC)


def vis_rows(block):
    count = block.shape[0] // 16
    return jnp.concatenate(
        [block[16 * k + 8 * part:16 * k + 8 * part + 8] for part in range(2) for k in range(count)], 1
    )


def grid_sums(parts):
    f32, bf16 = jnp.float32, jnp.bfloat16
    row_index, _ = place()
    chip = served().astype(f32)
    v_at = (sublanes(HALF) + (row_index % 2) * HALF).astype(f32)
    counter = sublanes(SG).astype(f32)
    total = jnp.zeros((SG, 3 * HALF), f32)
    planes = [jnp.zeros((SG, HALF), f32)] * 2
    for part in parts:
        one = vis_rows(part[2 * SG:].astype(f32))
        u_here = jnp.where(one[0:1] == chip, one[1:2], -1.0)
        hot = jnp.where(u_here == counter, 1.0, 0.0).astype(bf16)
        pick = one[2:3] == v_at
        right = jnp.concatenate(
            [jnp.where(pick, one[3:4], 0.0), jnp.where(pick, one[4:5], 0.0), jnp.where(pick, 1.0, 0.0)], 0
        ).astype(bf16)
        total = total + lax.dot_general(hot, right, (((1,), (1,)), ((), ())), preferred_element_type=f32)
        planes = [planes[p] + part[p * SG:(p + 1) * SG].astype(f32) for p in range(2)]
    return planes + [total[:, p * HALF:(p + 1) * HALF] for p in range(3)]


def first_sums_kernel(*refs):
    for p, plane in enumerate(grid_sums(refs[:-1])):
        refs[-1][p] = plane


def gridding_kernel(*refs):
    parts, (first, _, pieces, planes) = refs[:-4], refs[-4:]
    for p, plane in enumerate(grid_sums(parts)):
        planes[p] = first[p] + plane
    each = SG // pieces.shape[0]
    for j in range(pieces.shape[0]):
        rows = [planes[p, j * each:(j + 1) * each] for p in range(5)]
        pieces[j] = jnp.concatenate(rows, 0).astype(jnp.bfloat16)


def pieces_sum_kernel(pieces, out):
    f32, bf16 = jnp.float32, jnp.bfloat16
    total = pieces[0].astype(f32)
    for j in range(1, pieces.shape[0]):
        total = total + pieces[j].astype(f32)
    total = total.astype(bf16)
    for j in range(out.shape[0]):
        out[j] = total


def lay_out(pieces, half, planes, lanes_at):
    f32, bf16 = jnp.float32, jnp.bfloat16
    each = SG // pieces.shape[0]
    for j in range(pieces.shape[0]):
        some = pieces[j].astype(f32)
        for p in range(5):
            planes[p, j * each:(j + 1) * each, lanes_at] = some[p * each:(p + 1) * each]

    def step(forward):
        rows = [pl.ds(pl.multiple_of(p * SG + half * HALF, HALF), HALF) for p in range(2)]
        left = jnp.concatenate([planes[p, :, lanes_at].astype(bf16) for p in range(2)], 1)
        right = jnp.concatenate([forward[at] for at in rows], 0)
        return jnp.dot(left, right, preferred_element_type=f32)

    return step


def own_half_kernel(pieces, forward, out, wide, planes):
    wide[...] = lay_out(pieces, place()[0] % 2, planes, slice(0, HALF))(forward)
    out[...] = planes[2:]


def grids_kernel(chips, own, own_wide, other, *refs):
    f32, bf16 = jnp.float32, jnp.bfloat16
    parts, (grid_left, forward, inverse_left, inverse) = refs[:chips], refs[chips:chips + 4]
    outs, rest, (planes, cat, tall, hat) = refs[chips + 4:-5], refs[-5], refs[-4:]
    row_index, _ = place()
    core = row_index % 2
    chip = served().astype(f32)
    at = [pl.ds(pl.multiple_of(half * HALF, HALF), HALF) for half in (core, 1 - core)]
    wide = (own_wide[...] + lay_out(other, 1 - core, planes, at[1])(forward)).astype(bf16)
    for p in range(3):
        planes[2 + p, :, at[0]] = own[p]
    tall[:SG] = wide[:, :SG]
    tall[SG:] = wide[:, SG:]
    model = jnp.dot(grid_left[...], tall[...], preferred_element_type=f32) * (1.0 / SG)
    hat_real, hat_imag = model[:SG], model[SG:]
    cat[:, :SG] = (planes[2] - planes[4] * hat_real).astype(bf16)
    cat[:, SG:] = (planes[3] - planes[4] * hat_imag).astype(bf16)
    hat[:, :SG] = hat_real.astype(bf16)
    hat[:, SG:] = hat_imag.astype(bf16)
    wide = jnp.dot(cat[...], inverse[...], preferred_element_type=f32)
    for k in range(2):
        tall[k * SG:(k + 1) * SG] = wide[:, k * SG:(k + 1) * SG].astype(bf16)
    back = jnp.dot(inverse_left[...], tall[...], preferred_element_type=f32) * (1.0 / SG)
    rest[...] = jnp.where(core == 0, back[:, HALF:], back[:, :HALF]).astype(bf16)
    back = jnp.where(core == 0, back[:, :HALF], back[:, HALF:]).astype(bf16)
    counter = sublanes(SG).astype(f32)
    vis_each = (parts[0].shape[0] - 2 * SG) // 2
    for k, out in enumerate(outs):
        out[:2 * SG] = back
        ask = vis_rows(parts[-k % chips][2 * SG:2 * SG + vis_each].astype(f32))
        u_here = jnp.where(ask[0:1] == chip, ask[1:2], -1.0)
        hot = jnp.where(u_here == counter, 1.0, 0.0).astype(bf16)
        pick = ask[2:3] == counter
        line = lax.dot_general(hat[...], hot, (((0,), (0,)), ((), ())), preferred_element_type=f32)
        rows = []
        for part in range(2):
            value = jnp.sum(jnp.where(pick, line[part * SG:(part + 1) * SG], 0.0), axis=0, keepdims=True)
            rows += [value[:, i * LANES:(i + 1) * LANES] for i in range(value.shape[1] // LANES)]
        rows.append(jnp.zeros((16 - len(rows), LANES), f32))
        out[2 * SG:] = jnp.concatenate(rows, 0).astype(bf16)


def back_tables_kernel(rows_count, cols_count, side, offsets_row, offsets_col, row_tab, col_tab):
    bf16 = jnp.bfloat16
    row_index, col_index = place()
    unit = sublanes(16)
    row_step = SKY // (rows_count * side)
    row_base = row_index * (SKY // rows_count)
    for r in range(NR):
        freq = offsets_row[r] + lanes(SG)
        coarse = wave((row_base + 16 * row_step * sublanes(side // 16)) * freq)
        fine = wave((row_step * unit) * freq)

        def store(at, cos, sin, r=r):
            row_tab[at:at + 16, 2 * r * SG:(2 * r + 1) * SG] = cos.astype(bf16)
            row_tab[at:at + 16, (2 * r + 1) * SG:(2 * r + 2) * SG] = sin.astype(bf16)

        spread(coarse, fine, store)
    col_step = SKY // (cols_count * side)
    pos = col_index * (SKY // cols_count) + col_step * lanes(side)
    fine = wave(unit * pos)
    for c in range(NC):
        coarse = wave((offsets_col[c] + 16 * unit) * pos)

        def store(at, cos, sin, c=c):
            left = (2 * c + at // HALF) * 2 * HALF + at % HALF
            col_tab[left:left + 16] = cos.astype(bf16)
            col_tab[left + HALF:left + HALF + 16] = (-sin).astype(bf16)

        spread(coarse, fine, store)


def block_part(block, number, row_tab):
    r, _ = split_number(number)
    real, imag = block[:SG], block[SG:2 * SG]
    right = jnp.concatenate([jnp.concatenate([real, imag], 1), jnp.concatenate([-imag, real], 1)], 0)
    left = row_tab[:, pl.ds(pl.multiple_of(2 * r * SG, 2 * SG), 2 * SG)]
    return jnp.dot(left, right, preferred_element_type=jnp.float32)


def first_part_kernel(own, rest, row_tab, out):
    chip = served()
    for n, block in enumerate((own, rest)):
        out[:, n * SG:(n + 1) * SG] = block_part(block, chip, row_tab)


def column_rows(number):
    depth = 2 * SG
    return pl.ds(pl.multiple_of(split_number(number)[1] * depth, depth), depth)


def half_lanes(n):
    half = place()[0] % 2
    return pl.ds(pl.multiple_of((half if n == 0 else 1 - half) * SG, SG), SG)


def own_column_kernel(chips, opposite, own, rest, first, row_tab, col_tab, out, both):
    chip = served()
    for n, block in enumerate((own, rest)):
        part = first[:, n * SG:(n + 1) * SG] + block_part(block, chip + chips - opposite, row_tab)
        both[:, half_lanes(n)] = part.astype(jnp.bfloat16)
    out[...] = jnp.dot(both[...], col_tab[column_rows(chip)], preferred_element_type=jnp.float32)


def image_kernel(scale, chips, *refs):
    f32, bf16 = jnp.float32, jnp.bfloat16
    blocks, others, refs = refs[:chips], refs[chips:chips + 2], refs[chips + 2:]
    first, row_tab, col_tab, observed, out, residual, both, image, seen, sems = refs
    chip = served()
    model = jnp.zeros((16, LANES), f32)
    for block in blocks:
        model = model + block[2 * SG:].astype(f32)
    count = observed.shape[1] // LANES
    for part in range(2):
        for i in range(count):
            at = slice(i * LANES, (i + 1) * LANES)
            seen[part:part + 1, at] = observed[part:part + 1, at] - model[part * count + i:part * count + i + 1]
    writes = [pltpu.make_async_copy(seen, residual, sems.at[0])]
    writes[0].start()
    for n, pair in enumerate(((blocks[1], blocks[3]), others)):
        part = block_part(pair[0], chip + chips - 1, row_tab) + block_part(pair[1], chip + chips - 3, row_tab)
        both[:, half_lanes(n)] = part.astype(bf16)
    chunks = sems.shape[0] - 1
    step = image.shape[0] // chunks
    for n in range(chunks):
        at = slice(n * step, (n + 1) * step)
        part = jnp.dot(both[at], col_tab[column_rows(chip + 1)], preferred_element_type=f32)
        image[at] = (first[at] + part) * scale
        write = pltpu.make_async_copy(image.at[at], out.at[at], sems.at[1 + n])
        write.start()
        writes.append(write)
    for write in writes:
        write.wait()


def call(kernel, out_shape, name, spaces, scratch=(), cost=0, outs=None, room=24):
    kinds = {"s": pltpu.SMEM, "v": pltpu.VMEM, "a": pl.ANY}
    several = isinstance(out_shape, tuple)
    outs = outs or "v" * (len(out_shape) if several else 1)
    out_specs = tuple(pl.BlockSpec(memory_space=kinds[kind]) for kind in outs)
    return pl.pallas_call(
        kernel,
        out_shape=out_shape,
        in_specs=[pl.BlockSpec(memory_space=kinds[kind]) for kind in spaces],
        out_specs=out_specs if several else out_specs[0],
        scratch_shapes=list(scratch),
        compiler_params=pltpu.CompilerParams(vmem_limit_bytes=room * 2**20),
        cost_estimate=pl.CostEstimate(flops=cost, bytes_accessed=2**20, transcendentals=0),
        name=name,
    )


def grid_tables():
    counter = np.arange(SG)
    angles = (counter[:, None] * counter[None, :] % SG).astype(np.float64) * (2.0 * math.pi / SG)
    return np.cos(angles).astype(ml_dtypes.bfloat16), np.sin(angles).astype(ml_dtypes.bfloat16)


def exchange(blocks, axes, groups):
    return lax.all_to_all(blocks, axes, 0, 0, tiled=True, axis_index_groups=groups)


def shape(*dims, dtype=jnp.bfloat16):
    return jax.ShapeDtypeStruct(dims, dtype)


def shards(facet, row_offsets, col_offsets, vis_subgrid, vis_u, vis_v, observed):
    f32, bf16 = jnp.float32, jnp.bfloat16
    rows_count, cols_count = lax.axis_size("frow"), lax.axis_size("fcol")
    side = facet.shape[0]
    n_vis = vis_u.shape[0]
    chips = rows_count // 2
    each = SG // cols_count
    swap = [(index, index ^ 1) for index in range(rows_count)]
    line = NR * NC

    turns = [
        [(col, col // line * line + (col + k) % line) for col in range(cols_count)] for k in range(line)
    ]
    groups = [
        [(2 * chip + core) * cols_count + far * line + number for far in range(cols_count // line) for chip in range(chips)]
        for number in range(line) for core in range(2)
    ]

    def turned(blocks):
        moved = {k: lax.ppermute(blocks[k], "fcol", turns[k]) for k in (2, 1, 3)}
        return [blocks[0]] + [moved[k] for k in range(1, chips)]

    scale_in = 1.0 / (side * math.sqrt(rows_count * cols_count))
    scale_out = 1.0 / (SG * math.sqrt(NR * NC))
    flat = (1, n_vis)

    send, vis = call(
        functools.partial(send_columns_kernel, cols_count), (shape(side + 16, 4 * HALF), shape(16, n_vis // 2)),
        "send_columns", "aaaaaa",
        scratch=[
            pltpu.VMEM((side, 4 * HALF), bf16), pltpu.VMEM((side, side), bf16), pltpu.VMEM((3,) + flat, jnp.int32),
            pltpu.VMEM((2, n_vis), f32), pltpu.SMEM((NC,), jnp.int32), pltpu.VMEM((side, 4 * HALF), bf16),
            pltpu.VMEM((16, n_vis), bf16), pltpu.SemaphoreType.DMA((10,)),
        ],
        cost=10**9, room=60, outs="aa",
    )(col_offsets, facet, vis_subgrid.reshape(flat), vis_u.reshape(flat), vis_v.reshape(flat), observed)
    other = lax.ppermute(send, "frow", swap)
    own, row_tab = call(
        functools.partial(own_tables_kernel, rows_count, cols_count),
        (shape(side, 4 * HALF), shape(4, SG, 2 * side)), "own_tables", "ssv",
        scratch=[pltpu.VMEM((side, 4 * HALF), bf16)], cost=10**9,
    )(row_offsets, col_offsets, facet)
    vis_rows_count = 8 * 2 * n_vis // LANES
    parts = {}
    for k in (2, 1, 3, 0):
        parts[k] = call(
            functools.partial(contribution_kernel, scale_in, k), shape(2 * SG + vis_rows_count, HALF), "contribution",
            "vvvv", cost=5 * 10**8,
        )(own, vis, other, row_tab)
        own, parts[k] = lax.optimization_barrier((own, parts[k]))
    parts = turned(parts)

    sums = call(first_sums_kernel, shape(5, SG, HALF, dtype=f32), "first_sums", "vv", cost=10**9)(parts[0], parts[2])
    back_row, back_col = call(
        functools.partial(back_tables_kernel, rows_count, cols_count, side),
        (shape(side, 4 * SG), shape(4 * SG, side)), "back_tables", "ss", cost=10**9,
    )(row_offsets, col_offsets)
    pieces = call(
        gridding_kernel, shape(cols_count, 5 * each, HALF), "gridding", "v" * (chips - 1) + "a",
        scratch=[pltpu.VMEM((5, SG, HALF), f32)], cost=10**9,
    )(parts[1], parts[3], sums, back_col)
    pieces = exchange(pieces, BOTH, groups)
    pieces = call(pieces_sum_kernel, shape(cols_count, 5 * each, HALF), "pieces_sum", "v", cost=10**6)(pieces)
    pieces = exchange(pieces, BOTH, groups)
    pieces_other = lax.ppermute(pieces, "frow", swap)

    kcos, ksin = grid_tables()
    block = [np.concatenate(pair, 1) for pair in ((kcos, ksin), (-ksin, kcos), (kcos, -ksin), (ksin, kcos))]
    forward_block = np.concatenate([block[0], block[1]], 0)
    inverse_block = np.concatenate([block[2], block[3]], 0)
    own_planes, own_wide = call(
        own_half_kernel, (shape(3, SG, HALF, dtype=f32), shape(SG, 2 * SG, dtype=f32)), "own_half", "vv",
        scratch=[pltpu.VMEM((5, SG, HALF), f32)], cost=10**9,
    )(pieces, forward_block)
    *back, rest = call(
        functools.partial(grids_kernel, chips), (shape(2 * SG + 16, HALF),) * chips + (shape(2 * SG, HALF),), "grids",
        "v" * (7 + chips),
        scratch=[
            pltpu.VMEM((5, SG, SG), f32), pltpu.VMEM((SG, 2 * SG), bf16), pltpu.VMEM((2 * SG, SG), bf16),
            pltpu.VMEM((SG, 2 * SG), bf16),
        ],
        cost=10**9,
    )(own_planes, own_wide, pieces_other, *parts, inverse_block, forward_block, forward_block, inverse_block)
    back = turned(back)

    both = pltpu.VMEM((side, 2 * SG), bf16)
    square = shape(side, side, dtype=f32)
    first = call(first_part_kernel, square, "first_part", "vvv", cost=10**9)(back[0], rest, back_row)
    back[2], first = lax.optimization_barrier((back[2], first))
    rest = {k: lax.ppermute(back[k], "frow", swap) for k in (2, 1, 3)}
    first = call(
        functools.partial(own_column_kernel, chips, 2), square, "own_column", "v" * 5, scratch=[both], cost=10**9
    )(back[2], rest[2], first, back_row, back_col)
    return call(
        functools.partial(image_kernel, scale_out, chips), (square, shape(2, n_vis, dtype=f32)), "image",
        "v" * (chips + 6), outs="aa",
        scratch=[both, pltpu.VMEM((side, side), f32), pltpu.VMEM((2, n_vis), f32), pltpu.SemaphoreType.DMA((5,))],
        cost=10**9,
    )(*back, rest[1], rest[3], first, back_row, back_col, observed)


def solution(mesh):
    in_specs = (
        P("frow", "fcol"),
        P(),
        P(),
        P(("frow", "fcol")),
        P(("frow", "fcol")),
        P(("frow", "fcol")),
        P(None, ("frow", "fcol")),
    )
    out_specs = (P("frow", "fcol"), P(None, ("frow", "fcol")))
    return jax.shard_map(shards, mesh=mesh, in_specs=in_specs, out_specs=out_specs, check_vma=False)
```

```python
import functools
import math

import jax
import jax.numpy as jnp
import ml_dtypes
import numpy as np
from jax import lax
from jax.experimental import pallas as pl
from jax.experimental.pallas import tpu as pltpu
from jax.sharding import PartitionSpec as P

SKY = 65536
SG = 256
NR = 2
NC = 2
HALF = SG // 2
LANES = 128


def wave(count):
    count = count & (SKY - 1)
    turned = count + SKY // 8
    near = (turned & (SKY // 4 - 1)) - SKY // 8
    quarter = lax.shift_right_logical(turned, 14) & 3
    t = near.astype(jnp.float32) * (2.0 * math.pi / SKY)
    q = t * t
    sin = t * (1.0 + q * (-1.0 / 6 + q * (1.0 / 120 + q * (-1.0 / 5040 + q * (1.0 / 362880)))))
    cos = 1.0 + q * (-0.5 + q * (1.0 / 24 + q * (-1.0 / 720 + q * (1.0 / 40320))))
    odd = (quarter & 1) == 1
    one, two = jnp.where(odd, sin, cos), jnp.where(odd, cos, sin)
    return (
        jnp.where((quarter == 1) | (quarter == 2), -one, one),
        jnp.where(quarter >= 2, -two, two),
    )


def lanes(n):
    return lax.broadcasted_iota(jnp.int32, (1, n), 1)


def sublanes(n):
    return lax.broadcasted_iota(jnp.int32, (n, 1), 0)


def spread(coarse, fine, store):
    for k in range(coarse[0].shape[0]):
        c, s = coarse[0][k:k + 1], coarse[1][k:k + 1]
        store(k * 16, c * fine[0] - s * fine[1], s * fine[0] + c * fine[1])


def place():
    return lax.axis_index("frow"), lax.axis_index("fcol")


def half_columns(cols_count, offsets, half, side, col_tab):
    bf16 = jnp.bfloat16
    col_index = place()[1]
    unit = sublanes(16)
    col_step = SKY // (cols_count * side)
    col_base = col_index * (SKY // cols_count)
    freq = [offsets[c] + half * HALF + lanes(HALF) for c in range(NC)]
    freq = jnp.concatenate(freq, 1)
    coarse = wave((col_base + 16 * col_step * sublanes(side // 16)) * freq)
    fine = wave((col_step * unit) * freq)

    def store(at, cos, sin):
        for c in range(NC):
            some = slice(c * HALF, (c + 1) * HALF)
            col_tab[at:at + 16, 2 * c * HALF:(2 * c + 1) * HALF] = cos[:, some].astype(bf16)
            col_tab[at:at + 16, (2 * c + 1) * HALF:(2 * c + 2) * HALF] = sin[:, some].astype(bf16)

    spread(coarse, fine, store)


def send_columns_kernel(cols_count, offsets, facet, subgrid, u, v, observed, send, vis, *scratch):
    col_tab, image, indices, seen, first, made, tail, sems = scratch
    f32, bf16 = jnp.float32, jnp.bfloat16
    side = facet.shape[0]
    pairs = [
        (offsets, first), (facet, image), (subgrid, indices.at[0]), (u, indices.at[1]), (v, indices.at[2]), (observed, seen),
    ]
    copies = [pltpu.make_async_copy(source, target, sems.at[n]) for n, (source, target) in enumerate(pairs)]
    for copy in copies:
        copy.start()
    copies[0].wait()
    half_columns(cols_count, first, 1 - place()[0] % 2, side, col_tab)
    for copy in copies[2:]:
        copy.wait()
    some = jnp.concatenate([indices[n].astype(f32) for n in range(3)] + [seen[...], jnp.zeros((3, side), f32)], 0)
    some = jnp.concatenate([some[:, :side // 2], some[:, side // 2:]], 0).astype(bf16)
    tail[:, :side // 2] = some
    tail[:, side // 2:] = some
    writes = [
        pltpu.make_async_copy(tail.at[:, pl.ds(0, side // 2)], vis, sems.at[6]),
        pltpu.make_async_copy(tail, send.at[pl.ds(side, 16)], sems.at[7]),
    ]
    for write in writes:
        write.start()
    copies[1].wait()
    step = side // 2
    for n in range(2):
        at = pl.ds(n * step, step)
        made[at] = jnp.dot(image[at], col_tab[...], preferred_element_type=f32).astype(bf16)
        write = pltpu.make_async_copy(made.at[at], send.at[at], sems.at[8 + n])
        write.start()
        writes.append(write)
    for write in writes:
        write.wait()


def own_tables_kernel(rows_count, cols_count, offsets, col_offsets, facet, own, row_tab, col_tab):
    bf16 = jnp.bfloat16
    row_index, _ = place()
    side = facet.shape[0]
    half_columns(cols_count, col_offsets, row_index % 2, side, col_tab)
    own[...] = jnp.dot(facet[...], col_tab[...], preferred_element_type=jnp.float32).astype(bf16)
    unit = sublanes(16)
    row_step = SKY // (rows_count * side)
    for f in range(2):
        pos = (row_index ^ f) * (SKY // rows_count) + row_step * lanes(side)
        fine = wave(unit * pos)
        for r in range(NR):
            coarse = wave((offsets[r] + 16 * unit) * pos)

            def store(at, cos, sin, r=r, f=f):
                row_tab[2 * r, at:at + 16, f * side:(f + 1) * side] = cos.astype(bf16)
                row_tab[2 * r + 1, at:at + 16, f * side:(f + 1) * side] = sin.astype(bf16)

            spread(coarse, fine, store)


def contribution_kernel(scale, number, own, own_vis, other, row_tab, out):
    f32, bf16 = jnp.float32, jnp.bfloat16
    side = own.shape[0]
    vis = []
    for some in (own_vis[...], other[side:]):
        vis += [some[:, k * LANES:(k + 1) * LANES] for k in range(side // 2 // LANES)]
    for k, some in enumerate(vis):
        at = 2 * SG + 16 * k
        out[at:at + 16] = some
    r, c = split_number(place()[0] // 2 + number)
    at = pl.ds(pl.multiple_of(c * SG, SG), SG)
    right = jnp.concatenate([own[:, at], other[:side, at]], 0)
    with_cos = jnp.dot(row_tab[2 * r], right, preferred_element_type=f32)
    with_sin = jnp.dot(row_tab[2 * r + 1], right, preferred_element_type=f32)
    out[:SG] = ((with_cos[:, :HALF] - with_sin[:, HALF:]) * scale).astype(bf16)
    out[SG:2 * SG] = (-(with_cos[:, HALF:] + with_sin[:, :HALF]) * scale).astype(bf16)


def split_number(number):
    number = lax.rem(number, NR * NC)
    return number // NC, lax.rem(number, NC)


def vis_rows(block):
    count = block.shape[0] // 16
    return jnp.concatenate(
        [block[16 * k + 8 * part:16 * k + 8 * part + 8] for part in range(2) for k in range(count)], 1
    )


def grid_sums(parts):
    f32, bf16 = jnp.float32, jnp.bfloat16
    row_index, _ = place()
    chip = (row_index // 2).astype(f32)
    v_at = (sublanes(HALF) + (row_index % 2) * HALF).astype(f32)
    counter = sublanes(SG).astype(f32)
    total = jnp.zeros((SG, 3 * HALF), f32)
    planes = [jnp.zeros((SG, HALF), f32)] * 2
    for part in parts:
        one = vis_rows(part[2 * SG:].astype(f32))
        u_here = jnp.where(one[0:1] == chip, one[1:2], -1.0)
        hot = jnp.where(u_here == counter, 1.0, 0.0).astype(bf16)
        pick = one[2:3] == v_at
        right = jnp.concatenate(
            [jnp.where(pick, one[3:4], 0.0), jnp.where(pick, one[4:5], 0.0), jnp.where(pick, 1.0, 0.0)], 0
        ).astype(bf16)
        total = total + lax.dot_general(hot, right, (((1,), (1,)), ((), ())), preferred_element_type=f32)
        planes = [planes[p] + part[p * SG:(p + 1) * SG].astype(f32) for p in range(2)]
    return planes + [total[:, p * HALF:(p + 1) * HALF] for p in range(3)]


def first_sums_kernel(*refs):
    for p, plane in enumerate(grid_sums(refs[:-1])):
        refs[-1][p] = plane


def gridding_kernel(*refs):
    parts, (first, _, pieces, planes) = refs[:-4], refs[-4:]
    for p, plane in enumerate(grid_sums(parts)):
        planes[p] = first[p] + plane
    each = SG // pieces.shape[0]
    for j in range(pieces.shape[0]):
        rows = [planes[p, j * each:(j + 1) * each] for p in range(5)]
        pieces[j] = jnp.concatenate(rows, 0).astype(jnp.bfloat16)


def pieces_sum_kernel(pieces, out):
    f32, bf16 = jnp.float32, jnp.bfloat16
    total = pieces[0].astype(f32)
    for j in range(1, pieces.shape[0]):
        total = total + pieces[j].astype(f32)
    total = total.astype(bf16)
    for j in range(out.shape[0]):
        out[j] = total


def lay_out(pieces, half, planes, lanes_at):
    f32, bf16 = jnp.float32, jnp.bfloat16
    each = SG // pieces.shape[0]
    for j in range(pieces.shape[0]):
        some = pieces[j].astype(f32)
        for p in range(5):
            planes[p, j * each:(j + 1) * each, lanes_at] = some[p * each:(p + 1) * each]

    def step(forward):
        rows = [pl.ds(pl.multiple_of(p * SG + half * HALF, HALF), HALF) for p in range(2)]
        left = jnp.concatenate([planes[p, :, lanes_at].astype(bf16) for p in range(2)], 1)
        right = jnp.concatenate([forward[at] for at in rows], 0)
        return jnp.dot(left, right, preferred_element_type=f32)

    return step


def asked(part):
    each = (part.shape[0] - 2 * SG) // 2
    return vis_rows(part[2 * SG:2 * SG + each].astype(jnp.float32))


def own_half_kernel(chips, pieces, forward, *refs):
    parts, (out, wide, hots, planes) = refs[:chips], refs[chips:]
    chip = (place()[0] // 2).astype(jnp.float32)
    counter = sublanes(SG).astype(jnp.float32)
    for k in range(chips):
        ask = asked(parts[-k % chips])
        u_here = jnp.where(ask[0:1] == chip, ask[1:2], -1.0)
        hots[k] = jnp.where(u_here == counter, 1.0, 0.0).astype(jnp.bfloat16)
    wide[...] = lay_out(pieces, place()[0] % 2, planes, slice(0, HALF))(forward)
    out[...] = planes[2:]


def grids_kernel(chips, own, own_wide, hots, other, *refs):
    f32, bf16 = jnp.float32, jnp.bfloat16
    parts, (grid_left, forward, inverse_left, inverse) = refs[:chips], refs[chips:chips + 4]
    outs, rest, (planes, cat, tall, hat) = refs[chips + 4:-5], refs[-5], refs[-4:]
    row_index, _ = place()
    core = row_index % 2
    at = [pl.ds(pl.multiple_of(half * HALF, HALF), HALF) for half in (core, 1 - core)]
    wide = (own_wide[...] + lay_out(other, 1 - core, planes, at[1])(forward)).astype(bf16)
    for p in range(3):
        planes[2 + p, :, at[0]] = own[p]
    tall[:SG] = wide[:, :SG]
    tall[SG:] = wide[:, SG:]
    model = jnp.dot(grid_left[...], tall[...], preferred_element_type=f32) * (1.0 / SG)
    hat_real, hat_imag = model[:SG], model[SG:]
    cat[:, :SG] = (planes[2] - planes[4] * hat_real).astype(bf16)
    cat[:, SG:] = (planes[3] - planes[4] * hat_imag).astype(bf16)
    hat[:, :SG] = hat_real.astype(bf16)
    hat[:, SG:] = hat_imag.astype(bf16)
    wide = jnp.dot(cat[...], inverse[...], preferred_element_type=f32)
    for k in range(2):
        tall[k * SG:(k + 1) * SG] = wide[:, k * SG:(k + 1) * SG].astype(bf16)
    back = jnp.dot(inverse_left[...], tall[...], preferred_element_type=f32) * (1.0 / SG)
    rest[...] = jnp.where(core == 0, back[:, HALF:], back[:, :HALF]).astype(bf16)
    back = jnp.where(core == 0, back[:, :HALF], back[:, HALF:]).astype(bf16)
    counter = sublanes(SG).astype(f32)
    for k, out in enumerate(outs):
        out[:2 * SG] = back
        ask = asked(parts[-k % chips])
        pick = ask[2:3] == counter
        line = lax.dot_general(hat[...], hots[k], (((0,), (0,)), ((), ())), preferred_element_type=f32)
        rows = []
        for part in range(2):
            value = jnp.sum(jnp.where(pick, line[part * SG:(part + 1) * SG], 0.0), axis=0, keepdims=True)
            rows += [value[:, i * LANES:(i + 1) * LANES] for i in range(value.shape[1] // LANES)]
        rows.append(jnp.zeros((16 - len(rows), LANES), f32))
        out[2 * SG:] = jnp.concatenate(rows, 0).astype(bf16)


def back_tables_kernel(rows_count, cols_count, side, offsets_row, offsets_col, row_tab, col_tab):
    bf16 = jnp.bfloat16
    row_index, col_index = place()
    unit = sublanes(16)
    row_step = SKY // (rows_count * side)
    row_base = row_index * (SKY // rows_count)
    for r in range(NR):
        freq = offsets_row[r] + lanes(SG)
        coarse = wave((row_base + 16 * row_step * sublanes(side // 16)) * freq)
        fine = wave((row_step * unit) * freq)

        def store(at, cos, sin, r=r):
            row_tab[at:at + 16, 2 * r * SG:(2 * r + 1) * SG] = cos.astype(bf16)
            row_tab[at:at + 16, (2 * r + 1) * SG:(2 * r + 2) * SG] = sin.astype(bf16)

        spread(coarse, fine, store)
    col_step = SKY // (cols_count * side)
    pos = col_index * (SKY // cols_count) + col_step * lanes(side)
    fine = wave(unit * pos)
    for c in range(NC):
        coarse = wave((offsets_col[c] + 16 * unit) * pos)

        def store(at, cos, sin, c=c):
            left = (2 * c + at // HALF) * 2 * HALF + at % HALF
            col_tab[left:left + 16] = cos.astype(bf16)
            col_tab[left + HALF:left + HALF + 16] = (-sin).astype(bf16)

        spread(coarse, fine, store)


def block_part(block, number, row_tab):
    r, _ = split_number(number)
    real, imag = block[:SG], block[SG:2 * SG]
    right = jnp.concatenate([jnp.concatenate([real, imag], 1), jnp.concatenate([-imag, real], 1)], 0)
    left = row_tab[:, pl.ds(pl.multiple_of(2 * r * SG, 2 * SG), 2 * SG)]
    return jnp.dot(left, right, preferred_element_type=jnp.float32)


def first_part_kernel(own, rest, row_tab, out):
    chip = place()[0] // 2
    for n, block in enumerate((own, rest)):
        out[:, n * SG:(n + 1) * SG] = block_part(block, chip, row_tab)


def column_rows(number):
    depth = 2 * SG
    return pl.ds(pl.multiple_of(split_number(number)[1] * depth, depth), depth)


def half_lanes(n):
    half = place()[0] % 2
    return pl.ds(pl.multiple_of((half if n == 0 else 1 - half) * SG, SG), SG)


def own_column_kernel(chips, opposite, own, rest, first, row_tab, col_tab, out, both):
    chip = place()[0] // 2
    for n, block in enumerate((own, rest)):
        part = first[:, n * SG:(n + 1) * SG] + block_part(block, chip + chips - opposite, row_tab)
        both[:, half_lanes(n)] = part.astype(jnp.bfloat16)
    out[...] = jnp.dot(both[...], col_tab[column_rows(chip)], preferred_element_type=jnp.float32)


def image_kernel(scale, chips, *refs):
    f32, bf16 = jnp.float32, jnp.bfloat16
    blocks, others, refs = refs[:chips], refs[chips:chips + 2], refs[chips + 2:]
    first, row_tab, col_tab, observed, out, residual, both, image, seen, sems = refs
    chip = place()[0] // 2
    model = jnp.zeros((16, LANES), f32)
    for block in blocks:
        model = model + block[2 * SG:].astype(f32)
    count = observed.shape[1] // LANES
    for part in range(2):
        for i in range(count):
            at = slice(i * LANES, (i + 1) * LANES)
            seen[part:part + 1, at] = observed[part:part + 1, at] - model[part * count + i:part * count + i + 1]
    writes = [pltpu.make_async_copy(seen, residual, sems.at[0])]
    writes[0].start()
    for n, pair in enumerate(((blocks[1], blocks[3]), others)):
        part = block_part(pair[0], chip + chips - 1, row_tab) + block_part(pair[1], chip + chips - 3, row_tab)
        both[:, half_lanes(n)] = part.astype(bf16)
    chunks = sems.shape[0] - 1
    step = image.shape[0] // chunks
    for n in range(chunks):
        at = slice(n * step, (n + 1) * step)
        part = jnp.dot(both[at], col_tab[column_rows(chip + 1)], preferred_element_type=f32)
        image[at] = (first[at] + part) * scale
        write = pltpu.make_async_copy(image.at[at], out.at[at], sems.at[1 + n])
        write.start()
        writes.append(write)
    for write in writes:
        write.wait()


def call(kernel, out_shape, name, spaces, scratch=(), cost=0, outs=None, room=24):
    kinds = {"s": pltpu.SMEM, "v": pltpu.VMEM, "a": pl.ANY}
    several = isinstance(out_shape, tuple)
    outs = outs or "v" * (len(out_shape) if several else 1)
    out_specs = tuple(pl.BlockSpec(memory_space=kinds[kind]) for kind in outs)
    return pl.pallas_call(
        kernel,
        out_shape=out_shape,
        in_specs=[pl.BlockSpec(memory_space=kinds[kind]) for kind in spaces],
        out_specs=out_specs if several else out_specs[0],
        scratch_shapes=list(scratch),
        compiler_params=pltpu.CompilerParams(vmem_limit_bytes=room * 2**20),
        cost_estimate=pl.CostEstimate(flops=cost, bytes_accessed=2**20, transcendentals=0),
        name=name,
    )


def grid_tables():
    counter = np.arange(SG)
    angles = (counter[:, None] * counter[None, :] % SG).astype(np.float64) * (2.0 * math.pi / SG)
    return np.cos(angles).astype(ml_dtypes.bfloat16), np.sin(angles).astype(ml_dtypes.bfloat16)


def exchange(blocks, axes, groups):
    return lax.all_to_all(blocks, axes, 0, 0, tiled=True, axis_index_groups=groups)


def shape(*dims, dtype=jnp.bfloat16):
    return jax.ShapeDtypeStruct(dims, dtype)


def shards(facet, row_offsets, col_offsets, vis_subgrid, vis_u, vis_v, observed):
    f32, bf16 = jnp.float32, jnp.bfloat16
    rows_count, cols_count = lax.axis_size("frow"), lax.axis_size("fcol")
    side = facet.shape[0]
    n_vis = vis_u.shape[0]
    chips = rows_count // 2
    each = SG // cols_count
    swap = [(index, index ^ 1) for index in range(rows_count)]
    turns = [[(index, (index + 2 * k) % rows_count) for index in range(rows_count)] for k in range(chips)]

    def turned(blocks):
        moved = {k: lax.ppermute(blocks[k], "frow", turns[k]) for k in (2, 1, 3)}
        return [blocks[0]] + [moved[k] for k in range(1, chips)]

    scale_in = 1.0 / (side * math.sqrt(rows_count * cols_count))
    scale_out = 1.0 / (SG * math.sqrt(NR * NC))
    line = (1, n_vis)

    send, vis = call(
        functools.partial(send_columns_kernel, cols_count), (shape(side + 16, 4 * HALF), shape(16, n_vis // 2)),
        "send_columns", "aaaaaa",
        scratch=[
            pltpu.VMEM((side, 4 * HALF), bf16), pltpu.VMEM((side, side), bf16), pltpu.VMEM((3,) + line, jnp.int32),
            pltpu.VMEM((2, n_vis), f32), pltpu.SMEM((NC,), jnp.int32), pltpu.VMEM((side, 4 * HALF), bf16),
            pltpu.VMEM((16, n_vis), bf16), pltpu.SemaphoreType.DMA((10,)),
        ],
        cost=10**9, room=60, outs="aa",
    )(col_offsets, facet, vis_subgrid.reshape(line), vis_u.reshape(line), vis_v.reshape(line), observed)
    other = lax.ppermute(send, "frow", swap)
    own, row_tab = call(
        functools.partial(own_tables_kernel, rows_count, cols_count),
        (shape(side, 4 * HALF), shape(4, SG, 2 * side)), "own_tables", "ssv",
        scratch=[pltpu.VMEM((side, 4 * HALF), bf16)], cost=10**9,
    )(row_offsets, col_offsets, facet)
    vis_rows_count = 8 * 2 * n_vis // LANES
    parts = {}
    for k in (2, 1, 3, 0):
        parts[k] = call(
            functools.partial(contribution_kernel, scale_in, k), shape(2 * SG + vis_rows_count, HALF), "contribution",
            "vvvv", cost=5 * 10**8,
        )(own, vis, other, row_tab)
    parts = turned(parts)

    sums = call(first_sums_kernel, shape(5, SG, HALF, dtype=f32), "first_sums", "vv", cost=10**9)(parts[0], parts[2])
    back_row, back_col = call(
        functools.partial(back_tables_kernel, rows_count, cols_count, side),
        (shape(side, 4 * SG), shape(4 * SG, side)), "back_tables", "ss", cost=10**9,
    )(row_offsets, col_offsets)
    pieces = call(
        gridding_kernel, shape(cols_count, 5 * each, HALF), "gridding", "v" * (chips - 1) + "a",
        scratch=[pltpu.VMEM((5, SG, HALF), f32)], cost=10**9,
    )(parts[1], parts[3], sums, back_col)
    pieces = exchange(pieces, "fcol", None)
    pieces = call(pieces_sum_kernel, shape(cols_count, 5 * each, HALF), "pieces_sum", "v", cost=10**6)(pieces)
    pieces = exchange(pieces, "fcol", None)
    pieces_other = lax.ppermute(pieces, "frow", swap)

    kcos, ksin = grid_tables()
    block = [np.concatenate(pair, 1) for pair in ((kcos, ksin), (-ksin, kcos), (kcos, -ksin), (ksin, kcos))]
    forward_block = np.concatenate([block[0], block[1]], 0)
    inverse_block = np.concatenate([block[2], block[3]], 0)
    own_planes, own_wide, hots = call(
        functools.partial(own_half_kernel, chips),
        (shape(3, SG, HALF, dtype=f32), shape(SG, 2 * SG, dtype=f32), shape(chips, SG, n_vis)), "own_half", "vv" + "v" * chips,
        scratch=[pltpu.VMEM((5, SG, HALF), f32)], cost=10**9,
    )(pieces, forward_block, *parts)
    *back, rest = call(
        functools.partial(grids_kernel, chips), (shape(2 * SG + 16, HALF),) * chips + (shape(2 * SG, HALF),), "grids",
        "v" * (8 + chips),
        scratch=[
            pltpu.VMEM((5, SG, SG), f32), pltpu.VMEM((SG, 2 * SG), bf16), pltpu.VMEM((2 * SG, SG), bf16),
            pltpu.VMEM((SG, 2 * SG), bf16),
        ],
        cost=10**9,
    )(own_planes, own_wide, hots, pieces_other, *parts, inverse_block, forward_block, forward_block, inverse_block)
    back = turned(back)

    both = pltpu.VMEM((side, 2 * SG), bf16)
    square = shape(side, side, dtype=f32)
    first = call(first_part_kernel, square, "first_part", "vvv", cost=10**9)(back[0], rest, back_row)
    back[2], first = lax.optimization_barrier((back[2], first))
    rest = {k: lax.ppermute(back[k], "frow", swap) for k in (2, 1, 3)}
    first = call(
        functools.partial(own_column_kernel, chips, 2), square, "own_column", "v" * 5, scratch=[both], cost=10**9
    )(back[2], rest[2], first, back_row, back_col)
    return call(
        functools.partial(image_kernel, scale_out, chips), (square, shape(2, n_vis, dtype=f32)), "image",
        "v" * (chips + 6), outs="aa",
        scratch=[both, pltpu.VMEM((side, side), f32), pltpu.VMEM((2, n_vis), f32), pltpu.SemaphoreType.DMA((5,))],
        cost=10**9,
    )(*back, rest[1], rest[3], first, back_row, back_col, observed)


def solution(mesh):
    in_specs = (
        P("frow", "fcol"),
        P(),
        P(),
        P(("frow", "fcol")),
        P(("frow", "fcol")),
        P(("frow", "fcol")),
        P(None, ("frow", "fcol")),
    )
    out_specs = (P("frow", "fcol"), P(None, ("frow", "fcol")))
    return jax.shard_map(shards, mesh=mesh, in_specs=in_specs, out_specs=out_specs, check_vma=False)
```

```python
import functools
import math

import jax
import jax.numpy as jnp
import ml_dtypes
import numpy as np
from jax import lax
from jax.experimental import pallas as pl
from jax.experimental.pallas import tpu as pltpu
from jax.sharding import PartitionSpec as P

SKY = 65536
SG = 256
NR = 2
NC = 2
HALF = SG // 2
LANES = 128


def wave(count):
    count = count & (SKY - 1)
    turned = count + SKY // 8
    near = (turned & (SKY // 4 - 1)) - SKY // 8
    quarter = lax.shift_right_logical(turned, 14) & 3
    t = near.astype(jnp.float32) * (2.0 * math.pi / SKY)
    q = t * t
    sin = t * (1.0 + q * (-1.0 / 6 + q * (1.0 / 120 + q * (-1.0 / 5040 + q * (1.0 / 362880)))))
    cos = 1.0 + q * (-0.5 + q * (1.0 / 24 + q * (-1.0 / 720 + q * (1.0 / 40320))))
    odd = (quarter & 1) == 1
    one, two = jnp.where(odd, sin, cos), jnp.where(odd, cos, sin)
    return (
        jnp.where((quarter == 1) | (quarter == 2), -one, one),
        jnp.where(quarter >= 2, -two, two),
    )


def lanes(n):
    return lax.broadcasted_iota(jnp.int32, (1, n), 1)


def sublanes(n):
    return lax.broadcasted_iota(jnp.int32, (n, 1), 0)


def spread(coarse, fine, store):
    for k in range(coarse[0].shape[0]):
        c, s = coarse[0][k:k + 1], coarse[1][k:k + 1]
        store(k * 16, c * fine[0] - s * fine[1], s * fine[0] + c * fine[1])


def place():
    return lax.axis_index("frow"), lax.axis_index("fcol")


def half_columns(cols_count, offsets, half, side, col_tab):
    bf16 = jnp.bfloat16
    col_index = place()[1]
    unit = sublanes(16)
    col_step = SKY // (cols_count * side)
    col_base = col_index * (SKY // cols_count)
    freq = [offsets[c] + half * HALF + lanes(HALF) for c in range(NC)]
    freq = jnp.concatenate(freq, 1)
    coarse = wave((col_base + 16 * col_step * sublanes(side // 16)) * freq)
    fine = wave((col_step * unit) * freq)

    def store(at, cos, sin):
        for c in range(NC):
            some = slice(c * HALF, (c + 1) * HALF)
            col_tab[at:at + 16, 2 * c * HALF:(2 * c + 1) * HALF] = cos[:, some].astype(bf16)
            col_tab[at:at + 16, (2 * c + 1) * HALF:(2 * c + 2) * HALF] = sin[:, some].astype(bf16)

    spread(coarse, fine, store)


def send_columns_kernel(cols_count, offsets, facet, subgrid, u, v, observed, send, vis, *scratch):
    col_tab, image, indices, seen, first, made, tail, sems = scratch
    f32, bf16 = jnp.float32, jnp.bfloat16
    side = facet.shape[0]
    pairs = [
        (offsets, first), (facet, image), (subgrid, indices.at[0]), (u, indices.at[1]), (v, indices.at[2]), (observed, seen),
    ]
    copies = [pltpu.make_async_copy(source, target, sems.at[n]) for n, (source, target) in enumerate(pairs)]
    for copy in copies:
        copy.start()
    copies[0].wait()
    half_columns(cols_count, first, 1 - place()[0] % 2, side, col_tab)
    for copy in copies[2:]:
        copy.wait()
    some = jnp.concatenate([indices[n].astype(f32) for n in range(3)] + [seen[...], jnp.zeros((3, side), f32)], 0)
    some = jnp.concatenate([some[:, :side // 2], some[:, side // 2:]], 0).astype(bf16)
    tail[:, :side // 2] = some
    tail[:, side // 2:] = some
    writes = [
        pltpu.make_async_copy(tail.at[:, pl.ds(0, side // 2)], vis, sems.at[6]),
        pltpu.make_async_copy(tail, send.at[pl.ds(side, 16)], sems.at[7]),
    ]
    for write in writes:
        write.start()
    copies[1].wait()
    step = side // 2
    for n in range(2):
        at = pl.ds(n * step, step)
        made[at] = jnp.dot(image[at], col_tab[...], preferred_element_type=f32).astype(bf16)
        write = pltpu.make_async_copy(made.at[at], send.at[at], sems.at[8 + n])
        write.start()
        writes.append(write)
    for write in writes:
        write.wait()


def own_tables_kernel(rows_count, cols_count, offsets, col_offsets, facet, own, row_tab, col_tab):
    bf16 = jnp.bfloat16
    row_index, _ = place()
    side = facet.shape[0]
    half_columns(cols_count, col_offsets, row_index % 2, side, col_tab)
    own[...] = jnp.dot(facet[...], col_tab[...], preferred_element_type=jnp.float32).astype(bf16)
    unit = sublanes(16)
    row_step = SKY // (rows_count * side)
    for f in range(2):
        pos = (row_index ^ f) * (SKY // rows_count) + row_step * lanes(side)
        fine = wave(unit * pos)
        for r in range(NR):
            coarse = wave((offsets[r] + 16 * unit) * pos)

            def store(at, cos, sin, r=r, f=f):
                row_tab[2 * r, at:at + 16, f * side:(f + 1) * side] = cos.astype(bf16)
                row_tab[2 * r + 1, at:at + 16, f * side:(f + 1) * side] = sin.astype(bf16)

            spread(coarse, fine, store)


def contribution_kernel(scale, number, own, own_vis, other, row_tab, out):
    f32, bf16 = jnp.float32, jnp.bfloat16
    side = own.shape[0]
    vis = []
    for some in (own_vis[...], other[side:]):
        vis += [some[:, k * LANES:(k + 1) * LANES] for k in range(side // 2 // LANES)]
    for k, some in enumerate(vis):
        at = 2 * SG + 16 * k
        out[at:at + 16] = some
    r, c = split_number(place()[0] // 2 + number)
    at = pl.ds(pl.multiple_of(c * SG, SG), SG)
    right = jnp.concatenate([own[:, at], other[:side, at]], 0)
    with_cos = jnp.dot(row_tab[2 * r], right, preferred_element_type=f32)
    with_sin = jnp.dot(row_tab[2 * r + 1], right, preferred_element_type=f32)
    out[:SG] = ((with_cos[:, :HALF] - with_sin[:, HALF:]) * scale).astype(bf16)
    out[SG:2 * SG] = (-(with_cos[:, HALF:] + with_sin[:, :HALF]) * scale).astype(bf16)


def split_number(number):
    number = lax.rem(number, NR * NC)
    return number // NC, lax.rem(number, NC)


def vis_rows(block):
    count = block.shape[0] // 16
    return jnp.concatenate(
        [block[16 * k + 8 * part:16 * k + 8 * part + 8] for part in range(2) for k in range(count)], 1
    )


def grid_sums(parts):
    f32, bf16 = jnp.float32, jnp.bfloat16
    row_index, _ = place()
    chip = (row_index // 2).astype(f32)
    v_at = (sublanes(HALF) + (row_index % 2) * HALF).astype(f32)
    counter = sublanes(SG).astype(f32)
    total = jnp.zeros((SG, 3 * HALF), f32)
    planes = [jnp.zeros((SG, HALF), f32)] * 2
    for part in parts:
        one = vis_rows(part[2 * SG:].astype(f32))
        u_here = jnp.where(one[0:1] == chip, one[1:2], -1.0)
        hot = jnp.where(u_here == counter, 1.0, 0.0).astype(bf16)
        pick = one[2:3] == v_at
        right = jnp.concatenate(
            [jnp.where(pick, one[3:4], 0.0), jnp.where(pick, one[4:5], 0.0), jnp.where(pick, 1.0, 0.0)], 0
        ).astype(bf16)
        total = total + lax.dot_general(hot, right, (((1,), (1,)), ((), ())), preferred_element_type=f32)
        planes = [planes[p] + part[p * SG:(p + 1) * SG].astype(f32) for p in range(2)]
    return planes + [total[:, p * HALF:(p + 1) * HALF] for p in range(3)]


def first_sums_kernel(*refs):
    for p, plane in enumerate(grid_sums(refs[:-1])):
        refs[-1][p] = plane


def gridding_kernel(*refs):
    parts, (first, _, pieces, planes) = refs[:-4], refs[-4:]
    for p, plane in enumerate(grid_sums(parts)):
        planes[p] = first[p] + plane
    each = SG // pieces.shape[0]
    for j in range(pieces.shape[0]):
        rows = [planes[p, j * each:(j + 1) * each] for p in range(5)]
        pieces[j] = jnp.concatenate(rows, 0).astype(jnp.bfloat16)


def pieces_sum_kernel(pieces, out):
    f32, bf16 = jnp.float32, jnp.bfloat16
    total = pieces[0].astype(f32)
    for j in range(1, pieces.shape[0]):
        total = total + pieces[j].astype(f32)
    total = total.astype(bf16)
    for j in range(out.shape[0]):
        out[j] = total


def lay_out(pieces, half, planes, lanes_at):
    f32, bf16 = jnp.float32, jnp.bfloat16
    each = SG // pieces.shape[0]
    for j in range(pieces.shape[0]):
        some = pieces[j].astype(f32)
        for p in range(5):
            planes[p, j * each:(j + 1) * each, lanes_at] = some[p * each:(p + 1) * each]

    def step(forward):
        rows = [pl.ds(pl.multiple_of(p * SG + half * HALF, HALF), HALF) for p in range(2)]
        left = jnp.concatenate([planes[p, :, lanes_at].astype(bf16) for p in range(2)], 1)
        right = jnp.concatenate([forward[at] for at in rows], 0)
        return jnp.dot(left, right, preferred_element_type=f32)

    return step


def asked(part):
    each = (part.shape[0] - 2 * SG) // 2
    return vis_rows(part[2 * SG:2 * SG + each].astype(jnp.float32))


def own_half_kernel(chips, pieces, forward, *refs):
    parts, (out, wide, hots, planes) = refs[:chips], refs[chips:]
    chip = (place()[0] // 2).astype(jnp.float32)
    counter = sublanes(SG).astype(jnp.float32)
    for k in range(chips):
        ask = asked(parts[-k % chips])
        u_here = jnp.where(ask[0:1] == chip, ask[1:2], -1.0)
        hots[k] = jnp.where(u_here == counter, 1.0, 0.0).astype(jnp.bfloat16)
    wide[...] = lay_out(pieces, place()[0] % 2, planes, slice(0, HALF))(forward)
    out[...] = planes[2:]


def grids_kernel(chips, own, own_wide, hots, other, *refs):
    f32, bf16 = jnp.float32, jnp.bfloat16
    parts, (grid_left, forward, inverse_left, inverse) = refs[:chips], refs[chips:chips + 4]
    outs, rest, (planes, cat, tall, hat) = refs[chips + 4:-5], refs[-5], refs[-4:]
    row_index, _ = place()
    core = row_index % 2
    at = [pl.ds(pl.multiple_of(half * HALF, HALF), HALF) for half in (core, 1 - core)]
    wide = (own_wide[...] + lay_out(other, 1 - core, planes, at[1])(forward)).astype(bf16)
    for p in range(3):
        planes[2 + p, :, at[0]] = own[p]
    tall[:SG] = wide[:, :SG]
    tall[SG:] = wide[:, SG:]
    model = jnp.dot(grid_left[...], tall[...], preferred_element_type=f32) * (1.0 / SG)
    hat_real, hat_imag = model[:SG], model[SG:]
    cat[:, :SG] = (planes[2] - planes[4] * hat_real).astype(bf16)
    cat[:, SG:] = (planes[3] - planes[4] * hat_imag).astype(bf16)
    hat[:SG] = hat_real.T.astype(bf16)
    hat[SG:] = hat_imag.T.astype(bf16)
    wide = jnp.dot(cat[...], inverse[...], preferred_element_type=f32)
    for k in range(2):
        tall[k * SG:(k + 1) * SG] = wide[:, k * SG:(k + 1) * SG].astype(bf16)
    back = jnp.dot(inverse_left[...], tall[...], preferred_element_type=f32) * (1.0 / SG)
    rest[...] = jnp.where(core == 0, back[:, HALF:], back[:, :HALF]).astype(bf16)
    back = jnp.where(core == 0, back[:, :HALF], back[:, HALF:]).astype(bf16)
    counter = sublanes(SG).astype(f32)
    for k, out in enumerate(outs):
        out[:2 * SG] = back
        ask = asked(parts[-k % chips])
        pick = ask[2:3] == counter
        line = jnp.dot(hat[...], hots[k], preferred_element_type=f32)
        rows = []
        for part in range(2):
            value = jnp.sum(jnp.where(pick, line[part * SG:(part + 1) * SG], 0.0), axis=0, keepdims=True)
            rows += [value[:, i * LANES:(i + 1) * LANES] for i in range(value.shape[1] // LANES)]
        rows.append(jnp.zeros((16 - len(rows), LANES), f32))
        out[2 * SG:] = jnp.concatenate(rows, 0).astype(bf16)


def back_tables_kernel(rows_count, cols_count, side, offsets_row, offsets_col, row_tab, col_tab):
    bf16 = jnp.bfloat16
    row_index, col_index = place()
    unit = sublanes(16)
    row_step = SKY // (rows_count * side)
    row_base = row_index * (SKY // rows_count)
    for r in range(NR):
        freq = offsets_row[r] + lanes(SG)
        coarse = wave((row_base + 16 * row_step * sublanes(side // 16)) * freq)
        fine = wave((row_step * unit) * freq)

        def store(at, cos, sin, r=r):
            row_tab[at:at + 16, 2 * r * SG:(2 * r + 1) * SG] = cos.astype(bf16)
            row_tab[at:at + 16, (2 * r + 1) * SG:(2 * r + 2) * SG] = sin.astype(bf16)

        spread(coarse, fine, store)
    col_step = SKY // (cols_count * side)
    pos = col_index * (SKY // cols_count) + col_step * lanes(side)
    fine = wave(unit * pos)
    for c in range(NC):
        coarse = wave((offsets_col[c] + 16 * unit) * pos)

        def store(at, cos, sin, c=c):
            left = (2 * c + at // HALF) * 2 * HALF + at % HALF
            col_tab[left:left + 16] = cos.astype(bf16)
            col_tab[left + HALF:left + HALF + 16] = (-sin).astype(bf16)

        spread(coarse, fine, store)


def block_part(block, number, row_tab):
    r, _ = split_number(number)
    real, imag = block[:SG], block[SG:2 * SG]
    right = jnp.concatenate([jnp.concatenate([real, imag], 1), jnp.concatenate([-imag, real], 1)], 0)
    left = row_tab[:, pl.ds(pl.multiple_of(2 * r * SG, 2 * SG), 2 * SG)]
    return jnp.dot(left, right, preferred_element_type=jnp.float32)


def first_part_kernel(own, rest, row_tab, out):
    chip = place()[0] // 2
    for n, block in enumerate((own, rest)):
        out[:, n * SG:(n + 1) * SG] = block_part(block, chip, row_tab)


def column_rows(number):
    depth = 2 * SG
    return pl.ds(pl.multiple_of(split_number(number)[1] * depth, depth), depth)


def half_lanes(n):
    half = place()[0] % 2
    return pl.ds(pl.multiple_of((half if n == 0 else 1 - half) * SG, SG), SG)


def own_column_kernel(chips, opposite, own, rest, first, row_tab, col_tab, out, both):
    chip = place()[0] // 2
    for n, block in enumerate((own, rest)):
        part = first[:, n * SG:(n + 1) * SG] + block_part(block, chip + chips - opposite, row_tab)
        both[:, half_lanes(n)] = part.astype(jnp.bfloat16)
    out[...] = jnp.dot(both[...], col_tab[column_rows(chip)], preferred_element_type=jnp.float32)


def image_kernel(scale, chips, *refs):
    f32, bf16 = jnp.float32, jnp.bfloat16
    blocks, others, refs = refs[:chips], refs[chips:chips + 2], refs[chips + 2:]
    first, row_tab, col_tab, observed, out, residual, both, image, seen, sems = refs
    chip = place()[0] // 2
    model = jnp.zeros((16, LANES), f32)
    for block in blocks:
        model = model + block[2 * SG:].astype(f32)
    count = observed.shape[1] // LANES
    for part in range(2):
        for i in range(count):
            at = slice(i * LANES, (i + 1) * LANES)
            seen[part:part + 1, at] = observed[part:part + 1, at] - model[part * count + i:part * count + i + 1]
    writes = [pltpu.make_async_copy(seen, residual, sems.at[0])]
    writes[0].start()
    for n, pair in enumerate(((blocks[1], blocks[3]), others)):
        part = block_part(pair[0], chip + chips - 1, row_tab) + block_part(pair[1], chip + chips - 3, row_tab)
        both[:, half_lanes(n)] = part.astype(bf16)
    chunks = sems.shape[0] - 1
    step = image.shape[0] // chunks
    for n in range(chunks):
        at = slice(n * step, (n + 1) * step)
        part = jnp.dot(both[at], col_tab[column_rows(chip + 1)], preferred_element_type=f32)
        image[at] = (first[at] + part) * scale
        write = pltpu.make_async_copy(image.at[at], out.at[at], sems.at[1 + n])
        write.start()
        writes.append(write)
    for write in writes:
        write.wait()


def call(kernel, out_shape, name, spaces, scratch=(), cost=0, outs=None, room=24):
    kinds = {"s": pltpu.SMEM, "v": pltpu.VMEM, "a": pl.ANY}
    several = isinstance(out_shape, tuple)
    outs = outs or "v" * (len(out_shape) if several else 1)
    out_specs = tuple(pl.BlockSpec(memory_space=kinds[kind]) for kind in outs)
    return pl.pallas_call(
        kernel,
        out_shape=out_shape,
        in_specs=[pl.BlockSpec(memory_space=kinds[kind]) for kind in spaces],
        out_specs=out_specs if several else out_specs[0],
        scratch_shapes=list(scratch),
        compiler_params=pltpu.CompilerParams(vmem_limit_bytes=room * 2**20),
        cost_estimate=pl.CostEstimate(flops=cost, bytes_accessed=2**20, transcendentals=0),
        name=name,
    )


def grid_tables():
    counter = np.arange(SG)
    angles = (counter[:, None] * counter[None, :] % SG).astype(np.float64) * (2.0 * math.pi / SG)
    return np.cos(angles).astype(ml_dtypes.bfloat16), np.sin(angles).astype(ml_dtypes.bfloat16)


def exchange(blocks, axes, groups):
    return lax.all_to_all(blocks, axes, 0, 0, tiled=True, axis_index_groups=groups)


def shape(*dims, dtype=jnp.bfloat16):
    return jax.ShapeDtypeStruct(dims, dtype)


def shards(facet, row_offsets, col_offsets, vis_subgrid, vis_u, vis_v, observed):
    f32, bf16 = jnp.float32, jnp.bfloat16
    rows_count, cols_count = lax.axis_size("frow"), lax.axis_size("fcol")
    side = facet.shape[0]
    n_vis = vis_u.shape[0]
    chips = rows_count // 2
    each = SG // cols_count
    swap = [(index, index ^ 1) for index in range(rows_count)]
    turns = [[(index, (index + 2 * k) % rows_count) for index in range(rows_count)] for k in range(chips)]

    def turned(blocks):
        moved = {k: lax.ppermute(blocks[k], "frow", turns[k]) for k in (2, 1, 3)}
        return [blocks[0]] + [moved[k] for k in range(1, chips)]

    scale_in = 1.0 / (side * math.sqrt(rows_count * cols_count))
    scale_out = 1.0 / (SG * math.sqrt(NR * NC))
    line = (1, n_vis)

    send, vis = call(
        functools.partial(send_columns_kernel, cols_count), (shape(side + 16, 4 * HALF), shape(16, n_vis // 2)),
        "send_columns", "aaaaaa",
        scratch=[
            pltpu.VMEM((side, 4 * HALF), bf16), pltpu.VMEM((side, side), bf16), pltpu.VMEM((3,) + line, jnp.int32),
            pltpu.VMEM((2, n_vis), f32), pltpu.SMEM((NC,), jnp.int32), pltpu.VMEM((side, 4 * HALF), bf16),
            pltpu.VMEM((16, n_vis), bf16), pltpu.SemaphoreType.DMA((10,)),
        ],
        cost=10**9, room=60, outs="aa",
    )(col_offsets, facet, vis_subgrid.reshape(line), vis_u.reshape(line), vis_v.reshape(line), observed)
    other = lax.ppermute(send, "frow", swap)
    own, row_tab = call(
        functools.partial(own_tables_kernel, rows_count, cols_count),
        (shape(side, 4 * HALF), shape(4, SG, 2 * side)), "own_tables", "ssv",
        scratch=[pltpu.VMEM((side, 4 * HALF), bf16)], cost=10**9,
    )(row_offsets, col_offsets, facet)
    vis_rows_count = 8 * 2 * n_vis // LANES
    parts = {}
    for k in (2, 1, 3, 0):
        parts[k] = call(
            functools.partial(contribution_kernel, scale_in, k), shape(2 * SG + vis_rows_count, HALF), "contribution",
            "vvvv", cost=5 * 10**8,
        )(own, vis, other, row_tab)
    parts = turned(parts)

    sums = call(first_sums_kernel, shape(5, SG, HALF, dtype=f32), "first_sums", "vv", cost=10**9)(parts[0], parts[2])
    back_row, back_col = call(
        functools.partial(back_tables_kernel, rows_count, cols_count, side),
        (shape(side, 4 * SG), shape(4 * SG, side)), "back_tables", "ss", cost=10**9,
    )(row_offsets, col_offsets)
    pieces = call(
        gridding_kernel, shape(cols_count, 5 * each, HALF), "gridding", "v" * (chips - 1) + "a",
        scratch=[pltpu.VMEM((5, SG, HALF), f32)], cost=10**9,
    )(parts[1], parts[3], sums, back_col)
    pieces = exchange(pieces, "fcol", None)
    pieces = call(pieces_sum_kernel, shape(cols_count, 5 * each, HALF), "pieces_sum", "v", cost=10**6)(pieces)
    pieces = exchange(pieces, "fcol", None)
    pieces_other = lax.ppermute(pieces, "frow", swap)

    kcos, ksin = grid_tables()
    block = [np.concatenate(pair, 1) for pair in ((kcos, ksin), (-ksin, kcos), (kcos, -ksin), (ksin, kcos))]
    forward_block = np.concatenate([block[0], block[1]], 0)
    inverse_block = np.concatenate([block[2], block[3]], 0)
    own_planes, own_wide, hots = call(
        functools.partial(own_half_kernel, chips),
        (shape(3, SG, HALF, dtype=f32), shape(SG, 2 * SG, dtype=f32), shape(chips, SG, n_vis)), "own_half", "vv" + "v" * chips,
        scratch=[pltpu.VMEM((5, SG, HALF), f32)], cost=10**9,
    )(pieces, forward_block, *parts)
    *back, rest = call(
        functools.partial(grids_kernel, chips), (shape(2 * SG + 16, HALF),) * chips + (shape(2 * SG, HALF),), "grids",
        "v" * (8 + chips),
        scratch=[
            pltpu.VMEM((5, SG, SG), f32), pltpu.VMEM((SG, 2 * SG), bf16), pltpu.VMEM((2 * SG, SG), bf16),
            pltpu.VMEM((2 * SG, SG), bf16),
        ],
        cost=10**9,
    )(own_planes, own_wide, hots, pieces_other, *parts, inverse_block, forward_block, forward_block, inverse_block)
    back = turned(back)

    both = pltpu.VMEM((side, 2 * SG), bf16)
    square = shape(side, side, dtype=f32)
    first = call(first_part_kernel, square, "first_part", "vvv", cost=10**9)(back[0], rest, back_row)
    back[2], first = lax.optimization_barrier((back[2], first))
    rest = {k: lax.ppermute(back[k], "frow", swap) for k in (2, 1, 3)}
    first = call(
        functools.partial(own_column_kernel, chips, 2), square, "own_column", "v" * 5, scratch=[both], cost=10**9
    )(back[2], rest[2], first, back_row, back_col)
    return call(
        functools.partial(image_kernel, scale_out, chips), (square, shape(2, n_vis, dtype=f32)), "image",
        "v" * (chips + 6), outs="aa",
        scratch=[both, pltpu.VMEM((side, side), f32), pltpu.VMEM((2, n_vis), f32), pltpu.SemaphoreType.DMA((5,))],
        cost=10**9,
    )(*back, rest[1], rest[3], first, back_row, back_col, observed)


def solution(mesh):
    in_specs = (
        P("frow", "fcol"),
        P(),
        P(),
        P(("frow", "fcol")),
        P(("frow", "fcol")),
        P(("frow", "fcol")),
        P(None, ("frow", "fcol")),
    )
    out_specs = (P("frow", "fcol"), P(None, ("frow", "fcol")))
    return jax.shard_map(shards, mesh=mesh, in_specs=in_specs, out_specs=out_specs, check_vma=False)
```

```python
import functools
import math

import jax
import jax.numpy as jnp
import ml_dtypes
import numpy as np
from jax import lax
from jax.experimental import pallas as pl
from jax.experimental.pallas import tpu as pltpu
from jax.sharding import PartitionSpec as P

SKY = 65536
SG = 256
NR = 2
NC = 2
HALF = SG // 2
LANES = 128


def wave(count):
    count = count & (SKY - 1)
    turned = count + SKY // 8
    near = (turned & (SKY // 4 - 1)) - SKY // 8
    quarter = lax.shift_right_logical(turned, 14) & 3
    t = near.astype(jnp.float32) * (2.0 * math.pi / SKY)
    q = t * t
    sin = t * (1.0 + q * (-1.0 / 6 + q * (1.0 / 120 + q * (-1.0 / 5040 + q * (1.0 / 362880)))))
    cos = 1.0 + q * (-0.5 + q * (1.0 / 24 + q * (-1.0 / 720 + q * (1.0 / 40320))))
    odd = (quarter & 1) == 1
    one, two = jnp.where(odd, sin, cos), jnp.where(odd, cos, sin)
    return (
        jnp.where((quarter == 1) | (quarter == 2), -one, one),
        jnp.where(quarter >= 2, -two, two),
    )


def lanes(n):
    return lax.broadcasted_iota(jnp.int32, (1, n), 1)


def sublanes(n):
    return lax.broadcasted_iota(jnp.int32, (n, 1), 0)


def spread(coarse, fine, store):
    for k in range(coarse[0].shape[0]):
        c, s = coarse[0][k:k + 1], coarse[1][k:k + 1]
        store(k * 16, c * fine[0] - s * fine[1], s * fine[0] + c * fine[1])


def place():
    return lax.axis_index("frow"), lax.axis_index("fcol")


def half_columns(cols_count, offsets, half, side, col_tab):
    bf16 = jnp.bfloat16
    col_index = place()[1]
    unit = sublanes(16)
    col_step = SKY // (cols_count * side)
    col_base = col_index * (SKY // cols_count)
    freq = [offsets[c] + half * HALF + lanes(HALF) for c in range(NC)]
    freq = jnp.concatenate(freq, 1)
    coarse = wave((col_base + 16 * col_step * sublanes(side // 16)) * freq)
    fine = wave((col_step * unit) * freq)

    def store(at, cos, sin):
        for c in range(NC):
            some = slice(c * HALF, (c + 1) * HALF)
            col_tab[at:at + 16, 2 * c * HALF:(2 * c + 1) * HALF] = cos[:, some].astype(bf16)
            col_tab[at:at + 16, (2 * c + 1) * HALF:(2 * c + 2) * HALF] = sin[:, some].astype(bf16)

    spread(coarse, fine, store)


def send_columns_kernel(cols_count, offsets, facet, subgrid, u, v, observed, send, vis, *scratch):
    col_tab, image, indices, seen, first, made, tail, sems = scratch
    f32, bf16 = jnp.float32, jnp.bfloat16
    side = facet.shape[0]
    pairs = [
        (offsets, first), (facet, image), (subgrid, indices.at[0]), (u, indices.at[1]), (v, indices.at[2]), (observed, seen),
    ]
    copies = [pltpu.make_async_copy(source, target, sems.at[n]) for n, (source, target) in enumerate(pairs)]
    for copy in copies:
        copy.start()
    copies[0].wait()
    half_columns(cols_count, first, 1 - place()[0] % 2, side, col_tab)
    for copy in copies[2:]:
        copy.wait()
    some = jnp.concatenate([indices[n].astype(f32) for n in range(3)] + [seen[...], jnp.zeros((3, side), f32)], 0)
    some = jnp.concatenate([some[:, :side // 2], some[:, side // 2:]], 0).astype(bf16)
    tail[:, :side // 2] = some
    tail[:, side // 2:] = some
    writes = [
        pltpu.make_async_copy(tail.at[:, pl.ds(0, side // 2)], vis, sems.at[6]),
        pltpu.make_async_copy(tail, send.at[pl.ds(side, 16)], sems.at[7]),
    ]
    for write in writes:
        write.start()
    copies[1].wait()
    step = side // 2
    for n in range(2):
        at = pl.ds(n * step, step)
        made[at] = jnp.dot(image[at], col_tab[...], preferred_element_type=f32).astype(bf16)
        write = pltpu.make_async_copy(made.at[at], send.at[at], sems.at[8 + n])
        write.start()
        writes.append(write)
    for write in writes:
        write.wait()


def own_tables_kernel(rows_count, cols_count, offsets, col_offsets, facet, own, row_tab, col_tab):
    bf16 = jnp.bfloat16
    row_index, _ = place()
    side = facet.shape[0]
    half_columns(cols_count, col_offsets, row_index % 2, side, col_tab)
    own[...] = jnp.dot(facet[...], col_tab[...], preferred_element_type=jnp.float32).astype(bf16)
    unit = sublanes(16)
    row_step = SKY // (rows_count * side)
    for f in range(2):
        pos = (row_index ^ f) * (SKY // rows_count) + row_step * lanes(side)
        fine = wave(unit * pos)
        for r in range(NR):
            coarse = wave((offsets[r] + 16 * unit) * pos)

            def store(at, cos, sin, r=r, f=f):
                row_tab[2 * r, at:at + 16, f * side:(f + 1) * side] = cos.astype(bf16)
                row_tab[2 * r + 1, at:at + 16, f * side:(f + 1) * side] = sin.astype(bf16)

            spread(coarse, fine, store)


def contribution_kernel(scale, number, own, own_vis, other, row_tab, out):
    f32, bf16 = jnp.float32, jnp.bfloat16
    side = own.shape[0]
    vis = []
    for some in (own_vis[...], other[side:]):
        vis += [some[:, k * LANES:(k + 1) * LANES] for k in range(side // 2 // LANES)]
    for k, some in enumerate(vis):
        at = 2 * SG + 16 * k
        out[at:at + 16] = some
    r, c = split_number(place()[0] // 2 + number)
    at = pl.ds(pl.multiple_of(c * SG, SG), SG)
    right = jnp.concatenate([own[:, at], other[:side, at]], 0)
    with_cos = jnp.dot(row_tab[2 * r], right, preferred_element_type=f32)
    with_sin = jnp.dot(row_tab[2 * r + 1], right, preferred_element_type=f32)
    out[:SG] = ((with_cos[:, :HALF] - with_sin[:, HALF:]) * scale).astype(bf16)
    out[SG:2 * SG] = (-(with_cos[:, HALF:] + with_sin[:, :HALF]) * scale).astype(bf16)


def split_number(number):
    number = lax.rem(number, NR * NC)
    return number // NC, lax.rem(number, NC)


def vis_rows(block):
    count = block.shape[0] // 16
    return jnp.concatenate(
        [block[16 * k + 8 * part:16 * k + 8 * part + 8] for part in range(2) for k in range(count)], 1
    )


def grid_sums(parts):
    f32, bf16 = jnp.float32, jnp.bfloat16
    row_index, _ = place()
    chip = (row_index // 2).astype(f32)
    v_at = (sublanes(HALF) + (row_index % 2) * HALF).astype(f32)
    counter = sublanes(SG).astype(f32)
    total = jnp.zeros((SG, 3 * HALF), f32)
    planes = [jnp.zeros((SG, HALF), f32)] * 2
    for part in parts:
        one = vis_rows(part[2 * SG:].astype(f32))
        u_here = jnp.where(one[0:1] == chip, one[1:2], -1.0)
        hot = jnp.where(u_here == counter, 1.0, 0.0).astype(bf16)
        pick = one[2:3] == v_at
        right = jnp.concatenate(
            [jnp.where(pick, one[3:4], 0.0), jnp.where(pick, one[4:5], 0.0), jnp.where(pick, 1.0, 0.0)], 0
        ).astype(bf16)
        total = total + lax.dot_general(hot, right, (((1,), (1,)), ((), ())), preferred_element_type=f32)
        planes = [planes[p] + part[p * SG:(p + 1) * SG].astype(f32) for p in range(2)]
    return planes + [total[:, p * HALF:(p + 1) * HALF] for p in range(3)]


def first_sums_kernel(*refs):
    for p, plane in enumerate(grid_sums(refs[:-1])):
        refs[-1][p] = plane


def gridding_kernel(*refs):
    parts, (first, _, pieces, planes) = refs[:-4], refs[-4:]
    for p, plane in enumerate(grid_sums(parts)):
        planes[p] = first[p] + plane
    each = SG // pieces.shape[0]
    for j in range(pieces.shape[0]):
        rows = [planes[p, j * each:(j + 1) * each] for p in range(5)]
        pieces[j] = jnp.concatenate(rows, 0).astype(jnp.bfloat16)


def pieces_sum_kernel(pieces, out):
    f32, bf16 = jnp.float32, jnp.bfloat16
    total = pieces[0].astype(f32)
    for j in range(1, pieces.shape[0]):
        total = total + pieces[j].astype(f32)
    total = total.astype(bf16)
    for j in range(out.shape[0]):
        out[j] = total


def lay_out(pieces, half, planes, lanes_at):
    f32, bf16 = jnp.float32, jnp.bfloat16
    each = SG // pieces.shape[0]
    for j in range(pieces.shape[0]):
        some = pieces[j].astype(f32)
        for p in range(5):
            planes[p, j * each:(j + 1) * each, lanes_at] = some[p * each:(p + 1) * each]

    def step(forward):
        rows = [pl.ds(pl.multiple_of(p * SG + half * HALF, HALF), HALF) for p in range(2)]
        left = jnp.concatenate([planes[p, :, lanes_at].astype(bf16) for p in range(2)], 1)
        right = jnp.concatenate([forward[at] for at in rows], 0)
        return jnp.dot(left, right, preferred_element_type=f32)

    return step


def asked(part):
    each = (part.shape[0] - 2 * SG) // 2
    return vis_rows(part[2 * SG:2 * SG + each].astype(jnp.float32))


def own_half_kernel(chips, pieces, forward, *refs):
    parts, (out, wide, hots, planes) = refs[:chips], refs[chips:]
    chip = (place()[0] // 2).astype(jnp.float32)
    counter = sublanes(SG).astype(jnp.float32)
    for k in range(chips):
        ask = asked(parts[-k % chips])
        u_here = jnp.where(ask[0:1] == chip, ask[1:2], -1.0)
        hots[k] = jnp.where(u_here == counter, 1.0, 0.0).astype(jnp.bfloat16)
    wide[...] = lay_out(pieces, place()[0] % 2, planes, slice(0, HALF))(forward)
    out[...] = planes[2:]


def grids_kernel(chips, own, own_wide, hots, other, *refs):
    f32, bf16 = jnp.float32, jnp.bfloat16
    parts, (grid_left, forward, inverse_left, inverse) = refs[:chips], refs[chips:chips + 4]
    outs, rest, (planes, cat, tall, hat) = refs[chips + 4:-5], refs[-5], refs[-4:]
    row_index, _ = place()
    core = row_index % 2
    at = [pl.ds(pl.multiple_of(half * HALF, HALF), HALF) for half in (core, 1 - core)]
    wide = (own_wide[...] + lay_out(other, 1 - core, planes, at[1])(forward)).astype(bf16)
    for p in range(3):
        planes[2 + p, :, at[0]] = own[p]
    tall[:SG] = wide[:, :SG]
    tall[SG:] = wide[:, SG:]
    model = jnp.dot(grid_left[...], tall[...], preferred_element_type=f32) * (1.0 / SG)
    hat_real, hat_imag = model[:SG], model[SG:]
    cat[:, :SG] = (planes[2] - planes[4] * hat_real).astype(bf16)
    cat[:, SG:] = (planes[3] - planes[4] * hat_imag).astype(bf16)
    hat[:, :SG] = hat_real.astype(bf16)
    hat[:, SG:] = hat_imag.astype(bf16)
    wide = jnp.dot(cat[...], inverse[...], preferred_element_type=f32)
    for k in range(2):
        tall[k * SG:(k + 1) * SG] = wide[:, k * SG:(k + 1) * SG].astype(bf16)
    back = jnp.dot(inverse_left[...], tall[...], preferred_element_type=f32) * (1.0 / SG)
    rest[...] = jnp.where(core == 0, back[:, HALF:], back[:, :HALF]).astype(bf16)
    back = jnp.where(core == 0, back[:, :HALF], back[:, HALF:]).astype(bf16)
    counter = sublanes(SG).astype(f32)
    for k, out in enumerate(outs):
        out[:2 * SG] = back
        ask = asked(parts[-k % chips])
        pick = ask[2:3] == counter
        line = lax.dot_general(hat[...], hots[k], (((0,), (0,)), ((), ())), preferred_element_type=f32)
        rows = []
        for part in range(2):
            value = jnp.sum(jnp.where(pick, line[part * SG:(part + 1) * SG], 0.0), axis=0, keepdims=True)
            rows += [value[:, i * LANES:(i + 1) * LANES] for i in range(value.shape[1] // LANES)]
        rows.append(jnp.zeros((16 - len(rows), LANES), f32))
        out[2 * SG:] = jnp.concatenate(rows, 0).astype(bf16)


def back_tables_kernel(rows_count, cols_count, side, offsets_row, offsets_col, row_tab, col_tab):
    bf16 = jnp.bfloat16
    row_index, col_index = place()
    unit = sublanes(16)
    row_step = SKY // (rows_count * side)
    row_base = row_index * (SKY // rows_count)
    for r in range(NR):
        freq = offsets_row[r] + lanes(SG)
        coarse = wave((row_base + 16 * row_step * sublanes(side // 16)) * freq)
        fine = wave((row_step * unit) * freq)

        def store(at, cos, sin, r=r):
            row_tab[at:at + 16, 2 * r * SG:(2 * r + 1) * SG] = cos.astype(bf16)
            row_tab[at:at + 16, (2 * r + 1) * SG:(2 * r + 2) * SG] = sin.astype(bf16)

        spread(coarse, fine, store)
    col_step = SKY // (cols_count * side)
    pos = col_index * (SKY // cols_count) + col_step * lanes(side)
    fine = wave(unit * pos)
    for c in range(NC):
        coarse = wave((offsets_col[c] + 16 * unit) * pos)

        def store(at, cos, sin, c=c):
            left = (2 * c + at // HALF) * 2 * HALF + at % HALF
            col_tab[left:left + 16] = cos.astype(bf16)
            col_tab[left + HALF:left + HALF + 16] = (-sin).astype(bf16)

        spread(coarse, fine, store)


def block_part(block, number, row_tab):
    r, _ = split_number(number)
    real, imag = block[:SG], block[SG:2 * SG]
    right = jnp.concatenate([jnp.concatenate([real, imag], 1), jnp.concatenate([-imag, real], 1)], 0)
    left = row_tab[:, pl.ds(pl.multiple_of(2 * r * SG, 2 * SG), 2 * SG)]
    return jnp.dot(left, right, preferred_element_type=jnp.float32)


def first_part_kernel(own, rest, row_tab, out):
    chip = place()[0] // 2
    for n, block in enumerate((own, rest)):
        out[:, n * SG:(n + 1) * SG] = block_part(block, chip, row_tab)


def column_rows(number):
    depth = 2 * SG
    return pl.ds(pl.multiple_of(split_number(number)[1] * depth, depth), depth)


def half_lanes(n):
    half = place()[0] % 2
    return pl.ds(pl.multiple_of((half if n == 0 else 1 - half) * SG, SG), SG)


def own_column_kernel(chips, opposite, own, rest, first, row_tab, col_tab, out, both):
    chip = place()[0] // 2
    for n, block in enumerate((own, rest)):
        part = first[:, n * SG:(n + 1) * SG] + block_part(block, chip + chips - opposite, row_tab)
        both[:, half_lanes(n)] = part.astype(jnp.bfloat16)
    out[...] = jnp.dot(both[...], col_tab[column_rows(chip)], preferred_element_type=jnp.float32)


def image_kernel(scale, chips, *refs):
    f32, bf16 = jnp.float32, jnp.bfloat16
    blocks, others, refs = refs[:chips], refs[chips:chips + 2], refs[chips + 2:]
    first, row_tab, col_tab, observed, out, residual, both, image, seen, sems = refs
    chip = place()[0] // 2
    model = jnp.zeros((16, LANES), f32)
    for block in blocks:
        model = model + block[2 * SG:].astype(f32)
    count = observed.shape[1] // LANES
    for part in range(2):
        for i in range(count):
            at = slice(i * LANES, (i + 1) * LANES)
            seen[part:part + 1, at] = observed[part:part + 1, at] - model[part * count + i:part * count + i + 1]
    writes = [pltpu.make_async_copy(seen, residual, sems.at[0])]
    writes[0].start()
    for n, pair in enumerate(((blocks[1], blocks[3]), others)):
        part = block_part(pair[0], chip + chips - 1, row_tab) + block_part(pair[1], chip + chips - 3, row_tab)
        both[:, half_lanes(n)] = part.astype(bf16)
    chunks = sems.shape[0] - 1
    step = image.shape[0] // chunks
    for n in range(chunks):
        at = slice(n * step, (n + 1) * step)
        part = jnp.dot(both[at], col_tab[column_rows(chip + 1)], preferred_element_type=f32)
        image[at] = (first[at] + part) * scale
        write = pltpu.make_async_copy(image.at[at], out.at[at], sems.at[1 + n])
        write.start()
        writes.append(write)
    for write in writes:
        write.wait()


def call(kernel, out_shape, name, spaces, scratch=(), cost=0, outs=None, room=24):
    kinds = {"s": pltpu.SMEM, "v": pltpu.VMEM, "a": pl.ANY}
    several = isinstance(out_shape, tuple)
    outs = outs or "v" * (len(out_shape) if several else 1)
    out_specs = tuple(pl.BlockSpec(memory_space=kinds[kind]) for kind in outs)
    return pl.pallas_call(
        kernel,
        out_shape=out_shape,
        in_specs=[pl.BlockSpec(memory_space=kinds[kind]) for kind in spaces],
        out_specs=out_specs if several else out_specs[0],
        scratch_shapes=list(scratch),
        compiler_params=pltpu.CompilerParams(vmem_limit_bytes=room * 2**20),
        cost_estimate=pl.CostEstimate(flops=cost, bytes_accessed=2**20, transcendentals=0),
        name=name,
    )


def grid_tables():
    counter = np.arange(SG)
    angles = (counter[:, None] * counter[None, :] % SG).astype(np.float64) * (2.0 * math.pi / SG)
    return np.cos(angles).astype(ml_dtypes.bfloat16), np.sin(angles).astype(ml_dtypes.bfloat16)


def exchange(blocks, axes, groups):
    return lax.all_to_all(blocks, axes, 0, 0, tiled=True, axis_index_groups=groups)


def shape(*dims, dtype=jnp.bfloat16):
    return jax.ShapeDtypeStruct(dims, dtype)


def shards(facet, row_offsets, col_offsets, vis_subgrid, vis_u, vis_v, observed):
    f32, bf16 = jnp.float32, jnp.bfloat16
    rows_count, cols_count = lax.axis_size("frow"), lax.axis_size("fcol")
    side = facet.shape[0]
    n_vis = vis_u.shape[0]
    chips = rows_count // 2
    each = SG // cols_count
    swap = [(index, index ^ 1) for index in range(rows_count)]
    turns = [[(index, (index + 2 * k) % rows_count) for index in range(rows_count)] for k in range(chips)]

    def turned(blocks):
        moved = {k: lax.ppermute(blocks[k], "frow", turns[k]) for k in (2, 1, 3)}
        return [blocks[0]] + [moved[k] for k in range(1, chips)]

    scale_in = 1.0 / (side * math.sqrt(rows_count * cols_count))
    scale_out = 1.0 / (SG * math.sqrt(NR * NC))
    line = (1, n_vis)

    send, vis = call(
        functools.partial(send_columns_kernel, cols_count), (shape(side + 16, 4 * HALF), shape(16, n_vis // 2)),
        "send_columns", "aaaaaa",
        scratch=[
            pltpu.VMEM((side, 4 * HALF), bf16), pltpu.VMEM((side, side), bf16), pltpu.VMEM((3,) + line, jnp.int32),
            pltpu.VMEM((2, n_vis), f32), pltpu.SMEM((NC,), jnp.int32), pltpu.VMEM((side, 4 * HALF), bf16),
            pltpu.VMEM((16, n_vis), bf16), pltpu.SemaphoreType.DMA((10,)),
        ],
        cost=10**9, room=60, outs="aa",
    )(col_offsets, facet, vis_subgrid.reshape(line), vis_u.reshape(line), vis_v.reshape(line), observed)
    other = lax.ppermute(send, "frow", swap)
    own, row_tab = call(
        functools.partial(own_tables_kernel, rows_count, cols_count),
        (shape(side, 4 * HALF), shape(4, SG, 2 * side)), "own_tables", "ssv",
        scratch=[pltpu.VMEM((side, 4 * HALF), bf16)], cost=10**9,
    )(row_offsets, col_offsets, facet)
    vis_rows_count = 8 * 2 * n_vis // LANES
    parts = {}
    for k in (2, 1, 3, 0):
        parts[k] = call(
            functools.partial(contribution_kernel, scale_in, k), shape(2 * SG + vis_rows_count, HALF), "contribution",
            "vvvv", cost=5 * 10**8,
        )(own, vis, other, row_tab)
    parts = turned(parts)

    sums = call(first_sums_kernel, shape(5, SG, HALF, dtype=f32), "first_sums", "vv", cost=10**9)(parts[0], parts[2])
    back_row, back_col = call(
        functools.partial(back_tables_kernel, rows_count, cols_count, side),
        (shape(side, 4 * SG), shape(4 * SG, side)), "back_tables", "ss", cost=10**9,
    )(row_offsets, col_offsets)
    pieces = call(
        gridding_kernel, shape(cols_count, 5 * each, HALF), "gridding", "v" * (chips - 1) + "a",
        scratch=[pltpu.VMEM((5, SG, HALF), f32)], cost=10**9,
    )(parts[1], parts[3], sums, back_col)
    pieces = exchange(pieces, "fcol", None)
    pieces = call(pieces_sum_kernel, shape(cols_count, 5 * each, HALF), "pieces_sum", "v", cost=10**6)(pieces)
    pieces = exchange(pieces, "fcol", None)
    pieces_other = lax.ppermute(pieces, "frow", swap)

    kcos, ksin = grid_tables()
    block = [np.concatenate(pair, 1) for pair in ((kcos, ksin), (-ksin, kcos), (kcos, -ksin), (ksin, kcos))]
    forward_block = np.concatenate([block[0], block[1]], 0)
    inverse_block = np.concatenate([block[2], block[3]], 0)
    own_planes, own_wide, hots = call(
        functools.partial(own_half_kernel, chips),
        (shape(3, SG, HALF, dtype=f32), shape(SG, 2 * SG, dtype=f32), shape(chips, SG, n_vis)), "own_half", "vv" + "v" * chips,
        scratch=[pltpu.VMEM((5, SG, HALF), f32)], cost=10**9,
    )(pieces, forward_block, *parts)
    *back, rest = call(
        functools.partial(grids_kernel, chips), (shape(2 * SG + 16, HALF),) * chips + (shape(2 * SG, HALF),), "grids",
        "v" * (8 + chips),
        scratch=[
            pltpu.VMEM((5, SG, SG), f32), pltpu.VMEM((SG, 2 * SG), bf16), pltpu.VMEM((2 * SG, SG), bf16),
            pltpu.VMEM((SG, 2 * SG), bf16),
        ],
        cost=10**9,
    )(own_planes, own_wide, hots, pieces_other, *parts, inverse_block, forward_block, forward_block, inverse_block)
    back = turned(back)

    both = pltpu.VMEM((side, 2 * SG), bf16)
    square = shape(side, side, dtype=f32)
    first = call(first_part_kernel, square, "first_part", "vvv", cost=10**9)(back[0], rest, back_row)
    back[2], first = lax.optimization_barrier((back[2], first))
    rest = {k: lax.ppermute(back[k], "frow", swap) for k in (2, 1, 3)}
    first = call(
        functools.partial(own_column_kernel, chips, 2), square, "own_column", "v" * 5, scratch=[both], cost=10**9
    )(back[2], rest[2], first, back_row, back_col)
    return call(
        functools.partial(image_kernel, scale_out, chips), (square, shape(2, n_vis, dtype=f32)), "image",
        "v" * (chips + 6), outs="aa",
        scratch=[both, pltpu.VMEM((side, side), f32), pltpu.VMEM((2, n_vis), f32), pltpu.SemaphoreType.DMA((3,))],
        cost=10**9,
    )(*back, rest[1], rest[3], first, back_row, back_col, observed)


def solution(mesh):
    in_specs = (
        P("frow", "fcol"),
        P(),
        P(),
        P(("frow", "fcol")),
        P(("frow", "fcol")),
        P(("frow", "fcol")),
        P(None, ("frow", "fcol")),
    )
    out_specs = (P("frow", "fcol"), P(None, ("frow", "fcol")))
    return jax.shard_map(shards, mesh=mesh, in_specs=in_specs, out_specs=out_specs, check_vma=False)
```
